128 devices in a mesh: grp: 8 (over x_lo, y), shard: 16 (over x_hi, z, core).
Axes of the slice: x: 4 (x_hi: 2, x_lo: 2; x = x_hi * 2 + x_lo), y: 4, z: 4, core: 2. Of those that a mesh axis runs over, the one named last changes fastest.
Arguments:
- tokens: bfloat16 [2048, 4096], P('grp'), may hold values from -6 to 6
- gate_weight: bfloat16 [4096, 14336], P('grp', 'shard'), may hold values from -0.09375 to 0.09375
- up_weight: bfloat16 [4096, 14336], P('grp', 'shard'), may hold values from -0.09375 to 0.09375
- down_weight: bfloat16 [14336, 4096], P('shard', 'grp'), may hold values from -0.046875 to 0.046875
- grad_out: bfloat16 [2048, 4096], P('grp'), may hold values from -6 to 6
Outputs:
- grad_tokens: bfloat16 [2048, 4096], P('shard', 'grp')
- grad_gate: float32 [4096, 14336], P('grp', 'shard')
- grad_up: float32 [4096, 14336], P('grp', 'shard')
- grad_down: float32 [14336, 4096], P('shard', 'grp')
The draws below stay inside these ranges and needn't reach their ends.
All inputs are finite; a program needn't handle non-finite values.
Results may differ from the reference program's by a relative error of at most 0.013.
Values may be sent and summed in bfloat16 or wider, within the bound.
A program may use at most 128 MiB of HBM per device.

```python
import jax
import jax.numpy as jnp
from jax import lax

D = 4096
HIDDEN_SIZE = 14336
TOKENS = 2048


def block_levels(rng, dims, shards, low, largest):
    def one(position, parts):
        heights = jax.random.uniform(jax.random.fold_in(jax.random.fold_in(rng, 6), position), (parts,), jnp.float32, low / len(shards), largest / len(shards))
        return jnp.repeat(jnp.exp(heights), dims[position] // parts).reshape((-1,) + (1,) * (len(dims) - position - 1))

    loudness = one(*shards[0])
    for cut in shards[1:]:
        loudness = loudness * one(*cut)
    return loudness


def noise(key, dims, spread, most, shards=(), held_as=jnp.bfloat16):
    drawn = spread * jax.random.normal(key, dims, jnp.float32)
    if shards:
        drawn = drawn * block_levels(key, dims, shards, -0.22, 0.18)
    return jnp.clip(drawn, -most, most).astype(held_as)


def setup_inputs(seed: int = 0) -> dict:
    splits = jax.random.split(jax.random.key(seed), 6)
    tokens = noise(splits[0], (TOKENS, D), 1.0, 6.0, ((0, 8),))
    gate_weight = noise(splits[1], (D, HIDDEN_SIZE), D ** -0.5, 0.09375, ((0, 8), (1, 16)))
    up_weight = noise(splits[2], (D, HIDDEN_SIZE), D ** -0.5, 0.09375, ((0, 8), (1, 16)))
    down_weight = noise(splits[3], (HIDDEN_SIZE, D), HIDDEN_SIZE ** -0.5, 0.046875, ((0, 16), (1, 8)))
    grad_out = noise(splits[4], (TOKENS, D), 1.0, 6.0, ((0, 8),))
    return dict(tokens=tokens, gate_weight=gate_weight, up_weight=up_weight, down_weight=down_weight, grad_out=grad_out)


def contract_rows(left, right):
    return lax.dot_general(left, right, (((0,), (0,)), ((), ())), preferred_element_type=jnp.float32)


def contract_cols(left, right):
    return lax.dot_general(left, right, (((1,), (1,)), ((), ())), preferred_element_type=jnp.float32)


def reference(tokens, gate_weight, up_weight, down_weight, grad_out):
    gate_pre = jnp.dot(tokens, gate_weight, preferred_element_type=jnp.float32)
    up_pre = jnp.dot(tokens, up_weight, preferred_element_type=jnp.float32)
    gate_sigmoid = jax.nn.sigmoid(gate_pre)
    silu_gate = gate_pre * gate_sigmoid
    hidden = (silu_gate * up_pre).astype(jnp.bfloat16)
    back_grad = contract_cols(grad_out, down_weight)
    delta_gate = (back_grad * up_pre * gate_sigmoid * (1.0 + gate_pre * (1.0 - gate_sigmoid))).astype(jnp.bfloat16)
    delta_up = (back_grad * silu_gate).astype(jnp.bfloat16)
    grad_down = contract_rows(hidden, grad_out)
    grad_gate = contract_rows(tokens, delta_gate)
    grad_up = contract_rows(tokens, delta_up)
    grad_tokens = (contract_cols(delta_gate, gate_weight) + contract_cols(delta_up, up_weight)).astype(jnp.bfloat16)
    return grad_tokens, grad_gate, grad_up, grad_down
```

```python
import functools

import jax
import jax.numpy as jnp
from jax import lax
from jax.experimental import pallas as pl
from jax.experimental.pallas import tpu as pltpu
from jax.sharding import PartitionSpec as P

MESH = pl.DeviceIdType.MESH
BF16 = jnp.bfloat16
F32 = jnp.float32

Q = 224
DH = 2048
B = 512
CHUNK = 512


def dot_nt(left, right):
    return lax.dot_general(left, right, (((1,), (1,)), ((), ())), preferred_element_type=F32)


def dot_nn(left, right):
    return lax.dot_general(left, right, (((1,), (0,)), ((), ())), preferred_element_type=F32)


def dot_tn(left, right):
    return lax.dot_general(left, right, (((0,), (0,)), ((), ())), preferred_element_type=F32)


def kernel(
    tok, grd, w, dw, dx,
    buf, wbuf, part, other, acts, acc, dws, dxs, dxr, zr, ys, yr, xs, xr,
    ssem, rsem, lsem, zsem,
):
    grp, shard = lax.axis_index("grp"), lax.axis_index("shard")
    x_lo, y = lax.div(grp, 4), lax.rem(grp, 4)
    x_hi, z, c = lax.div(shard, 8), lax.rem(lax.div(shard, 2), 4), lax.rem(shard, 2)
    x = 2 * x_hi + x_lo

    def mod4(v):
        return lax.rem(v + 8, 4)

    def device(x, y, z, c):
        return (4 * lax.rem(x, 2) + y, 8 * lax.div(x, 2) + 2 * z + c)

    sibling = device(x, y, z, 1 - c)
    inner = device(x + 1 - 2 * x_lo, y, z, c)
    outer = device(mod4(x - 1 + 2 * x_lo), y, z, c)
    across = device(mod4(x + 2), y, z, c)
    along_y = {d: device(x, mod4(y + d), z, c) for d in (1, 2, 3)}
    along_z = {d: device(x, y, mod4(z + d), c) for d in (1, 2, 3)}

    barrier = pltpu.get_barrier_semaphore()
    partners = [sibling, inner, outer, across, *along_y.values(), *along_z.values()]
    for partner in partners:
        pl.semaphore_signal(barrier, inc=1, device_id=partner, device_id_type=MESH)
    pl.semaphore_wait(barrier, len(partners))

    count = [0]
    sent = []

    def push(src, dst, target, recv=None):
        n = count[0]
        count[0] += 1
        copy = pltpu.make_async_remote_copy(
            src_ref=src, dst_ref=dst, send_sem=ssem.at[n],
            recv_sem=rsem.at[n] if recv is None else recv,
            device_id=target, device_id_type=MESH,
        )
        copy.start()
        sent.append(copy)
        return copy

    local_count = [0]

    def bring(src, dst):
        n = local_count[0]
        local_count[0] += 1
        copy = pltpu.make_async_copy(src, dst, lsem.at[n])
        copy.start()
        return copy

    def rows(start, size):
        return pl.ds(pl.multiple_of(start, 32), size)

    def cols(block, size):
        return pl.ds(pl.multiple_of(block * size, size), size)

    mine, theirs = cols(x_lo, DH), cols(1 - x_lo, DH)
    own_rows, outer_rows = rows(32 * x_lo, 32), rows(32 * (1 - x_lo), 32)

    from_outer = {}
    for off in (0, 1, 3, 2):
        q = mod4(z + off)
        from_outer[off] = [
            push(src.at[c, q, :, theirs], buf.at[a, q, c, own_rows, :], outer)
            for a, src in enumerate((tok, grd))
        ]
    own = [
        bring(src.at[h, :, :, mine], buf.at[a, :, h, own_rows, :])
        for a, src in enumerate((tok, grd))
        for h in (0, 1)
    ]
    own_w = bring(w.at[:, y], wbuf.at[:, :, cols(y, B)])

    for copy in own:
        copy.wait()
    for copy in from_outer[0]:
        copy.wait_recv()
    from_y = [
        push(buf.at[:, z, c, 0:64, :], buf.at[:, z, c, 64 * (4 - d) : 64 * (5 - d), :], along_y[d])
        for d in (1, 3, 2)
    ]
    from_w = [
        push(w.at[:, mod4(y + d)], wbuf.at[:, :, cols(y, B)], along_y[d]) for d in (1, 3, 2)
    ]
    core_outer = []
    for off in (0, 1, 3, 2):
        q = mod4(z + off)
        if off:
            for copy in from_outer[off]:
                copy.wait_recv()
        part_ref = buf.at[:, q, c, outer_rows, :]
        core_outer.append(push(part_ref, part_ref, sibling))

    def piece(q):
        return buf.at[:, q, c, 64:256, :]

    for copy in from_y:
        copy.wait_recv()
    up = push(piece(z), piece(z), along_z[1])
    down = push(piece(z), piece(z), along_z[3])
    core_piece = {0: push(piece(z), piece(z), sibling)}

    own_w.wait()
    for copy in from_w:
        copy.wait_recv()

    offs = (0, 1, 3, 2)
    exchange = {}

    def forward(i):
        q = mod4(z + offs[i])

        def half(h, carry):
            at = cols(h, 256)
            weights = wbuf[...]
            part[i, 0 : 2 * Q, at] = dot_nt(
                weights[0:2].reshape(2 * Q, DH), buf[0, q, h]
            ).astype(BF16)
            part[i, 2 * Q :, at] = dot_nt(weights[2], buf[1, q, h]).astype(BF16)
            return carry

        lax.fori_loop(0, 2, half, 0)
        exchange[i] = push(part.at[i], other.at[i], inner)

    def activate(i):
        exchange[i].wait_recv()

        def some(r, carry):
            def full(m):
                at = pl.ds(pl.multiple_of(m * Q + 32 * r, 32), 32)
                return part[i, at, :].astype(F32) + other[i, at, :].astype(F32)

            gate, up_pre, back = full(0), full(1), full(2)
            s = jax.nn.sigmoid(gate)
            silu = gate * s

            def put(m, value):
                acts[i, pl.ds(pl.multiple_of(m * Q + 32 * r, 32), 32), :] = value.astype(BF16)

            put(0, back * up_pre * s * (1.0 + gate * (1.0 - s)))
            put(1, back * silu)
            put(2, silu * up_pre)
            return carry

        lax.fori_loop(0, Q // 32, some, 0)

    def weight_terms(i, n):
        q = mod4(z + offs[i])
        at = cols(n, B)
        return (
            dot_nn(acts[i, 0 : 2 * Q, :], buf[0, q, :, :, at].reshape(CHUNK, B)),
            dot_nn(acts[i, 2 * Q :, :], buf[1, q, :, :, at].reshape(CHUNK, B)),
        )

    def weight_grads(i):
        def block(n, carry):
            both, third = weight_terms(i, n)
            at = cols(n, B)
            if i:
                both = both + acc[0 : 2 * Q, at]
                third = third + acc[2 * Q :, at]
            acc[0 : 2 * Q, at] = both
            acc[2 * Q :, at] = third
            return carry

        lax.fori_loop(0, 4, block, 0)

    from_dw = []

    def last_weight_grads(i):
        for d in (1, 3, 2, 0):
            n = mod4(y + d)
            both, third = weight_terms(i, n)
            at = cols(n, B)
            dws[n, 0:2] = (both + acc[0 : 2 * Q, at]).astype(BF16).reshape(2, Q, B)
            dws[n, 2] = (third + acc[2 * Q :, at]).astype(BF16)
            if d:
                from_dw.append(push(dws.at[n], dw.at[:, y], along_y[d]))
        return bring(dws.at[y], dw.at[:, y])

    core_dx = {}

    def token_grads(i):
        def block(n, carry):
            at = cols(n, B)
            weights = wbuf[0:2, :, at].reshape(2 * Q, B)
            for h in (0, 1):
                left = acts[i, 0 : 2 * Q, 256 * h : 256 * h + 256]
                dxs[i, h, :, at] = dot_tn(left, weights).astype(BF16)
            return carry

        lax.fori_loop(0, 4, block, 0)
        core_dx[i] = push(dxs.at[i, 1 - c], dxr.at[i], sibling)

    from_z = []

    def along_z_grads(i):
        q = mod4(z + offs[i])
        core_dx[i].wait_recv()

        def some(r, carry):
            at = rows(32 * r, 32)
            dxs[i, c, at, :] = (
                dxs[i, c, at, :].astype(F32) + dxr[i, at, :].astype(F32)
            ).astype(BF16)
            return carry

        lax.fori_loop(0, 8, some, 0)
        for d in (1, 3, 2):
            at = rows(64 * mod4(z + d - y), 64)
            push(dxs.at[i, c, at, :], zr.at[q, d - 1], along_z[d], zsem.at[q, d - 1])

    for copy in core_outer:
        copy.wait_recv()
    core_piece[0].wait_recv()
    forward(0)
    up.wait_recv()
    q = mod4(z + 3)
    on_up = push(buf.at[0, q, c, 64:256, :], buf.at[0, q, c, 64:256, :], along_z[1])
    core_piece[3] = push(piece(q), piece(q), sibling)
    down.wait_recv()
    q = mod4(z + 1)
    on_down = push(buf.at[1, q, c, 64:256, :], buf.at[1, q, c, 64:256, :], along_z[3])
    core_piece[1] = push(piece(q), piece(q), sibling)
    core_piece[3].wait_recv()
    core_piece[1].wait_recv()
    forward(1)
    forward(2)
    activate(0)
    weight_grads(0)
    token_grads(0)
    on_up.wait_recv()
    on_down.wait_recv()
    q = mod4(z + 2)
    core_piece[2] = push(piece(q), piece(q), sibling)
    along_z_grads(0)
    core_piece[2].wait_recv()
    forward(3)
    activate(1)
    weight_grads(1)
    token_grads(1)
    activate(2)
    along_z_grads(1)
    weight_grads(2)
    token_grads(2)
    activate(3)
    along_z_grads(2)
    own_dw = last_weight_grads(3)
    token_grads(3)
    along_z_grads(3)

    from_yg = {}
    for i in range(4):
        q = mod4(z + offs[i])
        for d in (1, 2, 3):
            pltpu.make_async_remote_copy(
                src_ref=zr.at[q, d - 1], dst_ref=zr.at[q, d - 1], send_sem=ssem.at[0],
                recv_sem=zsem.at[q, d - 1], device_id=along_z[d], device_id_type=MESH,
            ).wait_recv()
    for i in range(4):
        q = mod4(z + offs[i])
        keep = rows(64 * mod4(z - y), 64)
        total = dxs[i, c, keep, :].astype(F32)
        for d in (0, 1, 2):
            total = total + zr[q, d].astype(F32)
        ys[i] = total.astype(BF16)
        for d in (1, 3, 2):
            from_yg[i, d] = push(ys.at[i, :, cols(mod4(y + d), B)], yr.at[i, d - 1], along_y[d])
    for i in range(4):
        q = mod4(z + offs[i])
        total = ys[i, :, cols(y, B)].astype(F32)
        for d in (1, 2, 3):
            from_yg[i, d].wait_recv()
            total = total + yr[i, d - 1].astype(F32)
        xs[0, q] = total[0:32].astype(BF16)
        xs[1, q] = total[32:64].astype(BF16)
    from_x = push(xs.at[1 - x_hi], xr, across)
    from_x.wait_recv()
    dx[...] = (xs[x_hi].astype(F32) + xr[...].astype(F32)).astype(BF16).reshape(128, B)

    own_dw.wait()
    for copy in from_dw:
        copy.wait_recv()
    for copy in sent:
        copy.wait_send()


def local(tokens, gate_weight, up_weight, down_weight, grad_out):
    w = jnp.stack([gate_weight.T, up_weight.T, down_weight]).reshape(3, 4, Q, B)
    flops = 8 * 2 * 2048 * 2048 * 256
    dw, dx = pl.pallas_call(
        kernel,
        out_shape=(
            jax.ShapeDtypeStruct((3, 4, Q, B), BF16),
            jax.ShapeDtypeStruct((128, B), BF16),
        ),
        in_specs=[pl.BlockSpec(memory_space=pl.ANY)] * 3,
        out_specs=(
            pl.BlockSpec(memory_space=pl.ANY),
            pl.BlockSpec(memory_space=pltpu.VMEM),
        ),
        scratch_shapes=[
            pltpu.VMEM((2, 4, 2, 256, DH), BF16),
            pltpu.VMEM((3, Q, DH), BF16),
            pltpu.VMEM((4, 3 * Q, CHUNK), BF16),
            pltpu.VMEM((4, 3 * Q, CHUNK), BF16),
            pltpu.VMEM((4, 3 * Q, CHUNK), BF16),
            pltpu.VMEM((3 * Q, DH), F32),
            pltpu.VMEM((4, 3, Q, B), BF16),
            pltpu.VMEM((4, 2, 256, DH), BF16),
            pltpu.VMEM((4, 256, DH), BF16),
            pltpu.VMEM((4, 3, 64, DH), BF16),
            pltpu.VMEM((4, 64, DH), BF16),
            pltpu.VMEM((4, 3, 64, B), BF16),
            pltpu.VMEM((2, 4, 32, B), BF16),
            pltpu.VMEM((4, 32, B), BF16),
            pltpu.SemaphoreType.DMA((72,)),
            pltpu.SemaphoreType.DMA((72,)),
            pltpu.SemaphoreType.DMA((8,)),
            pltpu.SemaphoreType.DMA((4, 3)),
        ],
        compiler_params=pltpu.CompilerParams(
            collective_id=0, has_side_effects=True, vmem_limit_bytes=60 * 2**20
        ),
        cost_estimate=pl.CostEstimate(flops=flops, bytes_accessed=2**24, transcendentals=2**20),
    )(tokens.reshape(2, 4, 32, 4096), grad_out.reshape(2, 4, 32, 4096), w)
    dw = dw.reshape(3, 4 * Q, B)
    return (dx, dw[0].T.astype(F32), dw[1].T.astype(F32), dw[2].astype(F32))


def solution(mesh):
    return jax.shard_map(
        local,
        mesh=mesh,
        in_specs=(
            P("grp", None),
            P("grp", "shard"),
            P("grp", "shard"),
            P("shard", "grp"),
            P("grp", None),
        ),
        out_specs=(P("shard", "grp"), P("grp", "shard"), P("grp", "shard"), P("shard", "grp")),
        check_vma=False,
    )
```

```python
import functools

import jax
import jax.numpy as jnp
from jax import lax
from jax.experimental import pallas as pl
from jax.experimental.pallas import tpu as pltpu
from jax.sharding import PartitionSpec as P

MESH = pl.DeviceIdType.MESH
BF16 = jnp.bfloat16
F32 = jnp.float32

Q = 224
DH = 2048
B = 512
CHUNK = 512
PARTS = ((0, 112), (112, 112))
PARTS = ((0, 112), (112, 112))
PARTS = ((0, 112), (112, 112))


def dot_nt(left, right):
    return lax.dot_general(left, right, (((1,), (1,)), ((), ())), preferred_element_type=F32)


def dot_nn(left, right):
    return lax.dot_general(left, right, (((1,), (0,)), ((), ())), preferred_element_type=F32)


def dot_tn(left, right):
    return lax.dot_general(left, right, (((0,), (0,)), ((), ())), preferred_element_type=F32)


def kernel(
    tok, grd, gate_w, up_w, down_w, dgate, dup, ddown, dx,
    buf, raw, wt, wbuf, part, other, acc, back, dxs, dxr, zr, ys, yr, xs, xr,
    ssem, rsem, lsem, zsem, lastsem,
):
    grp, shard = lax.axis_index("grp"), lax.axis_index("shard")
    x_lo, y = lax.div(grp, 4), lax.rem(grp, 4)
    x_hi, z, c = lax.div(shard, 8), lax.rem(lax.div(shard, 2), 4), lax.rem(shard, 2)
    x = 2 * x_hi + x_lo

    def mod4(v):
        return lax.rem(v + 8, 4)

    def slot(dy):
        return dy + lax.div(dy, 2) * (1 - 2 * lax.rem(dy, 2))

    def device(x, y, z, c):
        return (4 * lax.rem(x, 2) + y, 8 * lax.div(x, 2) + 2 * z + c)

    sibling = device(x, y, z, 1 - c)
    inner = device(x + 1 - 2 * x_lo, y, z, c)
    outer = device(mod4(x - 1 + 2 * x_lo), y, z, c)
    across = device(mod4(x + 2), y, z, c)
    along_y = {d: device(x, mod4(y + d), z, c) for d in (1, 2, 3)}
    along_z = {d: device(x, y, mod4(z + d), c) for d in (1, 2, 3)}

    barrier = pltpu.get_barrier_semaphore()
    partners = [sibling, inner, outer, across, *along_y.values(), *along_z.values()]
    for partner in partners:
        pl.semaphore_signal(barrier, inc=1, device_id=partner, device_id_type=MESH)
    pl.semaphore_wait(barrier, len(partners))

    count = [0]
    sent = []

    def push(src, dst, target, recv=None):
        n = count[0]
        count[0] += 1
        copy = pltpu.make_async_remote_copy(
            src_ref=src, dst_ref=dst, send_sem=ssem.at[n],
            recv_sem=rsem.at[n] if recv is None else recv,
            device_id=target, device_id_type=MESH,
        )
        copy.start()
        sent.append(copy)
        return copy

    local_count = [0]

    def bring(src, dst):
        n = local_count[0]
        local_count[0] += 1
        copy = pltpu.make_async_copy(src, dst, lsem.at[n])
        copy.start()
        return copy

    def arrived(*copies):
        for copy in copies:
            copy.wait_recv()

    gone = set()

    def left(*copies):
        for copy in copies:
            if id(copy) not in gone:
                gone.add(id(copy))
                copy.wait_send()

    def rows(start, size, step=32):
        return pl.ds(pl.multiple_of(start, step), size)

    def cols(block, size):
        return pl.ds(pl.multiple_of(block * size, size), size)

    mine, theirs = cols(x_lo, DH), cols(1 - x_lo, DH)
    own_rows, outer_rows = rows(32 * x_lo, 32), rows(32 * (1 - x_lo), 32)
    offs = (0, 1, 3, 2)
    quarter = [mod4(z + off) for off in offs]

    from_outer = [
        [
            push(src.at[c, q, :, theirs], buf.at[a, q, c, own_rows, :], outer)
            for a, src in enumerate((tok, grd))
        ]
        for q in quarter
    ]
    own_tok = [
        bring(src.at[h, :, :, mine], buf.at[a, :, h, own_rows, :])
        for h in (0, 1)
        for a, src in enumerate((tok, grd))
    ]
    own_raw = [bring(gate_w, raw.at[0]), bring(up_w, raw.at[1]), bring(down_w, wt.at[2])]

    for copy in own_tok:
        copy.wait()
    arrived(*from_outer[0])

    def send_y(d):
        at = {1: 2, 3: 1, 2: 3}[d] * 64
        return push(buf.at[:, z, c, 0:64, :], buf.at[:, z, c, at : at + 64, :], along_y[d])

    y_near = [send_y(1), send_y(3)]
    y_far = send_y(2)

    def outer_to_sibling(i):
        ref = buf.at[:, quarter[i], c, outer_rows, :]
        return push(ref, ref, sibling)

    core_outer = [outer_to_sibling(0)]

    for copy in own_raw:
        copy.wait()
    for m in (0, 1):
        def turn(n, carry):
            wt[m, cols(n, 128), :] = raw[m, :, cols(n, 128)].T
            return carry

        lax.fori_loop(0, 7, turn, 0)
    own_w = bring(wt.at[:, rows(Q * y, Q), :], wbuf.at[:, :, cols(y, B)])

    def near(a, q):
        return buf.at[a, q, c, 64:192, :]

    def far(a, q):
        return buf.at[a, q, c, 192:256, :]

    both = slice(None)
    core_piece = {}

    def to_sibling(i, which, a=both):
        ref = which(a, quarter[i])
        core_piece.setdefault(i, []).append(push(ref, ref, sibling))

    def spread(which):
        ref = which(both, z)
        return push(ref, ref, along_z[1]), push(ref, ref, along_z[3])

    arrived(*y_near)
    near_up, near_down = spread(near)
    to_sibling(0, near)
    for i in (1, 2, 3):
        arrived(*from_outer[i])
        core_outer.append(outer_to_sibling(i))
    arrived(y_far)
    far_up, far_down = spread(far)
    to_sibling(0, far)

    def send_w(h):
        start, size = PARTS[h]
        return [
            push(
                wt.at[:, rows(Q * mod4(y + d) + start, size, 16), :],
                wbuf.at[:, start : start + size, cols(y, B)],
                along_y[d],
            )
            for d in (1, 3, 2)
        ]

    from_w = [send_w(h) for h in range(len(PARTS))]

    def onward(which, up, down):
        arrived(up)
        ref = which(0, quarter[2])
        on_up = push(ref, ref, along_z[1])
        to_sibling(2, which)
        arrived(down)
        ref = which(1, quarter[1])
        on_down = push(ref, ref, along_z[3])
        to_sibling(1, which)
        return on_up, on_down

    exchange = {}

    def forward(i, h):
        q = quarter[i]
        start, size = PARTS[h]
        hidden = slice(start, start + size)

        def half(g, carry):
            at = cols(g, 256)
            part[i, 0:2, hidden, at] = dot_nt(
                wbuf[0:2, hidden, :].reshape(2 * size, DH), buf[0, q, g]
            ).astype(BF16).reshape(2, size, 256)
            part[i, 2, hidden, at] = dot_nt(wbuf[2, hidden, :], buf[1, q, g]).astype(BF16)
            return carry

        lax.fori_loop(0, 2, half, 0)
        exchange[i, h] = push(part.at[i, :, hidden, :], other.at[i, :, hidden, :], inner)

    def activate(i, h):
        arrived(exchange[i, h])
        left(exchange[i, h])
        start, size = PARTS[h]

        def some(r, carry):
            at = rows(start + 16 * r, 16, 16)

            def full(m):
                return part[i, m, at, :].astype(F32) + other[i, m, at, :].astype(F32)

            gate, up_pre, back_grad = full(0), full(1), full(2)
            s = jax.nn.sigmoid(gate)
            silu = gate * s
            part[i, 0, at, :] = (back_grad * up_pre * s * (1.0 + gate * (1.0 - s))).astype(BF16)
            part[i, 1, at, :] = (back_grad * silu).astype(BF16)
            part[i, 2, at, :] = (silu * up_pre).astype(BF16)
            return carry

        lax.fori_loop(0, size // 16, some, 0)

    def weight_terms(i, h, n):
        q = quarter[i]
        start, size = PARTS[h]
        hidden = slice(start, start + size)
        at = cols(n, B)
        return (
            dot_nn(
                part[i, 0:2, hidden, :].reshape(2 * size, CHUNK),
                buf[0, q, :, :, at].reshape(CHUNK, B),
            ).reshape(2, size, B),
            dot_nn(part[i, 2, hidden, :], buf[1, q, :, :, at].reshape(CHUNK, B)),
        )

    def weight_grads(i, h):
        start, size = PARTS[h]
        hidden = slice(start, start + size)

        def block(n, carry):
            pair, third = weight_terms(i, h, n)
            at = cols(n, B)
            if i:
                pair = pair + acc[0:2, hidden, at]
                third = third + acc[2, hidden, at]
            acc[0:2, hidden, at] = pair
            acc[2, hidden, at] = third
            return carry

        lax.fori_loop(0, 4, block, 0)

    from_dw, own_dw = {}, []

    def last_weight_grads(i, h):
        if h == 0:
            for copies in from_w:
                for copy in copies:
                    left(copy)
        start, size = PARTS[h]
        hidden = slice(start, start + size)
        from_dw[h] = []
        for d in (1, 3, 2, 0):
            n = mod4(y + d)
            pair, third = weight_terms(i, h, n)
            at = cols(n, B)
            held = rows(Q * n + start, size, 16)
            wt[0:2, held, :] = (pair + acc[0:2, hidden, at]).astype(BF16)
            wt[2, held, :] = (third + acc[2, hidden, at]).astype(BF16)
            there = rows(Q * y + start, size, 16)
            if d:
                from_dw[h].append(push(wt.at[0:2, held, :], back.at[:, there, :], along_y[d]))
                from_dw[h].append(push(wt.at[2, held, :], ddown.at[there, :], along_y[d]))
            else:
                own_dw.append(bring(wt.at[0:2, held, :], back.at[:, there, :]))
                own_dw.append(bring(wt.at[2, held, :], ddown.at[there, :]))

    def token_terms(i, n, g):
        at = cols(n, B)
        return dot_tn(
            part[i, 0:2, :, 256 * g : 256 * g + 256].reshape(2 * Q, 256),
            wbuf[0:2, :, at].reshape(2 * Q, B),
        ).astype(BF16)

    core_dx = {}

    def token_grads(i):
        def block(n, carry):
            for g in (0, 1):
                dxs[i, g, :, cols(n, B)] = token_terms(i, n, g)
            return carry

        lax.fori_loop(0, 4, block, 0)
        core_dx[i] = push(dxs.at[i, 1 - c], dxr.at[i], sibling)

    def z_rows(d):
        return rows(64 * slot(mod4(z + d - y)), 64)

    def along_z_grads(i):
        arrived(core_dx[i])

        def some(r, carry):
            at = rows(32 * r, 32)
            dxs[i, c, at, :] = (
                dxs[i, c, at, :].astype(F32) + dxr[i, at, :].astype(F32)
            ).astype(BF16)
            return carry

        lax.fori_loop(0, 8, some, 0)
        for d in (1, 3, 2):
            push(
                dxs.at[i, c, z_rows(d), :], zr.at[quarter[i], d - 1], along_z[d],
                zsem.at[quarter[i], d - 1],
            )

    def last_token_grads(i):
        core_last = {}
        for d in (1, 3, 2, 0):
            n = mod4(y + d)
            for g in (0, 1):
                dxs[i, g, :, cols(n, B)] = token_terms(i, n, g)
            core_last[d] = push(
                dxs.at[i, 1 - c, :, cols(n, B)], dxr.at[i, :, cols(n, B)], sibling
            )
        return core_last

    def last_along_z(i, core_last):
        for k, d in enumerate((1, 3, 2, 0)):
            at = cols(mod4(y + d), B)
            arrived(core_last[d])
            dxs[i, c, :, at] = (
                dxs[i, c, :, at].astype(F32) + dxr[i, :, at].astype(F32)
            ).astype(BF16)
            for e in (1, 3, 2):
                push(
                    dxs.at[i, c, z_rows(e), at], zr.at[quarter[i], e - 1, :, at], along_z[e],
                    lastsem.at[k, e - 1],
                )

    near_on = onward(near, near_up, near_down)
    arrived(*core_outer, *core_piece[0])
    own_w.wait()
    arrived(*from_w[0])
    forward(0, 0)
    far_on = onward(far, far_up, far_down)
    arrived(*core_piece[1])
    forward(1, 0)
    arrived(*core_piece[2])
    forward(2, 0)
    arrived(*from_w[1])
    forward(0, 1)
    activate(0, 0)
    weight_grads(0, 0)
    arrived(*near_on)
    to_sibling(3, near)
    activate(1, 0)
    weight_grads(1, 0)
    arrived(*far_on)
    to_sibling(3, far)
    arrived(*core_piece[3])
    forward(3, 0)
    forward(1, 1)
    forward(2, 1)
    forward(3, 1)
    activate(2, 0)
    weight_grads(2, 0)
    activate(0, 1)
    token_grads(0)
    weight_grads(0, 1)
    activate(3, 0)
    last_weight_grads(3, 0)
    along_z_grads(0)
    activate(1, 1)
    token_grads(1)
    weight_grads(1, 1)
    along_z_grads(1)
    activate(2, 1)
    token_grads(2)
    weight_grads(2, 1)
    along_z_grads(2)
    activate(3, 1)
    core_last = last_token_grads(3)
    last_weight_grads(3, 1)
    last_along_z(3, core_last)

    def landed(ref, sem):
        pltpu.make_async_remote_copy(
            src_ref=ref, dst_ref=ref, send_sem=ssem.at[0], recv_sem=sem,
            device_id=along_z[1], device_id_type=MESH,
        ).wait_recv()

    for d in (1, 2, 3):
        for off in (0, 1, 3):
            q = mod4(z - d + off)
            landed(zr.at[q, d - 1], zsem.at[q, d - 1])
    keep = z_rows(0)
    from_yg = {}
    for k, d in enumerate((1, 3, 2, 0)):
        at = cols(mod4(y + d), B)
        for e in (1, 2, 3):
            landed(zr.at[mod4(z - e + 2), e - 1, :, at], lastsem.at[k, e - 1])

        for i in range(4):
            q = quarter[i]
            total = dxs[i, c, keep, at].astype(F32)
            for e in (0, 1, 2):
                total = total + zr[q, e, :, at].astype(F32)
            ys[q, :, at] = total.astype(BF16)
        if d:
            from_yg[d] = push(ys.at[:, :, at], yr.at[d - 1], along_y[d])
    for copy in own_dw:
        copy.wait()
    arrived(*from_dw[0], *from_dw[1])
    for m, out in enumerate((dgate, dup)):
        def turn(n, carry):
            out[:, cols(n, 128)] = back[m, cols(n, 128), :].T
            return carry

        lax.fori_loop(0, 7, turn, 0)
    for d in (1, 3, 2):
        arrived(from_yg[d])
    for q in range(4):
        total = ys[q, :, cols(y, B)].astype(F32)
        for d in (0, 1, 2):
            total = total + yr[d, q].astype(F32)
        xs[0, q] = total[0:32].astype(BF16)
        xs[1, q] = total[32:64].astype(BF16)
    from_x = push(xs.at[1 - x_hi], xr, across)
    arrived(from_x)
    dx[...] = (xs[x_hi].astype(F32) + xr[...].astype(F32)).astype(BF16).reshape(128, B)
    left(*sent)


def local(tokens, gate_weight, up_weight, down_weight, grad_out):
    flops = 8 * 2 * 2048 * 2048 * 256
    dgate, dup, ddown, dx = pl.pallas_call(
        kernel,
        out_shape=(
            jax.ShapeDtypeStruct((B, 4 * Q), BF16),
            jax.ShapeDtypeStruct((B, 4 * Q), BF16),
            jax.ShapeDtypeStruct((4 * Q, B), BF16),
            jax.ShapeDtypeStruct((128, B), BF16),
        ),
        in_specs=[pl.BlockSpec(memory_space=pl.ANY)] * 5,
        out_specs=(
            pl.BlockSpec(memory_space=pltpu.VMEM),
            pl.BlockSpec(memory_space=pltpu.VMEM),
            pl.BlockSpec(memory_space=pl.ANY),
            pl.BlockSpec(memory_space=pltpu.VMEM),
        ),
        scratch_shapes=[
            pltpu.VMEM((2, 4, 2, 256, DH), BF16),
            pltpu.VMEM((2, B, 4 * Q), BF16),
            pltpu.VMEM((3, 4 * Q, B), BF16),
            pltpu.VMEM((3, Q, DH), BF16),
            pltpu.VMEM((4, 3, Q, CHUNK), BF16),
            pltpu.VMEM((4, 3, Q, CHUNK), BF16),
            pltpu.VMEM((3, Q, DH), F32),
            pltpu.VMEM((2, 4 * Q, B), BF16),
            pltpu.VMEM((4, 2, 256, DH), BF16),
            pltpu.VMEM((4, 256, DH), BF16),
            pltpu.VMEM((4, 3, 64, DH), BF16),
            pltpu.VMEM((4, 64, DH), BF16),
            pltpu.VMEM((3, 4, 64, B), BF16),
            pltpu.VMEM((2, 4, 32, B), BF16),
            pltpu.VMEM((4, 32, B), BF16),
            pltpu.SemaphoreType.DMA((96,)),
            pltpu.SemaphoreType.DMA((96,)),
            pltpu.SemaphoreType.DMA((16,)),
            pltpu.SemaphoreType.DMA((4, 3)),
            pltpu.SemaphoreType.DMA((4, 3)),
        ],
        compiler_params=pltpu.CompilerParams(
            collective_id=0, has_side_effects=True, vmem_limit_bytes=62 * 2**20
        ),
        cost_estimate=pl.CostEstimate(flops=flops, bytes_accessed=2**24, transcendentals=2**20),
    )(
        tokens.reshape(2, 4, 32, 4096), grad_out.reshape(2, 4, 32, 4096),
        gate_weight, up_weight, down_weight,
    )
    return (dx, dgate.astype(F32), dup.astype(F32), ddown.astype(F32))


def solution(mesh):
    return jax.shard_map(
        local,
        mesh=mesh,
        in_specs=(
            P("grp", None),
            P("grp", "shard"),
            P("grp", "shard"),
            P("shard", "grp"),
            P("grp", None),
        ),
        out_specs=(P("shard", "grp"), P("grp", "shard"), P("grp", "shard"), P("shard", "grp")),
        check_vma=False,
    )
```

```python
import functools

import jax
import jax.numpy as jnp
from jax import lax
from jax.experimental import pallas as pl
from jax.experimental.pallas import tpu as pltpu
from jax.sharding import PartitionSpec as P

MESH = pl.DeviceIdType.MESH
BF16 = jnp.bfloat16
F32 = jnp.float32

Q = 224
DH = 2048
B = 512
CHUNK = 512
PARTS = ((0, 128), (128, 96))


def dot_nt(left, right):
    return lax.dot_general(left, right, (((1,), (1,)), ((), ())), preferred_element_type=F32)


def dot_nn(left, right):
    return lax.dot_general(left, right, (((1,), (0,)), ((), ())), preferred_element_type=F32)


def dot_tn(left, right):
    return lax.dot_general(left, right, (((0,), (0,)), ((), ())), preferred_element_type=F32)


def kernel(
    tok, grd, gate_w, up_w, down_w, dgate, dup, ddown, dx,
    buf, raw, wt, wbuf, part, other, acc, back, dxs, dxr, zr, ys, xr, yr,
    ssem, rsem, lsem, zsem, lastsem,
):
    grp, shard = lax.axis_index("grp"), lax.axis_index("shard")
    x_lo, y = lax.div(grp, 4), lax.rem(grp, 4)
    x_hi, z, c = lax.div(shard, 8), lax.rem(lax.div(shard, 2), 4), lax.rem(shard, 2)
    x = 2 * x_hi + x_lo

    def mod4(v):
        return lax.rem(v + 8, 4)

    def slot(dy):
        return dy + lax.div(dy, 2) * (1 - 2 * lax.rem(dy, 2))

    def device(x, y, z, c):
        return (4 * lax.rem(x, 2) + y, 8 * lax.div(x, 2) + 2 * z + c)

    sibling = device(x, y, z, 1 - c)
    inner = device(x + 1 - 2 * x_lo, y, z, c)
    outer = device(mod4(x - 1 + 2 * x_lo), y, z, c)
    across = device(mod4(x + 2), y, z, c)
    along_y = {d: device(x, mod4(y + d), z, c) for d in (1, 2, 3)}
    along_z = {d: device(x, y, mod4(z + d), c) for d in (1, 2, 3)}

    barrier = pltpu.get_barrier_semaphore()
    partners = [sibling, inner, outer, across, *along_y.values(), *along_z.values()]
    for partner in partners:
        pl.semaphore_signal(barrier, inc=1, device_id=partner, device_id_type=MESH)
    pl.semaphore_wait(barrier, len(partners))

    count = [0]
    sent = []

    def push(src, dst, target, recv=None):
        n = count[0]
        count[0] += 1
        copy = pltpu.make_async_remote_copy(
            src_ref=src, dst_ref=dst, send_sem=ssem.at[n],
            recv_sem=rsem.at[n] if recv is None else recv,
            device_id=target, device_id_type=MESH,
        )
        copy.start()
        sent.append(copy)
        return copy

    local_count = [0]

    def bring(src, dst):
        n = local_count[0]
        local_count[0] += 1
        copy = pltpu.make_async_copy(src, dst, lsem.at[n])
        copy.start()
        return copy

    def arrived(*copies):
        for copy in copies:
            copy.wait_recv()

    gone = set()

    def left(*copies):
        for copy in copies:
            if id(copy) not in gone:
                gone.add(id(copy))
                copy.wait_send()

    def rows(start, size, step=32):
        return pl.ds(pl.multiple_of(start, step), size)

    def cols(block, size):
        return pl.ds(pl.multiple_of(block * size, size), size)

    mine, theirs = cols(x_lo, DH), cols(1 - x_lo, DH)
    own_rows, outer_rows = rows(32 * x_lo, 32), rows(32 * (1 - x_lo), 32)
    offs = (0, 1, 3, 2)
    quarter = [mod4(z + off) for off in offs]

    def send_outer(i):
        q = quarter[i]
        return [
            push(src.at[c, q, :, theirs], buf.at[a, q, c, own_rows, :], outer)
            for a, src in enumerate((tok, grd))
        ]

    from_outer = [send_outer(0)]
    own_tok = [
        bring(src.at[h, :, :, mine], buf.at[a, :, h, own_rows, :])
        for h in (0, 1)
        for a, src in enumerate((tok, grd))
    ]
    own_raw = [bring(gate_w, raw.at[0]), bring(up_w, raw.at[1]), bring(down_w, wt.at[2])]
    for copy in own_raw:
        copy.wait()
    for m in (0, 1):
        def turn(n, carry):
            wt[m, cols(n, 128), :] = raw[m, :, cols(n, 128)].T
            return carry

        lax.fori_loop(0, 7, turn, 0)
    own_w = bring(wt.at[:, rows(Q * y, Q), :], wbuf.at[:, :, cols(y, B)])

    first, second = x_hi, 1 - x_hi
    for copy in own_tok:
        copy.wait()
    arrived(*from_outer[0])

    def send_y(d):
        at = {1: 2, 3: 1, 2: 3}[d] * 64
        return push(
            buf.at[first, z, c, 0:64, :], buf.at[first, z, c, at : at + 64, :], along_y[d]
        )

    y_near = [send_y(1), send_y(3)]
    y_far = send_y(2)

    def send_w(h):
        start, size = PARTS[h]
        return [
            push(
                wt.at[:, rows(Q * mod4(y + d) + start, size, 16), :],
                wbuf.at[:, start : start + size, cols(y, B)],
                along_y[d],
            )
            for d in (1, 3, 2)
        ]

    from_w = [send_w(h) for h in range(len(PARTS))]

    def outer_to_sibling(i):
        ref = buf.at[:, quarter[i], c, outer_rows, :]
        return push(ref, ref, sibling)

    core_outer = [outer_to_sibling(0)]

    def near(a, q):
        return buf.at[a, q, c, 64:192, :]

    def far(a, q):
        return buf.at[a, q, c, 192:256, :]

    core_piece = {0: [], 1: [], 2: [], 3: []}

    def to_sibling(i, which, a):
        ref = which(a, quarter[i])
        core_piece[i].append(push(ref, ref, sibling))

    from_z = {}

    def spread(which, a, name):
        ref = which(a, z)
        from_z[name] = push(ref, ref, along_z[1]), push(ref, ref, along_z[3])
        to_sibling(0, which, a)

    arrived(*y_near)
    swap_near = push(near(first, z), near(first, z), across)
    spread(near, first, "near 0")
    arrived(y_far)
    swap_far = push(far(first, z), far(first, z), across)
    spread(far, first, "far 0")
    from_outer += [send_outer(i) for i in (1, 2, 3)]
    arrived(swap_near)
    spread(near, second, "near 1")

    onward = []

    def relay(which, name):
        up, down = from_z[name]
        kind = 0 if name.endswith("0") else 1
        a = second if kind else first
        arrived(up)
        if kind == 0:
            ref = which(a, quarter[2])
            onward.append((push(ref, ref, along_z[1]), which, a))
        to_sibling(2, which, a)
        arrived(down)
        if kind == 1:
            ref = which(a, quarter[1])
            onward.append((push(ref, ref, along_z[3]), which, a))
        to_sibling(1, which, a)

    exchange = {}

    def forward(i, h):
        q = quarter[i]
        start, size = PARTS[h]
        hidden = slice(start, start + size)

        def half(g, carry):
            at = cols(g, 256)
            part[i, 0:2, hidden, at] = dot_nt(
                wbuf[0:2, hidden, :].reshape(2 * size, DH), buf[0, q, g]
            ).astype(BF16).reshape(2, size, 256)
            part[i, 2, hidden, at] = dot_nt(wbuf[2, hidden, :], buf[1, q, g]).astype(BF16)
            return carry

        lax.fori_loop(0, 2, half, 0)
        exchange[i, h] = push(part.at[i, :, hidden, :], other.at[i, :, hidden, :], inner)

    def activate(i, h):
        arrived(exchange[i, h])
        left(exchange[i, h])
        start, size = PARTS[h]

        def some(r, carry):
            at = rows(start + 16 * r, 16, 16)

            def full(m):
                return part[i, m, at, :].astype(F32) + other[i, m, at, :].astype(F32)

            gate, up_pre, back_grad = full(0), full(1), full(2)
            s = jax.nn.sigmoid(gate)
            silu = gate * s
            part[i, 0, at, :] = (back_grad * up_pre * s * (1.0 + gate * (1.0 - s))).astype(BF16)
            part[i, 1, at, :] = (back_grad * silu).astype(BF16)
            part[i, 2, at, :] = (silu * up_pre).astype(BF16)
            return carry

        lax.fori_loop(0, size // 16, some, 0)

    def weight_terms(i, h, n):
        q = quarter[i]
        start, size = PARTS[h]
        hidden = slice(start, start + size)
        at = cols(n, B)
        return (
            dot_nn(
                part[i, 0:2, hidden, :].reshape(2 * size, CHUNK),
                buf[0, q, :, :, at].reshape(CHUNK, B),
            ).reshape(2, size, B),
            dot_nn(part[i, 2, hidden, :], buf[1, q, :, :, at].reshape(CHUNK, B)),
        )

    def weight_grads(i, h):
        start, size = PARTS[h]
        hidden = slice(start, start + size)

        def block(n, carry):
            pair, third = weight_terms(i, h, n)
            at = cols(n, B)
            if i:
                pair = pair + acc[0:2, hidden, at]
                third = third + acc[2, hidden, at]
            acc[0:2, hidden, at] = pair
            acc[2, hidden, at] = third
            return carry

        lax.fori_loop(0, 4, block, 0)

    from_dw, own_dw = {}, []

    def last_weight_grads(i, h):
        if h == 0:
            for copies in from_w:
                for copy in copies:
                    left(copy)
        start, size = PARTS[h]
        hidden = slice(start, start + size)
        from_dw[h] = []
        for d in (1, 3, 2, 0):
            n = mod4(y + d)
            pair, third = weight_terms(i, h, n)
            at = cols(n, B)
            held = rows(Q * n + start, size, 16)
            wt[0:2, held, :] = (pair + acc[0:2, hidden, at]).astype(BF16)
            wt[2, held, :] = (third + acc[2, hidden, at]).astype(BF16)
            there = rows(Q * y + start, size, 16)
            if d:
                from_dw[h].append(push(wt.at[0:2, held, :], back.at[:, there, :], along_y[d]))
                from_dw[h].append(push(wt.at[2, held, :], ddown.at[there, :], along_y[d]))
            else:
                own_dw.append(bring(wt.at[0:2, held, :], back.at[:, there, :]))
                own_dw.append(bring(wt.at[2, held, :], ddown.at[there, :]))

    def token_terms(i, n, g):
        at = cols(n, B)
        return dot_tn(
            part[i, 0:2, :, 256 * g : 256 * g + 256].reshape(2 * Q, 256),
            wbuf[0:2, :, at].reshape(2 * Q, B),
        ).astype(BF16)

    core_dx = {}

    def token_grads(i):
        def block(n, carry):
            for g in (0, 1):
                dxs[i, g, :, cols(n, B)] = token_terms(i, n, g)
            return carry

        lax.fori_loop(0, 4, block, 0)
        core_dx[i] = push(dxs.at[i, 1 - c], dxr.at[i], sibling)

    def z_rows(d):
        return rows(64 * slot(mod4(z + d - y)), 64)

    def along_z_grads(i):
        arrived(core_dx[i])

        def some(r, carry):
            at = rows(32 * r, 32)
            dxs[i, c, at, :] = (
                dxs[i, c, at, :].astype(F32) + dxr[i, at, :].astype(F32)
            ).astype(BF16)
            return carry

        lax.fori_loop(0, 8, some, 0)
        for d in (1, 3, 2):
            push(
                dxs.at[i, c, z_rows(d), :], zr.at[quarter[i], d - 1], along_z[d],
                zsem.at[quarter[i], d - 1],
            )

    def last_token_grads(i):
        core_last = {}
        for d in (1, 3, 2, 0):
            n = mod4(y + d)
            for g in (0, 1):
                dxs[i, g, :, cols(n, B)] = token_terms(i, n, g)
            core_last[d] = push(
                dxs.at[i, 1 - c, :, cols(n, B)], dxr.at[i, :, cols(n, B)], sibling
            )
        return core_last

    def last_along_z(i, core_last):
        for k, d in enumerate((1, 3, 2, 0)):
            at = cols(mod4(y + d), B)
            arrived(core_last[d])
            dxs[i, c, :, at] = (
                dxs[i, c, :, at].astype(F32) + dxr[i, :, at].astype(F32)
            ).astype(BF16)
            for e in (1, 3, 2):
                push(
                    dxs.at[i, c, z_rows(e), at], zr.at[quarter[i], e - 1, :, at], along_z[e],
                    lastsem.at[k, e - 1],
                )

    relay(near, "near 0")
    arrived(swap_far)
    spread(far, second, "far 1")
    relay(far, "far 0")
    arrived(*core_outer, *core_piece[0])
    own_w.wait()
    arrived(*from_w[0])
    forward(0, 0)
    for i in (1, 2, 3):
        arrived(*from_outer[i])
        core_outer.append(outer_to_sibling(i))
    relay(near, "near 1")
    arrived(*from_w[1])
    forward(0, 1)
    activate(0, 0)
    relay(far, "far 1")
    weight_grads(0, 0)
    arrived(*core_outer[1:], *core_piece[1])
    forward(1, 0)
    arrived(*core_piece[2])
    forward(2, 0)
    activate(0, 1)
    token_grads(0)
    weight_grads(0, 1)
    along_z_grads(0)
    for copy, which, a in onward:
        arrived(copy)
        to_sibling(3, which, a)
    activate(1, 0)
    weight_grads(1, 0)
    arrived(*core_piece[3])
    forward(3, 0)
    forward(1, 1)
    forward(2, 1)
    forward(3, 1)
    activate(2, 0)
    weight_grads(2, 0)
    activate(3, 0)
    last_weight_grads(3, 0)
    activate(1, 1)
    token_grads(1)
    weight_grads(1, 1)
    along_z_grads(1)
    activate(2, 1)
    token_grads(2)
    weight_grads(2, 1)
    along_z_grads(2)
    activate(3, 1)
    core_last = last_token_grads(3)
    last_weight_grads(3, 1)
    last_along_z(3, core_last)

    def landed(ref, sem):
        pltpu.make_async_remote_copy(
            src_ref=ref, dst_ref=ref, send_sem=ssem.at[0], recv_sem=sem,
            device_id=along_z[1], device_id_type=MESH,
        ).wait_recv()

    for d in (1, 2, 3):
        for off in (0, 1, 3):
            q = mod4(z - d + off)
            landed(zr.at[q, d - 1], zsem.at[q, d - 1])
    keep = z_rows(0)
    from_x, from_yg = [], {}

    def over_x(k, d):
        at = cols(mod4(y + d), B)
        for e in (1, 2, 3):
            landed(zr.at[mod4(z - e + 2), e - 1, :, at], lastsem.at[k, e - 1])

        for i in range(4):
            q = quarter[i]
            total = dxs[i, c, keep, at].astype(F32)
            for e in (0, 1, 2):
                total = total + zr[q, e, :, at].astype(F32)
            total = total.astype(BF16)
            ys[0, q, :, at] = total[0:32]
            ys[1, q, :, at] = total[32:64]
        from_x.append(push(ys.at[1 - x_hi, :, :, at], xr.at[:, :, at], across))

    def over_y(k, d):
        at = cols(mod4(y + d), B)
        arrived(from_x[k])
        ys[x_hi, :, :, at] = (
            ys[x_hi, :, :, at].astype(F32) + xr[:, :, at].astype(F32)
        ).astype(BF16)
        if d:
            from_yg[d] = push(ys.at[x_hi, :, :, at], yr.at[d - 1], along_y[d])

    order = (1, 3, 2, 0)
    over_x(0, order[0])
    for k in (1, 2, 3):
        over_x(k, order[k])
        over_y(k - 1, order[k - 1])
    over_y(3, order[3])
    for copy in own_dw:
        copy.wait()
    arrived(*from_dw[0], *from_dw[1])
    for m, out in enumerate((dgate, dup)):
        def turn(n, carry):
            out[:, cols(n, 128)] = back[m, cols(n, 128), :].T
            return carry

        lax.fori_loop(0, 7, turn, 0)
    total = ys[x_hi, :, :, cols(y, B)].astype(F32)
    for d in (1, 3, 2):
        arrived(from_yg[d])
        total = total + yr[d - 1].astype(F32)
    dx[...] = total.astype(BF16).reshape(128, B)
    left(*sent)


def local(tokens, gate_weight, up_weight, down_weight, grad_out):
    flops = 8 * 2 * 2048 * 2048 * 256
    dgate, dup, ddown, dx = pl.pallas_call(
        kernel,
        out_shape=(
            jax.ShapeDtypeStruct((B, 4 * Q), BF16),
            jax.ShapeDtypeStruct((B, 4 * Q), BF16),
            jax.ShapeDtypeStruct((4 * Q, B), BF16),
            jax.ShapeDtypeStruct((128, B), BF16),
        ),
        in_specs=[pl.BlockSpec(memory_space=pl.ANY)] * 5,
        out_specs=(
            pl.BlockSpec(memory_space=pltpu.VMEM),
            pl.BlockSpec(memory_space=pltpu.VMEM),
            pl.BlockSpec(memory_space=pl.ANY),
            pl.BlockSpec(memory_space=pltpu.VMEM),
        ),
        scratch_shapes=[
            pltpu.VMEM((2, 4, 2, 256, DH), BF16),
            pltpu.VMEM((2, B, 4 * Q), BF16),
            pltpu.VMEM((3, 4 * Q, B), BF16),
            pltpu.VMEM((3, Q, DH), BF16),
            pltpu.VMEM((4, 3, Q, CHUNK), BF16),
            pltpu.VMEM((4, 3, Q, CHUNK), BF16),
            pltpu.VMEM((3, Q, DH), F32),
            pltpu.VMEM((2, 4 * Q, B), BF16),
            pltpu.VMEM((4, 2, 256, DH), BF16),
            pltpu.VMEM((4, 256, DH), BF16),
            pltpu.VMEM((4, 3, 64, DH), BF16),
            pltpu.VMEM((2, 4, 32, DH), BF16),
            pltpu.VMEM((4, 32, DH), BF16),
            pltpu.VMEM((3, 4, 32, B), BF16),
            pltpu.SemaphoreType.DMA((128,)),
            pltpu.SemaphoreType.DMA((128,)),
            pltpu.SemaphoreType.DMA((16,)),
            pltpu.SemaphoreType.DMA((4, 3)),
            pltpu.SemaphoreType.DMA((4, 3)),
        ],
        compiler_params=pltpu.CompilerParams(
            collective_id=0, has_side_effects=True, vmem_limit_bytes=62 * 2**20
        ),
        cost_estimate=pl.CostEstimate(flops=flops, bytes_accessed=2**24, transcendentals=2**20),
    )(
        tokens.reshape(2, 4, 32, 4096), grad_out.reshape(2, 4, 32, 4096),
        gate_weight, up_weight, down_weight,
    )
    return (dx, dgate.astype(F32), dup.astype(F32), ddown.astype(F32))


def solution(mesh):
    return jax.shard_map(
        local,
        mesh=mesh,
        in_specs=(
            P("grp", None),
            P("grp", "shard"),
            P("grp", "shard"),
            P("shard", "grp"),
            P("grp", None),
        ),
        out_specs=(P("shard", "grp"), P("grp", "shard"), P("grp", "shard"), P("shard", "grp")),
        check_vma=False,
    )
```

```python
import functools

import jax
import jax.numpy as jnp
from jax import lax
from jax.experimental import pallas as pl
from jax.experimental.pallas import tpu as pltpu
from jax.sharding import PartitionSpec as P

MESH = pl.DeviceIdType.MESH
BF16 = jnp.bfloat16
F32 = jnp.float32

Q = 224
DH = 2048
B = 512
CHUNK = 512
PARTS = ((0, 128), (128, 96))


def dot_nt(left, right):
    return lax.dot_general(left, right, (((1,), (1,)), ((), ())), preferred_element_type=F32)


def dot_nn(left, right):
    return lax.dot_general(left, right, (((1,), (0,)), ((), ())), preferred_element_type=F32)


def dot_tn(left, right):
    return lax.dot_general(left, right, (((0,), (0,)), ((), ())), preferred_element_type=F32)


def kernel(
    tok, grd, gate_w, up_w, down_w, dgate, dup, ddown, dx,
    buf, raw, wt, wbuf, part, other, acc, back, dxs, dxr, zr, ys, xr, yr,
    ssem, rsem, lsem, zsem, lastsem,
):
    grp, shard = lax.axis_index("grp"), lax.axis_index("shard")
    x_lo, y = lax.div(grp, 4), lax.rem(grp, 4)
    x_hi, z, c = lax.div(shard, 8), lax.rem(lax.div(shard, 2), 4), lax.rem(shard, 2)
    x = 2 * x_hi + x_lo

    def mod4(v):
        return lax.rem(v + 8, 4)

    def slot(dy):
        return dy + lax.div(dy, 2) * (1 - 2 * lax.rem(dy, 2))

    def device(x, y, z, c):
        return (4 * lax.rem(x, 2) + y, 8 * lax.div(x, 2) + 2 * z + c)

    sibling = device(x, y, z, 1 - c)
    inner = device(x + 1 - 2 * x_lo, y, z, c)
    outer = device(mod4(x - 1 + 2 * x_lo), y, z, c)
    across = device(mod4(x + 2), y, z, c)
    along_y = {d: device(x, mod4(y + d), z, c) for d in (1, 2, 3)}
    along_z = {d: device(x, y, mod4(z + d), c) for d in (1, 2, 3)}

    barrier = pltpu.get_barrier_semaphore()
    partners = [sibling, inner, outer, across, *along_y.values(), *along_z.values()]
    for partner in partners:
        pl.semaphore_signal(barrier, inc=1, device_id=partner, device_id_type=MESH)
    pl.semaphore_wait(barrier, len(partners))

    count = [0]
    sent = []

    def push(src, dst, target, recv=None):
        n = count[0]
        count[0] += 1
        copy = pltpu.make_async_remote_copy(
            src_ref=src, dst_ref=dst, send_sem=ssem.at[n],
            recv_sem=rsem.at[n] if recv is None else recv,
            device_id=target, device_id_type=MESH,
        )
        copy.start()
        sent.append(copy)
        return copy

    local_count = [0]

    def bring(src, dst):
        n = local_count[0]
        local_count[0] += 1
        copy = pltpu.make_async_copy(src, dst, lsem.at[n])
        copy.start()
        return copy

    def arrived(*copies):
        for copy in copies:
            copy.wait_recv()

    gone = set()

    def left(*copies):
        for copy in copies:
            if id(copy) not in gone:
                gone.add(id(copy))
                copy.wait_send()

    def rows(start, size, step=32):
        return pl.ds(pl.multiple_of(start, step), size)

    def cols(block, size):
        return pl.ds(pl.multiple_of(block * size, size), size)

    mine, theirs = cols(x_lo, DH), cols(1 - x_lo, DH)
    own_rows, outer_rows = rows(32 * x_lo, 32), rows(32 * (1 - x_lo), 32)
    offs = (0, 1, 3, 2)
    quarter = [mod4(z + off) for off in offs]

    def send_outer(i):
        q = quarter[i]
        return [
            push(src.at[c, q, :, theirs], buf.at[a, q, c, own_rows, :], outer)
            for a, src in enumerate((tok, grd))
        ]

    from_outer = [send_outer(0)]
    own_tok = [
        bring(src.at[h, :, :, mine], buf.at[a, :, h, own_rows, :])
        for h in (0, 1)
        for a, src in enumerate((tok, grd))
    ]
    own_raw = [bring(gate_w, raw.at[0]), bring(up_w, raw.at[1]), bring(down_w, wt.at[2])]

    first, second = x_hi, 1 - x_hi

    def send_y(d, start):
        at = rows({1: 2, 3: 1, 2: 3}[d] * 64 + start, 32)
        return push(
            buf.at[first, z, c, rows(start, 32), :], buf.at[first, z, c, at, :], along_y[d]
        )

    for copy in own_tok:
        copy.wait()
    y_near = [send_y(1, 32 * x_lo), send_y(3, 32 * x_lo)]
    y_far = [send_y(2, 32 * x_lo)]
    for copy in own_raw:
        copy.wait()
    for m in (0, 1):
        def turn(n, carry):
            wt[m, cols(n, 128), :] = raw[m, :, cols(n, 128)].T
            return carry

        lax.fori_loop(0, 7, turn, 0)
    own_w = bring(wt.at[:, rows(Q * y, Q), :], wbuf.at[:, :, cols(y, B)])
    arrived(*from_outer[0])
    y_near += [send_y(1, 32 * (1 - x_lo)), send_y(3, 32 * (1 - x_lo))]
    y_far += [send_y(2, 32 * (1 - x_lo))]

    def send_w(h):
        start, size = PARTS[h]
        return [
            push(
                wt.at[:, rows(Q * mod4(y + d) + start, size, 16), :],
                wbuf.at[:, start : start + size, cols(y, B)],
                along_y[d],
            )
            for d in (1, 3, 2)
        ]

    from_w = [send_w(h) for h in range(len(PARTS))]

    def outer_to_sibling(i):
        ref = buf.at[:, quarter[i], c, outer_rows, :]
        return push(ref, ref, sibling)

    core_outer = [outer_to_sibling(0)]

    def near(a, q):
        return buf.at[a, q, c, 64:192, :]

    def far(a, q):
        return buf.at[a, q, c, 192:256, :]

    core_piece = {0: [], 1: [], 2: [], 3: []}

    def to_sibling(i, which, a):
        ref = which(a, quarter[i])
        core_piece[i].append(push(ref, ref, sibling))

    from_z = {}

    def spread(which, a, name):
        ref = which(a, z)
        from_z[name] = push(ref, ref, along_z[1]), push(ref, ref, along_z[3])
        to_sibling(0, which, a)

    arrived(*y_near)
    swap_near = push(near(first, z), near(first, z), across)
    spread(near, first, "near 0")
    arrived(*y_far)
    swap_far = push(far(first, z), far(first, z), across)
    spread(far, first, "far 0")
    from_outer += [send_outer(i) for i in (1, 2, 3)]
    arrived(swap_near)
    spread(near, second, "near 1")

    onward = []

    def relay(which, name):
        up, down = from_z[name]
        kind = 0 if name.endswith("0") else 1
        a = second if kind else first
        arrived(up)
        if kind == 0:
            ref = which(a, quarter[2])
            onward.append((push(ref, ref, along_z[1]), which, a))
        to_sibling(2, which, a)
        arrived(down)
        if kind == 1:
            ref = which(a, quarter[1])
            onward.append((push(ref, ref, along_z[3]), which, a))
        to_sibling(1, which, a)

    exchange = {}

    def forward(i, h):
        q = quarter[i]
        start, size = PARTS[h]
        hidden = slice(start, start + size)

        def half(g, carry):
            at = cols(g, 256)
            part[i, 0:2, hidden, at] = dot_nt(
                wbuf[0:2, hidden, :].reshape(2 * size, DH), buf[0, q, g]
            ).astype(BF16).reshape(2, size, 256)
            part[i, 2, hidden, at] = dot_nt(wbuf[2, hidden, :], buf[1, q, g]).astype(BF16)
            return carry

        lax.fori_loop(0, 2, half, 0)
        exchange[i, h] = push(part.at[i, :, hidden, :], other.at[i, :, hidden, :], inner)

    def activate(i, h):
        arrived(exchange[i, h])
        left(exchange[i, h])
        start, size = PARTS[h]

        def some(r, carry):
            at = rows(start + 16 * r, 16, 16)

            def full(m):
                return part[i, m, at, :].astype(F32) + other[i, m, at, :].astype(F32)

            gate, up_pre, back_grad = full(0), full(1), full(2)
            s = jax.nn.sigmoid(gate)
            silu = gate * s
            part[i, 0, at, :] = (back_grad * up_pre * s * (1.0 + gate * (1.0 - s))).astype(BF16)
            part[i, 1, at, :] = (back_grad * silu).astype(BF16)
            part[i, 2, at, :] = (silu * up_pre).astype(BF16)
            return carry

        lax.fori_loop(0, size // 16, some, 0)

    def weight_terms(i, h, n):
        q = quarter[i]
        start, size = PARTS[h]
        hidden = slice(start, start + size)
        at = cols(n, B)
        return (
            dot_nn(
                part[i, 0:2, hidden, :].reshape(2 * size, CHUNK),
                buf[0, q, :, :, at].reshape(CHUNK, B),
            ).reshape(2, size, B),
            dot_nn(part[i, 2, hidden, :], buf[1, q, :, :, at].reshape(CHUNK, B)),
        )

    def weight_grads(i, h):
        start, size = PARTS[h]
        hidden = slice(start, start + size)

        def block(n, carry):
            pair, third = weight_terms(i, h, n)
            at = cols(n, B)
            if i:
                pair = pair + acc[0:2, hidden, at]
                third = third + acc[2, hidden, at]
            acc[0:2, hidden, at] = pair
            acc[2, hidden, at] = third
            return carry

        lax.fori_loop(0, 4, block, 0)

    from_dw, own_dw = {}, []

    def last_weight_grads(i, h):
        if h == 0:
            for copies in from_w:
                for copy in copies:
                    left(copy)
        start, size = PARTS[h]
        hidden = slice(start, start + size)
        from_dw[h] = []
        for d in (1, 3, 2, 0):
            n = mod4(y + d)
            pair, third = weight_terms(i, h, n)
            at = cols(n, B)
            held = rows(Q * n + start, size, 16)
            wt[0:2, held, :] = (pair + acc[0:2, hidden, at]).astype(BF16)
            wt[2, held, :] = (third + acc[2, hidden, at]).astype(BF16)
            there = rows(Q * y + start, size, 16)
            if d:
                from_dw[h].append(push(wt.at[0:2, held, :], back.at[:, there, :], along_y[d]))
                from_dw[h].append(push(wt.at[2, held, :], ddown.at[there, :], along_y[d]))
            else:
                own_dw.append(bring(wt.at[0:2, held, :], back.at[:, there, :]))
                own_dw.append(bring(wt.at[2, held, :], ddown.at[there, :]))

    def token_terms(i, n, g):
        at = cols(n, B)
        return dot_tn(
            part[i, 0:2, :, 256 * g : 256 * g + 256].reshape(2 * Q, 256),
            wbuf[0:2, :, at].reshape(2 * Q, B),
        ).astype(BF16)

    core_dx = {}

    def token_grads(i):
        def block(n, carry):
            for g in (0, 1):
                dxs[i, g, :, cols(n, B)] = token_terms(i, n, g)
            return carry

        lax.fori_loop(0, 4, block, 0)
        core_dx[i] = push(dxs.at[i, 1 - c], dxr.at[i], sibling)

    def z_rows(d):
        return rows(64 * slot(mod4(z + d - y)), 64)

    def along_z_grads(i):
        arrived(core_dx[i])

        def some(r, carry):
            at = rows(32 * r, 32)
            dxs[i, c, at, :] = (
                dxs[i, c, at, :].astype(F32) + dxr[i, at, :].astype(F32)
            ).astype(BF16)
            return carry

        lax.fori_loop(0, 8, some, 0)
        for d in (1, 3, 2):
            push(
                dxs.at[i, c, z_rows(d), :], zr.at[quarter[i], d - 1], along_z[d],
                zsem.at[quarter[i], d - 1],
            )

    def last_token_grads(i):
        core_last = {}
        for d in (1, 3, 2, 0):
            n = mod4(y + d)
            for g in (0, 1):
                dxs[i, g, :, cols(n, B)] = token_terms(i, n, g)
            core_last[d] = push(
                dxs.at[i, 1 - c, :, cols(n, B)], dxr.at[i, :, cols(n, B)], sibling
            )
        return core_last

    def last_along_z(i, core_last):
        for k, d in enumerate((1, 3, 2, 0)):
            at = cols(mod4(y + d), B)
            arrived(core_last[d])
            dxs[i, c, :, at] = (
                dxs[i, c, :, at].astype(F32) + dxr[i, :, at].astype(F32)
            ).astype(BF16)
            for e in (1, 3, 2):
                push(
                    dxs.at[i, c, z_rows(e), at], zr.at[quarter[i], e - 1, :, at], along_z[e],
                    lastsem.at[k, e - 1],
                )

    arrived(swap_far)
    spread(far, second, "far 1")
    relay(near, "near 0")
    relay(far, "far 0")
    arrived(*core_outer, *core_piece[0])
    own_w.wait()
    arrived(*from_w[0])
    forward(0, 0)
    for i in (1, 2, 3):
        arrived(*from_outer[i])
        core_outer.append(outer_to_sibling(i))
    relay(near, "near 1")
    activate(0, 0)
    weight_grads(0, 0)
    arrived(*from_w[1])
    forward(0, 1)
    relay(far, "far 1")
    arrived(*core_outer[1:], *core_piece[1])
    forward(1, 0)
    forward(1, 1)
    arrived(*core_piece[2])
    forward(2, 0)
    activate(0, 1)
    token_grads(0)
    weight_grads(0, 1)
    along_z_grads(0)
    activate(1, 0)
    weight_grads(1, 0)
    for copy, which, a in onward:
        arrived(copy)
        to_sibling(3, which, a)
    activate(1, 1)
    token_grads(1)
    arrived(*core_piece[3])
    forward(3, 0)
    forward(2, 1)
    forward(3, 1)
    along_z_grads(1)
    weight_grads(1, 1)
    activate(2, 0)
    weight_grads(2, 0)
    activate(3, 0)
    last_weight_grads(3, 0)
    activate(2, 1)
    token_grads(2)
    weight_grads(2, 1)
    along_z_grads(2)
    activate(3, 1)
    core_last = last_token_grads(3)
    last_weight_grads(3, 1)
    last_along_z(3, core_last)

    def landed(ref, sem):
        pltpu.make_async_remote_copy(
            src_ref=ref, dst_ref=ref, send_sem=ssem.at[0], recv_sem=sem,
            device_id=along_z[1], device_id_type=MESH,
        ).wait_recv()

    for d in (1, 2, 3):
        for off in (0, 1, 3):
            q = mod4(z - d + off)
            landed(zr.at[q, d - 1], zsem.at[q, d - 1])
    keep = z_rows(0)
    from_x, from_yg = [], {}

    def over_x(k, d):
        at = cols(mod4(y + d), B)
        for e in (1, 2, 3):
            landed(zr.at[mod4(z - e + 2), e - 1, :, at], lastsem.at[k, e - 1])

        for i in range(4):
            q = quarter[i]
            total = dxs[i, c, keep, at].astype(F32)
            for e in (0, 1, 2):
                total = total + zr[q, e, :, at].astype(F32)
            total = total.astype(BF16)
            ys[0, q, :, at] = total[0:32]
            ys[1, q, :, at] = total[32:64]
        from_x.append(push(ys.at[1 - x_hi, :, :, at], xr.at[:, :, at], across))

    def over_y(k, d):
        at = cols(mod4(y + d), B)
        arrived(from_x[k])
        ys[x_hi, :, :, at] = (
            ys[x_hi, :, :, at].astype(F32) + xr[:, :, at].astype(F32)
        ).astype(BF16)
        if d:
            from_yg[d] = push(ys.at[x_hi, :, :, at], yr.at[d - 1], along_y[d])

    order = (1, 3, 2, 0)
    over_x(0, order[0])
    for k in (1, 2, 3):
        over_x(k, order[k])
        over_y(k - 1, order[k - 1])
    over_y(3, order[3])
    for copy in own_dw:
        copy.wait()
    arrived(*from_dw[0], *from_dw[1])
    for m, out in enumerate((dgate, dup)):
        def turn(n, carry):
            out[:, cols(n, 128)] = back[m, cols(n, 128), :].T
            return carry

        lax.fori_loop(0, 7, turn, 0)
    total = ys[x_hi, :, :, cols(y, B)].astype(F32)
    for d in (1, 3, 2):
        arrived(from_yg[d])
        total = total + yr[d - 1].astype(F32)
    dx[...] = total.astype(BF16).reshape(128, B)
    left(*sent)


def local(tokens, gate_weight, up_weight, down_weight, grad_out):
    flops = 8 * 2 * 2048 * 2048 * 256
    dgate, dup, ddown, dx = pl.pallas_call(
        kernel,
        out_shape=(
            jax.ShapeDtypeStruct((B, 4 * Q), BF16),
            jax.ShapeDtypeStruct((B, 4 * Q), BF16),
            jax.ShapeDtypeStruct((4 * Q, B), BF16),
            jax.ShapeDtypeStruct((128, B), BF16),
        ),
        in_specs=[pl.BlockSpec(memory_space=pl.ANY)] * 5,
        out_specs=(
            pl.BlockSpec(memory_space=pltpu.VMEM),
            pl.BlockSpec(memory_space=pltpu.VMEM),
            pl.BlockSpec(memory_space=pl.ANY),
            pl.BlockSpec(memory_space=pltpu.VMEM),
        ),
        scratch_shapes=[
            pltpu.VMEM((2, 4, 2, 256, DH), BF16),
            pltpu.VMEM((2, B, 4 * Q), BF16),
            pltpu.VMEM((3, 4 * Q, B), BF16),
            pltpu.VMEM((3, Q, DH), BF16),
            pltpu.VMEM((4, 3, Q, CHUNK), BF16),
            pltpu.VMEM((4, 3, Q, CHUNK), BF16),
            pltpu.VMEM((3, Q, DH), F32),
            pltpu.VMEM((2, 4 * Q, B), BF16),
            pltpu.VMEM((4, 2, 256, DH), BF16),
            pltpu.VMEM((4, 256, DH), BF16),
            pltpu.VMEM((4, 3, 64, DH), BF16),
            pltpu.VMEM((2, 4, 32, DH), BF16),
            pltpu.VMEM((4, 32, DH), BF16),
            pltpu.VMEM((3, 4, 32, B), BF16),
            pltpu.SemaphoreType.DMA((128,)),
            pltpu.SemaphoreType.DMA((128,)),
            pltpu.SemaphoreType.DMA((16,)),
            pltpu.SemaphoreType.DMA((4, 3)),
            pltpu.SemaphoreType.DMA((4, 3)),
        ],
        compiler_params=pltpu.CompilerParams(
            collective_id=0, has_side_effects=True, vmem_limit_bytes=62 * 2**20
        ),
        cost_estimate=pl.CostEstimate(flops=flops, bytes_accessed=2**24, transcendentals=2**20),
    )(
        tokens.reshape(2, 4, 32, 4096), grad_out.reshape(2, 4, 32, 4096),
        gate_weight, up_weight, down_weight,
    )
    return (dx, dgate.astype(F32), dup.astype(F32), ddown.astype(F32))


def solution(mesh):
    return jax.shard_map(
        local,
        mesh=mesh,
        in_specs=(
            P("grp", None),
            P("grp", "shard"),
            P("grp", "shard"),
            P("shard", "grp"),
            P("grp", None),
        ),
        out_specs=(P("shard", "grp"), P("grp", "shard"), P("grp", "shard"), P("shard", "grp")),
        check_vma=False,
    )
```

```python
import functools

import jax
import jax.numpy as jnp
from jax import lax
from jax.experimental import pallas as pl
from jax.experimental.pallas import tpu as pltpu
from jax.sharding import PartitionSpec as P

MESH = pl.DeviceIdType.MESH
BF16 = jnp.bfloat16
F32 = jnp.float32

Q = 224
DH = 2048
B = 512
CHUNK = 512
PARTS = ((0, 80), (80, 80), (160, 64))


def dot_nt(left, right):
    return lax.dot_general(left, right, (((1,), (1,)), ((), ())), preferred_element_type=F32)


def dot_nn(left, right):
    return lax.dot_general(left, right, (((1,), (0,)), ((), ())), preferred_element_type=F32)


def dot_tn(left, right):
    return lax.dot_general(left, right, (((0,), (0,)), ((), ())), preferred_element_type=F32)


def kernel(
    tok, grd, gate_w, up_w, down_w, back, ddown, dx,
    buf, raw, wt, wbuf, part, other, acc, dxs, dxr, zr, ys, xr, yr,
    ssem, rsem, lsem, zsem, lastsem,
):
    grp, shard = lax.axis_index("grp"), lax.axis_index("shard")
    x_lo, y = lax.div(grp, 4), lax.rem(grp, 4)
    x_hi, z, c = lax.div(shard, 8), lax.rem(lax.div(shard, 2), 4), lax.rem(shard, 2)
    x = 2 * x_hi + x_lo

    def mod4(v):
        return lax.rem(v + 8, 4)

    def slot(dy):
        return dy + lax.div(dy, 2) * (1 - 2 * lax.rem(dy, 2))

    def device(x, y, z, c):
        return (4 * lax.rem(x, 2) + y, 8 * lax.div(x, 2) + 2 * z + c)

    sibling = device(x, y, z, 1 - c)
    inner = device(x + 1 - 2 * x_lo, y, z, c)
    outer = device(mod4(x - 1 + 2 * x_lo), y, z, c)
    across = device(mod4(x + 2), y, z, c)
    along_y = {d: device(x, mod4(y + d), z, c) for d in (1, 2, 3)}
    along_z = {d: device(x, y, mod4(z + d), c) for d in (1, 2, 3)}

    barrier = pltpu.get_barrier_semaphore()
    partners = [sibling, inner, outer, across, *along_y.values(), *along_z.values()]
    for partner in partners:
        pl.semaphore_signal(barrier, inc=1, device_id=partner, device_id_type=MESH)
    pl.semaphore_wait(barrier, len(partners))

    count = [0]
    sent = []

    def push(src, dst, target, recv=None):
        n = count[0]
        count[0] += 1
        copy = pltpu.make_async_remote_copy(
            src_ref=src, dst_ref=dst, send_sem=ssem.at[n],
            recv_sem=rsem.at[n] if recv is None else recv,
            device_id=target, device_id_type=MESH,
        )
        copy.start()
        sent.append(copy)
        return copy

    local_count = [0]

    def bring(src, dst):
        n = local_count[0]
        local_count[0] += 1
        copy = pltpu.make_async_copy(src, dst, lsem.at[n])
        copy.start()
        return copy

    def arrived(*copies):
        for copy in copies:
            copy.wait_recv()

    gone = set()

    def left(*copies):
        for copy in copies:
            if id(copy) not in gone:
                gone.add(id(copy))
                copy.wait_send()

    def rows(start, size, step=32):
        return pl.ds(pl.multiple_of(start, step), size)

    def cols(block, size):
        return pl.ds(pl.multiple_of(block * size, size), size)

    mine, theirs = cols(x_lo, DH), cols(1 - x_lo, DH)
    own_rows, outer_rows = rows(32 * x_lo, 32), rows(32 * (1 - x_lo), 32)
    offs = (0, 1, 3, 2)
    quarter = [mod4(z + off) for off in offs]

    def send_outer(i):
        q = quarter[i]
        return [
            push(src.at[c, q, :, theirs], buf.at[a, q, c, own_rows, :], outer)
            for a, src in enumerate((tok, grd))
        ]

    from_outer = [send_outer(0)]
    own_tok = [
        bring(src.at[h, :, :, mine], buf.at[a, :, h, own_rows, :])
        for h in (0, 1)
        for a, src in enumerate((tok, grd))
    ]
    own_raw = [bring(gate_w, raw.at[0]), bring(up_w, raw.at[1]), bring(down_w, wt.at[2])]

    first, second = x_hi, 1 - x_hi

    def send_y(d, start):
        at = rows({1: 2, 3: 1, 2: 3}[d] * 64 + start, 32)
        return push(
            buf.at[first, z, c, rows(start, 32), :], buf.at[first, z, c, at, :], along_y[d]
        )

    for copy in own_tok:
        copy.wait()
    y_near = [send_y(1, 32 * x_lo), send_y(3, 32 * x_lo)]
    y_far = [send_y(2, 32 * x_lo)]
    for copy in own_raw:
        copy.wait()
    for m in (0, 1):
        def turn(n, carry):
            wt[m, cols(n, 128), :] = raw[m, :, cols(n, 128)].T
            return carry

        lax.fori_loop(0, 7, turn, 0)
    own_w = bring(wt.at[:, rows(Q * y, Q), :], wbuf.at[:, :, cols(y, B)])
    arrived(*from_outer[0])
    y_near += [send_y(1, 32 * (1 - x_lo)), send_y(3, 32 * (1 - x_lo))]
    y_far += [send_y(2, 32 * (1 - x_lo))]

    def send_w(h):
        start, size = PARTS[h]
        return [
            push(
                wt.at[:, rows(Q * mod4(y + d) + start, size, 16), :],
                wbuf.at[:, start : start + size, cols(y, B)],
                along_y[d],
            )
            for d in (1, 3, 2)
        ]

    from_w = [send_w(h) for h in range(len(PARTS))]

    def outer_to_sibling(i):
        ref = buf.at[:, quarter[i], c, outer_rows, :]
        return push(ref, ref, sibling)

    core_outer = [outer_to_sibling(0)]

    def near(a, q):
        return buf.at[a, q, c, 64:192, :]

    def far(a, q):
        return buf.at[a, q, c, 192:256, :]

    core_piece = {0: [], 1: [], 2: [], 3: []}

    def to_sibling(i, which, a):
        ref = which(a, quarter[i])
        core_piece[i].append(push(ref, ref, sibling))

    from_z = {}

    def spread(which, a, name):
        ref = which(a, z)
        from_z[name] = push(ref, ref, along_z[1]), push(ref, ref, along_z[3])
        to_sibling(0, which, a)

    arrived(*y_near)
    swap_near = push(near(first, z), near(first, z), across)
    spread(near, first, "near 0")
    arrived(*y_far)
    swap_far = push(far(first, z), far(first, z), across)
    spread(far, first, "far 0")
    from_outer += [send_outer(i) for i in (1, 2, 3)]
    arrived(swap_near)
    spread(near, second, "near 1")

    onward = []

    def relay(which, name):
        up, down = from_z[name]
        kind = 0 if name.endswith("0") else 1
        a = second if kind else first
        arrived(up)
        if kind == 0:
            ref = which(a, quarter[2])
            onward.append((push(ref, ref, along_z[1]), which, a))
        to_sibling(2, which, a)
        arrived(down)
        if kind == 1:
            ref = which(a, quarter[1])
            onward.append((push(ref, ref, along_z[3]), which, a))
        to_sibling(1, which, a)

    exchange = {}

    def forward(i, h):
        q = quarter[i]
        start, size = PARTS[h]
        hidden = slice(start, start + size)

        def half(g, carry):
            at = cols(g, 256)
            part[i, 0:2, hidden, at] = dot_nt(
                wbuf[0:2, hidden, :].reshape(2 * size, DH), buf[0, q, g]
            ).astype(BF16).reshape(2, size, 256)
            part[i, 2, hidden, at] = dot_nt(wbuf[2, hidden, :], buf[1, q, g]).astype(BF16)
            return carry

        lax.fori_loop(0, 2, half, 0)
        exchange[i, h] = push(part.at[i, :, hidden, :], other.at[i, :, hidden, :], inner)

    def activate(i, h):
        arrived(exchange[i, h])
        left(exchange[i, h])
        start, size = PARTS[h]

        def some(r, carry):
            at = rows(start + 16 * r, 16, 16)

            def full(m):
                return part[i, m, at, :].astype(F32) + other[i, m, at, :].astype(F32)

            gate, up_pre, back_grad = full(0), full(1), full(2)
            s = jax.nn.sigmoid(gate)
            silu = gate * s
            part[i, 0, at, :] = (back_grad * up_pre * s * (1.0 + gate * (1.0 - s))).astype(BF16)
            part[i, 1, at, :] = (back_grad * silu).astype(BF16)
            part[i, 2, at, :] = (silu * up_pre).astype(BF16)
            return carry

        lax.fori_loop(0, size // 16, some, 0)

    def weight_terms(i, h, n):
        q = quarter[i]
        start, size = PARTS[h]
        hidden = slice(start, start + size)
        at = cols(n, B)
        return (
            dot_nn(
                part[i, 0:2, hidden, :].reshape(2 * size, CHUNK),
                buf[0, q, :, :, at].reshape(CHUNK, B),
            ).reshape(2, size, B),
            dot_nn(part[i, 2, hidden, :], buf[1, q, :, :, at].reshape(CHUNK, B)),
        )

    def weight_grads(i, h):
        start, size = PARTS[h]
        hidden = slice(start, start + size)

        def block(n, carry):
            pair, third = weight_terms(i, h, n)
            at = cols(n, B)
            if i:
                pair = pair + acc[0:2, hidden, at]
                third = third + acc[2, hidden, at]
            acc[0:2, hidden, at] = pair
            acc[2, hidden, at] = third
            return carry

        lax.fori_loop(0, 4, block, 0)

    from_dw, own_dw = {}, []

    def last_weight_grads(i, h):
        if h == 0:
            for copies in from_w:
                for copy in copies:
                    left(copy)
        start, size = PARTS[h]
        hidden = slice(start, start + size)
        from_dw[h] = []
        for d in (1, 3, 2, 0):
            n = mod4(y + d)
            pair, third = weight_terms(i, h, n)
            at = cols(n, B)
            held = rows(Q * n + start, size, 16)
            wt[0:2, held, :] = (pair + acc[0:2, hidden, at]).astype(BF16)
            wt[2, held, :] = (third + acc[2, hidden, at]).astype(BF16)
            there = rows(Q * y + start, size, 16)
            if d:
                from_dw[h].append(push(wt.at[0:2, held, :], back.at[:, there, :], along_y[d]))
                from_dw[h].append(push(wt.at[2, held, :], ddown.at[there, :], along_y[d]))
            else:
                own_dw.append(bring(wt.at[0:2, held, :], back.at[:, there, :]))
                own_dw.append(bring(wt.at[2, held, :], ddown.at[there, :]))

    def token_terms(i, n, g):
        at = cols(n, B)
        return dot_tn(
            part[i, 0:2, :, 256 * g : 256 * g + 256].reshape(2 * Q, 256),
            wbuf[0:2, :, at].reshape(2 * Q, B),
        ).astype(BF16)

    core_dx = {}

    def token_grads(i):
        def block(n, carry):
            for g in (0, 1):
                dxs[i, g, :, cols(n, B)] = token_terms(i, n, g)
            return carry

        lax.fori_loop(0, 4, block, 0)
        core_dx[i] = push(dxs.at[i, 1 - c], dxr.at[i], sibling)

    def z_rows(d):
        return rows(64 * slot(mod4(z + d - y)), 64)

    def along_z_grads(i):
        arrived(core_dx[i])

        def some(r, carry):
            at = rows(32 * r, 32)
            dxs[i, c, at, :] = (
                dxs[i, c, at, :].astype(F32) + dxr[i, at, :].astype(F32)
            ).astype(BF16)
            return carry

        lax.fori_loop(0, 8, some, 0)
        for d in (1, 3, 2):
            push(
                dxs.at[i, c, z_rows(d), :], zr.at[quarter[i], d - 1], along_z[d],
                zsem.at[quarter[i], d - 1],
            )

    def last_token_grads(i):
        core_last = {}
        for d in (1, 3, 2, 0):
            n = mod4(y + d)
            for g in (0, 1):
                dxs[i, g, :, cols(n, B)] = token_terms(i, n, g)
            core_last[d] = push(
                dxs.at[i, 1 - c, :, cols(n, B)], dxr.at[i, :, cols(n, B)], sibling
            )
        return core_last

    def last_along_z(i, core_last):
        for k, d in enumerate((1, 3, 2, 0)):
            at = cols(mod4(y + d), B)
            arrived(core_last[d])
            dxs[i, c, :, at] = (
                dxs[i, c, :, at].astype(F32) + dxr[i, :, at].astype(F32)
            ).astype(BF16)
            for e in (1, 3, 2):
                push(
                    dxs.at[i, c, z_rows(e), at], zr.at[quarter[i], e - 1, :, at], along_z[e],
                    lastsem.at[k, e - 1],
                )

    arrived(swap_far)
    spread(far, second, "far 1")
    relay(near, "near 0")
    arrived(*core_outer, *core_piece[0])
    own_w.wait()
    arrived(*from_w[0])
    forward(0, 0)
    relay(far, "far 0")
    arrived(*from_w[1])
    forward(0, 1)
    for i in (1, 2, 3):
        arrived(*from_outer[i])
        core_outer.append(outer_to_sibling(i))
    activate(0, 0)
    weight_grads(0, 0)
    relay(near, "near 1")
    activate(0, 1)
    weight_grads(0, 1)
    arrived(*from_w[2])
    forward(0, 2)
    relay(far, "far 1")
    arrived(*core_outer[1:], *core_piece[1])
    forward(1, 0)
    forward(1, 1)
    forward(1, 2)
    activate(0, 2)
    token_grads(0)
    arrived(*core_piece[2])
    forward(2, 0)
    forward(2, 1)
    weight_grads(0, 2)
    along_z_grads(0)
    activate(1, 0)
    weight_grads(1, 0)
    activate(1, 1)
    weight_grads(1, 1)
    for copy, which, a in onward:
        arrived(copy)
        to_sibling(3, which, a)
    activate(1, 2)
    token_grads(1)
    arrived(*core_piece[3])
    forward(3, 0)
    forward(2, 2)
    along_z_grads(1)
    weight_grads(1, 2)
    forward(3, 1)
    forward(3, 2)
    activate(2, 0)
    weight_grads(2, 0)
    activate(2, 1)
    weight_grads(2, 1)
    activate(3, 0)
    last_weight_grads(3, 0)
    activate(2, 2)
    token_grads(2)
    weight_grads(2, 2)
    along_z_grads(2)
    activate(3, 1)
    last_weight_grads(3, 1)
    activate(3, 2)
    core_last = last_token_grads(3)
    last_weight_grads(3, 2)
    last_along_z(3, core_last)

    def landed(ref, sem):
        pltpu.make_async_remote_copy(
            src_ref=ref, dst_ref=ref, send_sem=ssem.at[0], recv_sem=sem,
            device_id=along_z[1], device_id_type=MESH,
        ).wait_recv()

    for d in (1, 2, 3):
        for off in (0, 1, 3):
            q = mod4(z - d + off)
            landed(zr.at[q, d - 1], zsem.at[q, d - 1])
    keep = z_rows(0)
    from_x, from_yg = [], {}

    def over_x(k, d):
        at = cols(mod4(y + d), B)
        for e in (1, 2, 3):
            landed(zr.at[mod4(z - e + 2), e - 1, :, at], lastsem.at[k, e - 1])

        for i in range(4):
            q = quarter[i]
            total = dxs[i, c, keep, at].astype(F32)
            for e in (0, 1, 2):
                total = total + zr[q, e, :, at].astype(F32)
            total = total.astype(BF16)
            ys[0, q, :, at] = total[0:32]
            ys[1, q, :, at] = total[32:64]
        from_x.append(push(ys.at[1 - x_hi, :, :, at], xr.at[:, :, at], across))

    def over_y(k, d):
        at = cols(mod4(y + d), B)
        arrived(from_x[k])
        ys[x_hi, :, :, at] = (
            ys[x_hi, :, :, at].astype(F32) + xr[:, :, at].astype(F32)
        ).astype(BF16)
        if d:
            from_yg[d] = push(ys.at[x_hi, :, :, at], yr.at[d - 1], along_y[d])

    order = (1, 3, 2, 0)
    over_x(0, order[0])
    for k in (1, 2, 3):
        over_x(k, order[k])
        over_y(k - 1, order[k - 1])
    over_y(3, order[3])
    for copy in own_dw:
        copy.wait()
    for h in range(len(PARTS)):
        arrived(*from_dw[h])
    total = ys[x_hi, :, :, cols(y, B)].astype(F32)
    for d in (1, 3, 2):
        arrived(from_yg[d])
        total = total + yr[d - 1].astype(F32)
    dx[...] = total.astype(BF16).reshape(128, B)
    left(*sent)


def finish(back, down, dgate, dup, ddown):
    dgate[...] = back[0].T.astype(F32)
    dup[...] = back[1].T.astype(F32)
    ddown[...] = down[...].astype(F32)


def local(tokens, gate_weight, up_weight, down_weight, grad_out):
    flops = 8 * 2 * 2048 * 2048 * 256
    back, ddown, dx = pl.pallas_call(
        kernel,
        out_shape=(
            jax.ShapeDtypeStruct((2, 4 * Q, B), BF16),
            jax.ShapeDtypeStruct((4 * Q, B), BF16),
            jax.ShapeDtypeStruct((128, B), BF16),
        ),
        in_specs=[pl.BlockSpec(memory_space=pl.ANY)] * 5,
        out_specs=(
            pl.BlockSpec(memory_space=pl.ANY),
            pl.BlockSpec(memory_space=pl.ANY),
            pl.BlockSpec(memory_space=pltpu.VMEM),
        ),
        scratch_shapes=[
            pltpu.VMEM((2, 4, 2, 256, DH), BF16),
            pltpu.VMEM((2, B, 4 * Q), BF16),
            pltpu.VMEM((3, 4 * Q, B), BF16),
            pltpu.VMEM((3, Q, DH), BF16),
            pltpu.VMEM((4, 3, Q, CHUNK), BF16),
            pltpu.VMEM((4, 3, Q, CHUNK), BF16),
            pltpu.VMEM((3, Q, DH), F32),
            pltpu.VMEM((4, 2, 256, DH), BF16),
            pltpu.VMEM((4, 256, DH), BF16),
            pltpu.VMEM((4, 3, 64, DH), BF16),
            pltpu.VMEM((2, 4, 32, DH), BF16),
            pltpu.VMEM((4, 32, DH), BF16),
            pltpu.VMEM((3, 4, 32, B), BF16),
            pltpu.SemaphoreType.DMA((128,)),
            pltpu.SemaphoreType.DMA((128,)),
            pltpu.SemaphoreType.DMA((16,)),
            pltpu.SemaphoreType.DMA((4, 3)),
            pltpu.SemaphoreType.DMA((4, 3)),
        ],
        compiler_params=pltpu.CompilerParams(
            collective_id=0, has_side_effects=True, vmem_limit_bytes=62 * 2**20
        ),
        cost_estimate=pl.CostEstimate(flops=flops, bytes_accessed=2**24, transcendentals=2**20),
    )(
        tokens.reshape(2, 4, 32, 4096), grad_out.reshape(2, 4, 32, 4096),
        gate_weight, up_weight, down_weight,
    )
    grads = pl.pallas_call(
        finish,
        grid=(7,),
        out_shape=(
            jax.ShapeDtypeStruct((B, 4 * Q), F32),
            jax.ShapeDtypeStruct((B, 4 * Q), F32),
            jax.ShapeDtypeStruct((4 * Q, B), F32),
        ),
        in_specs=[
            pl.BlockSpec((2, 128, B), lambda n: (0, n, 0)),
            pl.BlockSpec((128, B), lambda n: (n, 0)),
        ],
        out_specs=(
            pl.BlockSpec((B, 128), lambda n: (0, n)),
            pl.BlockSpec((B, 128), lambda n: (0, n)),
            pl.BlockSpec((128, B), lambda n: (n, 0)),
        ),
        cost_estimate=pl.CostEstimate(flops=0, bytes_accessed=2**23, transcendentals=0),
    )(back, ddown)
    return (dx, *grads)


def solution(mesh):
    return jax.shard_map(
        local,
        mesh=mesh,
        in_specs=(
            P("grp", None),
            P("grp", "shard"),
            P("grp", "shard"),
            P("shard", "grp"),
            P("grp", None),
        ),
        out_specs=(P("shard", "grp"), P("grp", "shard"), P("grp", "shard"), P("shard", "grp")),
        check_vma=False,
    )
```

```python
import functools

import jax
import jax.numpy as jnp
from jax import lax
from jax.experimental import pallas as pl
from jax.experimental.pallas import tpu as pltpu
from jax.sharding import PartitionSpec as P

MESH = pl.DeviceIdType.MESH
BF16 = jnp.bfloat16
F32 = jnp.float32

Q = 224
DH = 2048
B = 512
CHUNK = 512
H0, H1, H2 = PARTS = ((0, 80), (80, 80), (160, 64))
H01, H12, ALL = (0, 160), (80, 144), (0, Q)


def dot_nt(left, right):
    return lax.dot_general(left, right, (((1,), (1,)), ((), ())), preferred_element_type=F32)


def dot_nn(left, right):
    return lax.dot_general(left, right, (((1,), (0,)), ((), ())), preferred_element_type=F32)


def dot_tn(left, right):
    return lax.dot_general(left, right, (((0,), (0,)), ((), ())), preferred_element_type=F32)


def kernel(
    tok, grd, gate_w, up_w, down_w, back, ddown, dx,
    buf, raw, wt, wbuf, part, other, acc, dxs, dxr, zr, ys, xr, yr, yf, zs, zy,
    ssem, rsem, lsem, zsem, lastsem,
):
    grp, shard = lax.axis_index("grp"), lax.axis_index("shard")
    x_lo, y = lax.div(grp, 4), lax.rem(grp, 4)
    x_hi, z, c = lax.div(shard, 8), lax.rem(lax.div(shard, 2), 4), lax.rem(shard, 2)
    x = 2 * x_hi + x_lo

    def mod4(v):
        return lax.rem(v + 8, 4)

    def slot(dy):
        return dy + lax.div(dy, 2) * (1 - 2 * lax.rem(dy, 2))

    def device(x, y, z, c):
        return (4 * lax.rem(x, 2) + y, 8 * lax.div(x, 2) + 2 * z + c)

    sibling = device(x, y, z, 1 - c)
    inner = device(x + 1 - 2 * x_lo, y, z, c)
    outer = device(mod4(x - 1 + 2 * x_lo), y, z, c)
    across = device(mod4(x + 2), y, z, c)
    along_y = {d: device(x, mod4(y + d), z, c) for d in (1, 2, 3)}
    along_z = {d: device(x, y, mod4(z + d), c) for d in (1, 2, 3)}

    barrier = pltpu.get_barrier_semaphore()
    partners = [sibling, inner, outer, across, *along_y.values(), *along_z.values()]
    for partner in partners:
        pl.semaphore_signal(barrier, inc=1, device_id=partner, device_id_type=MESH)

    count = [0]
    sent = []

    def push(src, dst, target, recv=None):
        n = count[0]
        count[0] += 1
        copy = pltpu.make_async_remote_copy(
            src_ref=src, dst_ref=dst, send_sem=ssem.at[n],
            recv_sem=rsem.at[n] if recv is None else recv,
            device_id=target, device_id_type=MESH,
        )
        copy.start()
        sent.append(copy)
        return copy

    local_count = [0]

    def bring(src, dst):
        n = local_count[0]
        local_count[0] += 1
        copy = pltpu.make_async_copy(src, dst, lsem.at[n])
        copy.start()
        return copy

    def arrived(*copies):
        for copy in copies:
            copy.wait_recv()

    gone = set()

    def left(*copies):
        for copy in copies:
            if id(copy) not in gone:
                gone.add(id(copy))
                copy.wait_send()

    def rows(start, size, step=32):
        return pl.ds(pl.multiple_of(start, step), size)

    def cols(block, size):
        return pl.ds(pl.multiple_of(block * size, size), size)

    mine, theirs = cols(x_lo, DH), cols(1 - x_lo, DH)
    own_rows, outer_rows = rows(16 * x_lo, 16, 16), rows(16 * (1 - x_lo), 16, 16)
    offs = (0, 1, 3, 2)
    quarter = [mod4(z + off) for off in offs]
    first, second = x_hi, 1 - x_hi

    def half(u):
        return first + u * (1 - 2 * first)

    own_tok = [
        bring(src.at[h, :, s, :, mine], buf.at[a, :, s, h, own_rows, :])
        for s in (0, 1)
        for h in (0, 1)
        for a, src in enumerate((tok, grd))
    ]
    own_raw = [bring(gate_w, raw.at[0]), bring(up_w, raw.at[1]), bring(down_w, wt.at[2])]
    for copy in own_raw:
        copy.wait()
    for m in (0, 1):
        def turn(n, carry):
            wt[m, cols(n, 128), :] = raw[m, :, cols(n, 128)].T
            return carry

        lax.fori_loop(0, 7, turn, 0)
    own_w = bring(wt.at[:, rows(Q * y, Q), :], wbuf.at[:, :, cols(y, B)])
    for copy in own_tok:
        copy.wait()
    pl.semaphore_wait(barrier, len(partners))

    def send_outer(i, target):
        q = quarter[i]
        return [
            push(src.at[c, q, :, :, theirs], buf.at[a, q, :, c, own_rows, :], target)
            for a, src in enumerate((tok, grd))
        ]

    from_outer = {0: send_outer(0, outer), 2: send_outer(2, inner), 1: send_outer(1, outer)}

    def send_y(d, lo):
        src = rows(16 * lo, 16, 16)
        dst = rows({1: 2, 3: 1, 2: 3}[d] * 32 + 16 * lo, 16, 16)
        return push(buf.at[:, z, first, c, src, :], buf.at[:, z, first, c, dst, :], along_y[d])

    y_near = [send_y(1, x_lo), send_y(3, x_lo)]
    y_far = [send_y(2, x_lo)]
    arrived(*from_outer[0])
    y_near += [send_y(1, 1 - x_lo), send_y(3, 1 - x_lo)]
    y_far += [send_y(2, 1 - x_lo)]

    def send_w(h):
        start, size = PARTS[h]
        return [
            push(
                wt.at[:, rows(Q * mod4(y + d) + start, size, 16), :],
                wbuf.at[:, start : start + size, cols(y, B)],
                along_y[d],
            )
            for d in (1, 3, 2)
        ]

    from_w = [send_w(h) for h in range(len(PARTS))]

    def outer_to_sibling(i):
        ref = buf.at[:, quarter[i], :, c, outer_rows, :]
        return push(ref, ref, sibling)

    core_outer = [outer_to_sibling(0)]

    def near(s, q):
        return buf.at[:, q, s, c, 32:96, :]

    def far(s, q):
        return buf.at[:, q, s, c, 96:128, :]

    core_piece = {(i, u): [] for i in range(4) for u in (0, 1)}

    def to_sibling(i, u, which):
        ref = which(half(u), quarter[i])
        core_piece[i, u].append(push(ref, ref, sibling))

    from_z = {}

    def spread(which, u):
        ref = which(half(u), z)
        from_z[which, u] = push(ref, ref, along_z[1]), push(ref, ref, along_z[3])
        to_sibling(0, u, which)

    arrived(*y_near)
    swap_near = push(near(first, z), near(first, z), across)
    spread(near, 0)
    arrived(*y_far)
    swap_far = push(far(first, z), far(first, z), across)
    spread(far, 0)
    from_outer[3] = send_outer(3, outer)
    arrived(swap_near)
    spread(near, 1)

    onward = []

    def relay(which, u):
        up, down = from_z[which, u]
        arrived(up)
        if u == 0:
            ref = which(half(u), quarter[2])
            onward.append((push(ref, ref, along_z[1]), which, u))
        to_sibling(2, u, which)
        arrived(down)
        if u == 1:
            ref = which(half(u), quarter[1])
            onward.append((push(ref, ref, along_z[3]), which, u))
        to_sibling(1, u, which)

    exchange = {}

    def forward(i, us, span):
        q = quarter[i]
        start, size = span
        hidden = slice(start, start + size)

        def one(u, carry):
            s = half(u)
            part[i, u, 0:2, hidden, :] = dot_nt(
                wbuf[0:2, hidden, :].reshape(2 * size, DH), buf[0, q, s].reshape(256, DH)
            ).astype(BF16).reshape(2, size, 256)
            part[i, u, 2, hidden, :] = dot_nt(
                wbuf[2, hidden, :], buf[1, q, s].reshape(256, DH)
            ).astype(BF16)
            return carry

        lax.fori_loop(us[0], us[-1] + 1, one, 0)
        at = slice(us[0], us[-1] + 1)
        exchange[i, us, span] = push(
            part.at[i, at, :, hidden, :], other.at[i, at, :, hidden, :], inner
        )

    def activate(i, us, span):
        arrived(exchange[i, us, span])
        left(exchange[i, us, span])
        start, size = span
        pair = slice(us[0], us[-1] + 1)
        step = 16 if len(us) == 2 or size % 32 else 32

        def some(r, carry):
            at = rows(start + step * r, step, 16)

            def full(m):
                return part[i, pair, m, at, :].astype(F32) + other[i, pair, m, at, :].astype(F32)

            gate, up_pre, back_grad = full(0), full(1), full(2)
            s = jax.nn.sigmoid(gate)
            silu = gate * s
            part[i, pair, 0, at, :] = (
                back_grad * up_pre * s * (1.0 + gate * (1.0 - s))
            ).astype(BF16)
            part[i, pair, 1, at, :] = (back_grad * silu).astype(BF16)
            part[i, pair, 2, at, :] = (silu * up_pre).astype(BF16)
            return carry

        lax.fori_loop(0, size // step, some, 0)

    def weight_terms(i, span, n):
        q = quarter[i]
        start, size = span
        hidden = slice(start, start + size)
        at = cols(n, B)
        pair, third = 0.0, 0.0
        for u in (0, 1):
            pair = pair + dot_nn(
                part[i, u, 0:2, hidden, :].reshape(2 * size, 256),
                buf[0, q, half(u), :, :, at].reshape(256, B),
            )
            third = third + dot_nn(
                part[i, u, 2, hidden, :], buf[1, q, half(u), :, :, at].reshape(256, B)
            )
        return pair.reshape(2, size, B), third

    def weight_grads(i, span):
        start, size = span
        hidden = slice(start, start + size)

        def block(n, carry):
            pair, third = weight_terms(i, span, n)
            at = cols(n, B)
            if i:
                pair = pair + acc[0:2, hidden, at]
                third = third + acc[2, hidden, at]
            acc[0:2, hidden, at] = pair
            acc[2, hidden, at] = third
            return carry

        lax.fori_loop(0, 4, block, 0)

    from_dw, own_dw = {}, []

    def last_weight_grads(i, span):
        if span == H0:
            for copies in from_w:
                for copy in copies:
                    left(copy)
        start, size = span
        hidden = slice(start, start + size)
        from_dw[span] = []
        for d in (1, 3, 2, 0):
            n = mod4(y + d)
            pair, third = weight_terms(i, span, n)
            at = cols(n, B)
            held = rows(Q * n + start, size, 16)
            wt[0:2, held, :] = (pair + acc[0:2, hidden, at]).astype(BF16)
            wt[2, held, :] = (third + acc[2, hidden, at]).astype(BF16)
            there = rows(Q * y + start, size, 16)
            if d:
                from_dw[span].append(push(wt.at[0:2, held, :], back.at[:, there, :], along_y[d]))
                from_dw[span].append(push(wt.at[2, held, :], ddown.at[there, :], along_y[d]))
            else:
                own_dw.append(bring(wt.at[0:2, held, :], back.at[:, there, :]))
                own_dw.append(bring(wt.at[2, held, :], ddown.at[there, :]))

    def turned(i, u):
        return part[i, u, 0:2].reshape(2 * Q, 256).T

    def token_terms(i, u, n, deltas):
        at = cols(n, B)
        dxs[i, u, :, :, at] = dot_nn(
            deltas, wbuf[0:2, :, at].reshape(2 * Q, B)
        ).astype(BF16).reshape(2, 128, B)

    core_dx = {}

    def token_grads(i, us):
        for u in us:
            deltas = turned(i, u)

            def block(n, carry):
                token_terms(i, u, n, deltas)
                return carry

            lax.fori_loop(0, 4, block, 0)
            core_dx[i, u] = push(dxs.at[i, u, 1 - c], dxr.at[i, u], sibling)

    def add_core(i, u, at):
        dxs[i, u, c, :, at] = (
            dxs[i, u, c, :, at].astype(F32) + dxr[i, u, :, at].astype(F32)
        ).astype(BF16)

    def add_core_whole(i, u):
        arrived(core_dx[i, u])

        def some(n, carry):
            add_core(i, u, cols(n, B))
            return carry

        lax.fori_loop(0, 4, some, 0)

    def block_rows(yb):
        return rows(32 * slot(mod4(yb)), 32)

    def along_z_grads(i, us):
        q = quarter[i]
        for u in us:
            add_core_whole(i, u)
            for d in (1, 3, 2):
                push(
                    dxs.at[i, u, c, block_rows(z + d - y), :], zr.at[q, u, d - 1], along_z[d],
                    zsem.at[q, u, d - 1],
                )

    from_yf, from_zy = {}, {}

    def along_y_grads():
        for u in (0, 1):
            add_core_whole(0, u)
        for d in (1, 3, 2):
            at = cols(mod4(y + d), B)
            from_yf[d] = push(dxs.at[0, :, c, :, at], yf.at[d - 1], along_y[d])

    def then_along_z():
        for d in (1, 3, 2):
            arrived(from_yf[d])
        for e in (1, 3, 2, 0):
            total = dxs[0, :, c, block_rows(z + e - y), cols(y, B)].astype(F32)
            for d in (1, 2, 3):
                total = total + yf[d - 1, :, block_rows(z + e - y + d), :].astype(F32)
            zs[e] = total.astype(BF16)
            if e:
                from_zy[e] = push(zs.at[e], zy.at[e - 1], along_z[e])

    def last_token_grads():
        core_last = {}
        deltas = turned(3, 1)
        for d in (1, 3, 2, 0):
            n = mod4(y + d)
            token_terms(3, 1, n, deltas)
            at = cols(n, B)
            core_last[d] = push(dxs.at[3, 1, 1 - c, :, at], dxr.at[3, 1, :, at], sibling)
        return core_last

    def last_along_z(core_last):
        for k, d in enumerate((1, 3, 2, 0)):
            at = cols(mod4(y + d), B)
            arrived(core_last[d])
            add_core(3, 1, at)
            for e in (1, 3, 2):
                push(
                    dxs.at[3, 1, c, block_rows(z + e - y), at],
                    zr.at[quarter[3], 1, e - 1, :, at], along_z[e], lastsem.at[k, e - 1],
                )

    whole, one, two = (0, 1), (0,), (1,)
    arrived(swap_far)
    spread(far, 1)
    relay(near, 0)
    arrived(*core_outer, *core_piece[0, 0], *core_piece[0, 1])
    own_w.wait()
    arrived(*from_w[0])
    forward(0, whole, H0)
    relay(far, 0)
    arrived(*from_w[1])
    forward(0, whole, H1)
    for i in (1, 2):
        arrived(*from_outer[i])
        core_outer.append(outer_to_sibling(i))
    arrived(*core_outer[1:], *core_piece[1, 0], *core_piece[2, 0])
    forward(1, one, H01)
    forward(2, one, H01)
    activate(0, whole, H0)
    relay(near, 1)
    activate(0, whole, H1)
    arrived(*from_w[2])
    forward(0, whole, H2)
    forward(1, one, H2)
    forward(2, one, H2)
    relay(far, 1)
    arrived(*core_piece[1, 1])
    forward(1, two, ALL)
    activate(1, one, H01)
    activate(2, one, H01)
    arrived(*core_piece[2, 1])
    forward(2, two, H0)
    activate(0, whole, H2)
    token_grads(0, whole)
    weight_grads(0, ALL)
    along_y_grads()
    activate(1, one, H2)
    token_grads(1, one)
    activate(2, one, H2)
    token_grads(2, one)
    along_z_grads(1, one)
    for copy, which, u in onward:
        arrived(copy)
        to_sibling(3, u, which)
    arrived(*from_outer[3])
    core_outer.append(outer_to_sibling(3))
    along_z_grads(2, one)
    activate(1, two, ALL)
    token_grads(1, two)
    arrived(core_outer[3], *core_piece[3, 0], *core_piece[3, 1])
    forward(3, whole, H0)
    forward(2, two, H12)
    along_z_grads(1, two)
    forward(3, whole, H1)
    weight_grads(1, ALL)
    activate(2, two, H0)
    weight_grads(2, H0)
    then_along_z()
    forward(3, one, H2)
    forward(3, two, H2)
    activate(3, whole, H0)
    last_weight_grads(3, H0)
    activate(2, two, H12)
    token_grads(2, two)
    weight_grads(2, H12)
    along_z_grads(2, two)
    activate(3, whole, H1)
    last_weight_grads(3, H1)
    activate(3, one, H2)
    token_grads(3, one)
    activate(3, two, H2)
    core_last = last_token_grads()
    last_weight_grads(3, H2)
    along_z_grads(3, one)
    last_along_z(core_last)

    def landed(ref, sem):
        pltpu.make_async_remote_copy(
            src_ref=ref, dst_ref=ref, send_sem=ssem.at[0], recv_sem=sem,
            device_id=along_z[1], device_id_type=MESH,
        ).wait_recv()

    for d in (1, 2, 3):
        for i, u in ((1, 0), (1, 1), (2, 0), (2, 1), (3, 0)):
            q = mod4(z - d + offs[i])
            landed(zr.at[q, u, d - 1], zsem.at[q, u, d - 1])
    keep = block_rows(z - y)
    from_x, from_yg = [], {}

    def over_x(k, d):
        at = cols(mod4(y + d), B)
        for e in (1, 2, 3):
            landed(zr.at[mod4(z - e + 2), 1, e - 1, :, at], lastsem.at[k, e - 1])

        for i in range(4):
            q = quarter[i]
            for u in (0, 1):
                terms = [zr[q, u, e - 1, :, at] for e in (1, 2, 3) if (offs[i] + e) % 4]
                if i:
                    terms.append(dxs[i, u, c, keep, at])
                if d == 0:
                    terms.append(zy[3 - offs[i], u] if i else zs[0, u])
                total = sum(term.astype(F32) for term in terms).astype(BF16)
                ys[0, q, half(u), :, at] = total[0:16]
                ys[1, q, half(u), :, at] = total[16:32]
        from_x.append(push(ys.at[1 - x_hi, :, :, :, at], xr.at[:, :, :, at], across))

    def over_y(k, d):
        at = cols(mod4(y + d), B)
        arrived(from_x[k])
        ys[x_hi, :, :, :, at] = (
            ys[x_hi, :, :, :, at].astype(F32) + xr[:, :, :, at].astype(F32)
        ).astype(BF16)
        if d:
            from_yg[d] = push(ys.at[x_hi, :, :, :, at], yr.at[d - 1], along_y[d])

    order = (1, 3, 2, 0)
    arrived(*from_zy.values())
    over_x(0, order[0])
    for k in (1, 2, 3):
        over_x(k, order[k])
        over_y(k - 1, order[k - 1])
    over_y(3, order[3])
    for copy in own_dw:
        copy.wait()
    for span in PARTS:
        arrived(*from_dw[span])
    total = ys[x_hi, :, :, :, cols(y, B)].astype(F32)
    for d in (1, 3, 2):
        arrived(from_yg[d])
        total = total + yr[d - 1].astype(F32)
    dx[...] = total.astype(BF16).reshape(128, B)
    left(*sent)


def finish(back, down, dgate, dup, ddown):
    dgate[...] = back[0].T.astype(F32)
    dup[...] = back[1].T.astype(F32)
    ddown[...] = down[...].astype(F32)


def local(tokens, gate_weight, up_weight, down_weight, grad_out):
    flops = 8 * 2 * 2048 * 2048 * 256
    back, ddown, dx = pl.pallas_call(
        kernel,
        out_shape=(
            jax.ShapeDtypeStruct((2, 4 * Q, B), BF16),
            jax.ShapeDtypeStruct((4 * Q, B), BF16),
            jax.ShapeDtypeStruct((128, B), BF16),
        ),
        in_specs=[pl.BlockSpec(memory_space=pl.ANY)] * 5,
        out_specs=(
            pl.BlockSpec(memory_space=pl.ANY),
            pl.BlockSpec(memory_space=pl.ANY),
            pl.BlockSpec(memory_space=pltpu.VMEM),
        ),
        scratch_shapes=[
            pltpu.VMEM((2, 4, 2, 2, 128, DH), BF16),
            pltpu.VMEM((2, B, 4 * Q), BF16),
            pltpu.VMEM((3, 4 * Q, B), BF16),
            pltpu.VMEM((3, Q, DH), BF16),
            pltpu.VMEM((4, 2, 3, Q, 256), BF16),
            pltpu.VMEM((4, 2, 3, Q, 256), BF16),
            pltpu.VMEM((3, Q, DH), F32),
            pltpu.VMEM((4, 2, 2, 128, DH), BF16),
            pltpu.VMEM((4, 2, 128, DH), BF16),
            pltpu.VMEM((4, 2, 3, 32, DH), BF16),
            pltpu.VMEM((2, 4, 2, 16, DH), BF16),
            pltpu.VMEM((4, 2, 16, DH), BF16),
            pltpu.VMEM((3, 4, 2, 16, B), BF16),
            pltpu.VMEM((3, 2, 128, B), BF16),
            pltpu.VMEM((4, 2, 32, B), BF16),
            pltpu.VMEM((3, 2, 32, B), BF16),
            pltpu.SemaphoreType.DMA((160,)),
            pltpu.SemaphoreType.DMA((160,)),
            pltpu.SemaphoreType.DMA((24,)),
            pltpu.SemaphoreType.DMA((4, 2, 3)),
            pltpu.SemaphoreType.DMA((4, 3)),
        ],
        compiler_params=pltpu.CompilerParams(
            collective_id=0, has_side_effects=True, vmem_limit_bytes=62 * 2**20
        ),
        cost_estimate=pl.CostEstimate(flops=flops, bytes_accessed=2**24, transcendentals=2**20),
    )(
        tokens.reshape(2, 4, 2, 16, 4096), grad_out.reshape(2, 4, 2, 16, 4096),
        gate_weight, up_weight, down_weight,
    )
    grads = pl.pallas_call(
        finish,
        grid=(7,),
        out_shape=(
            jax.ShapeDtypeStruct((B, 4 * Q), F32),
            jax.ShapeDtypeStruct((B, 4 * Q), F32),
            jax.ShapeDtypeStruct((4 * Q, B), F32),
        ),
        in_specs=[
            pl.BlockSpec((2, 128, B), lambda n: (0, n, 0)),
            pl.BlockSpec((128, B), lambda n: (n, 0)),
        ],
        out_specs=(
            pl.BlockSpec((B, 128), lambda n: (0, n)),
            pl.BlockSpec((B, 128), lambda n: (0, n)),
            pl.BlockSpec((128, B), lambda n: (n, 0)),
        ),
        cost_estimate=pl.CostEstimate(flops=0, bytes_accessed=2**23, transcendentals=0),
    )(back, ddown)
    return (dx, *grads)


def solution(mesh):
    return jax.shard_map(
        local,
        mesh=mesh,
        in_specs=(
            P("grp", None),
            P("grp", "shard"),
            P("grp", "shard"),
            P("shard", "grp"),
            P("grp", None),
        ),
        out_specs=(P("shard", "grp"), P("grp", "shard"), P("grp", "shard"), P("shard", "grp")),
        check_vma=False,
    )
```

```python
import functools

import jax
import jax.numpy as jnp
from jax import lax
from jax.experimental import pallas as pl
from jax.experimental.pallas import tpu as pltpu
from jax.sharding import PartitionSpec as P

MESH = pl.DeviceIdType.MESH
BF16 = jnp.bfloat16
F32 = jnp.float32

Q = 224
DH = 2048
B = 512
CHUNK = 512
H0, H1, H2 = COME = ((0, 80), (80, 80), (160, 64))
D0, D1, D2 = GO = ((0, 96), (96, 64), (160, 64))
H01, H12, D12, ALL = (0, 160), (80, 144), (96, 128), (0, Q)


def dot_nt(left, right):
    return lax.dot_general(left, right, (((1,), (1,)), ((), ())), preferred_element_type=F32)


def dot_nn(left, right):
    return lax.dot_general(left, right, (((1,), (0,)), ((), ())), preferred_element_type=F32)


def dot_tn(left, right):
    return lax.dot_general(left, right, (((0,), (0,)), ((), ())), preferred_element_type=F32)


def kernel(
    tok, grd, gate_w, up_w, down_w, back, ddown, dx,
    buf, raw, wt, wbuf, part, other, acc, dxs, dxr, zr, ys, xr, yr, yf, zs, zy,
    ssem, rsem, lsem, zsem, lastsem,
):
    grp, shard = lax.axis_index("grp"), lax.axis_index("shard")
    x_lo, y = lax.div(grp, 4), lax.rem(grp, 4)
    x_hi, z, c = lax.div(shard, 8), lax.rem(lax.div(shard, 2), 4), lax.rem(shard, 2)
    x = 2 * x_hi + x_lo

    def mod4(v):
        return lax.rem(v + 8, 4)

    def slot(dy):
        return dy + lax.div(dy, 2) * (1 - 2 * lax.rem(dy, 2))

    def device(x, y, z, c):
        return (4 * lax.rem(x, 2) + y, 8 * lax.div(x, 2) + 2 * z + c)

    sibling = device(x, y, z, 1 - c)
    inner = device(x + 1 - 2 * x_lo, y, z, c)
    outer = device(mod4(x - 1 + 2 * x_lo), y, z, c)
    across = device(mod4(x + 2), y, z, c)
    along_y = {d: device(x, mod4(y + d), z, c) for d in (1, 2, 3)}
    along_z = {d: device(x, y, mod4(z + d), c) for d in (1, 2, 3)}

    barrier = pltpu.get_barrier_semaphore()
    partners = [sibling, inner, outer, across, *along_y.values(), *along_z.values()]
    for partner in partners:
        pl.semaphore_signal(barrier, inc=1, device_id=partner, device_id_type=MESH)

    count = [0]
    sent = []

    def push(src, dst, target, recv=None):
        n = count[0]
        count[0] += 1
        copy = pltpu.make_async_remote_copy(
            src_ref=src, dst_ref=dst, send_sem=ssem.at[n],
            recv_sem=rsem.at[n] if recv is None else recv,
            device_id=target, device_id_type=MESH,
        )
        copy.start()
        sent.append(copy)
        return copy

    local_count = [0]

    def bring(src, dst):
        n = local_count[0]
        local_count[0] += 1
        copy = pltpu.make_async_copy(src, dst, lsem.at[n])
        copy.start()
        return copy

    def arrived(*copies):
        for copy in copies:
            copy.wait_recv()

    gone = set()

    def left(*copies):
        for copy in copies:
            if id(copy) not in gone:
                gone.add(id(copy))
                copy.wait_send()

    def rows(start, size, step=32):
        return pl.ds(pl.multiple_of(start, step), size)

    def cols(block, size):
        return pl.ds(pl.multiple_of(block * size, size), size)

    mine, theirs = cols(x_lo, DH), cols(1 - x_lo, DH)
    offs = (0, 1, 3, 2)
    quarter = [mod4(z + off) for off in offs]
    first, second = x_hi, 1 - x_hi

    def half(u):
        return first + u * (1 - 2 * first)

    own_tok = [
        bring(src.at[h, :, s, :, mine], buf.at[a, :, s, h, 0, x_lo])
        for s in (0, 1)
        for h in (0, 1)
        for a, src in enumerate((tok, grd))
    ]
    own_raw = [bring(gate_w, raw.at[0]), bring(up_w, raw.at[1]), bring(down_w, wt.at[2])]
    for copy in own_raw:
        copy.wait()
    for m in (0, 1):
        def turn(n, carry):
            wt[m, cols(n, 128), :] = raw[m, :, cols(n, 128)].T
            return carry

        lax.fori_loop(0, 7, turn, 0)
    own_w = bring(wt.at[:, rows(Q * y, Q), :], wbuf.at[:, :, cols(y, B)])
    for copy in own_tok:
        copy.wait()
    pl.semaphore_wait(barrier, len(partners))

    def send_outer(i, target):
        q = quarter[i]
        return [
            push(src.at[c, q, :, :, theirs], buf.at[a, q, :, c, 0, x_lo], target)
            for a, src in enumerate((tok, grd))
        ]

    from_outer = {0: send_outer(0, outer), 2: send_outer(2, inner)}

    blocks = (x_lo, 1 - x_lo)

    def send_y(d, b):
        n = {1: 2, 3: 1, 2: 3}[d]
        lo = blocks[b]
        return push(buf.at[:, z, first, c, 0, lo], buf.at[:, z, first, c, n, lo], along_y[d])

    def near(b, s, q):
        return buf.at[:, q, s, c, 1:3, blocks[b]]

    def far(b, s, q):
        return buf.at[:, q, s, c, 3:4, blocks[b]]

    core_piece = {(i, u): [] for i in range(4) for u in (0, 1)}

    def to_sibling(i, u, which, b):
        ref = which(b, half(u), quarter[i])
        core_piece[i, u].append(push(ref, ref, sibling))

    from_z, swaps = {}, {}

    def spread(which, b, u):
        ref = which(b, half(u), z)
        from_z[which, b, u] = push(ref, ref, along_z[1]), push(ref, ref, along_z[3])
        to_sibling(0, u, which, b)

    def swap(which, b):
        ref = which(b, first, z)
        swaps[which, b] = push(ref, ref, across)

    y_near, y_far = [send_y(1, 0), send_y(3, 0)], [send_y(2, 0)]
    arrived(*y_near)
    spread(near, 0, 0)
    arrived(*y_far)
    spread(far, 0, 0)
    arrived(*from_outer[0])
    y_near, y_far = [send_y(1, 1), send_y(3, 1)], [send_y(2, 1)]
    swap(near, 0)
    swap(far, 0)

    def send_w(h):
        start, size = COME[h]
        return [
            push(
                wt.at[:, rows(Q * mod4(y + d) + start, size, 16), :],
                wbuf.at[:, start : start + size, cols(y, B)],
                along_y[d],
            )
            for d in (1, 3, 2)
        ]

    from_w = [send_w(h) for h in range(len(COME))]

    def outer_to_sibling(i):
        ref = buf.at[:, quarter[i], :, c, 0, 1 - x_lo]
        return push(ref, ref, sibling)

    core_outer = [outer_to_sibling(0)]

    arrived(*y_near)
    swap(near, 1)
    spread(near, 1, 0)
    arrived(*y_far)
    swap(far, 1)
    spread(far, 1, 0)
    from_outer[1] = send_outer(1, outer)
    from_outer[3] = send_outer(3, outer)
    for b in (0, 1):
        for which in (near, far):
            arrived(swaps[which, b])
            spread(which, b, 1)
    for i in (1, 2):
        arrived(*from_outer[i])
        core_outer.append(outer_to_sibling(i))

    onward = []

    def relay(which, b, u):
        up, down = from_z[which, b, u]
        arrived(up)
        if u == 0:
            ref = which(b, half(u), quarter[2])
            onward.append((push(ref, ref, along_z[1]), which, b, u))
        to_sibling(2, u, which, b)
        arrived(down)
        if u == 1:
            ref = which(b, half(u), quarter[1])
            onward.append((push(ref, ref, along_z[3]), which, b, u))
        to_sibling(1, u, which, b)

    exchange = {}

    def forward(i, us, span):
        q = quarter[i]
        start, size = span
        hidden = slice(start, start + size)

        def one(u, carry):
            s = half(u)
            part[i, u, 0:2, hidden, :] = dot_nt(
                wbuf[0:2, hidden, :].reshape(2 * size, DH), buf[0, q, s].reshape(256, DH)
            ).astype(BF16).reshape(2, size, 256)
            part[i, u, 2, hidden, :] = dot_nt(
                wbuf[2, hidden, :], buf[1, q, s].reshape(256, DH)
            ).astype(BF16)
            return carry

        lax.fori_loop(us[0], us[-1] + 1, one, 0)
        at = slice(us[0], us[-1] + 1)
        exchange[i, us, span] = push(
            part.at[i, at, :, hidden, :], other.at[i, at, :, hidden, :], inner
        )

    def activate(i, us, span):
        arrived(exchange[i, us, span])
        left(exchange[i, us, span])
        start, size = span
        pair = slice(us[0], us[-1] + 1)
        step = 16 if len(us) == 2 or size % 32 else 32

        def some(r, carry):
            at = rows(start + step * r, step, 16)

            def full(m):
                return part[i, pair, m, at, :].astype(F32) + other[i, pair, m, at, :].astype(F32)

            gate, up_pre, back_grad = full(0), full(1), full(2)
            s = jax.nn.sigmoid(gate)
            silu = gate * s
            part[i, pair, 0, at, :] = (
                back_grad * up_pre * s * (1.0 + gate * (1.0 - s))
            ).astype(BF16)
            part[i, pair, 1, at, :] = (back_grad * silu).astype(BF16)
            part[i, pair, 2, at, :] = (silu * up_pre).astype(BF16)
            return carry

        lax.fori_loop(0, size // step, some, 0)

    def weight_terms(i, span, n):
        q = quarter[i]
        start, size = span
        hidden = slice(start, start + size)
        at = cols(n, B)
        pair, third = 0.0, 0.0
        for u in (0, 1):
            pair = pair + dot_nn(
                part[i, u, 0:2, hidden, :].reshape(2 * size, 256),
                buf[0, q, half(u), :, :, :, :, at].reshape(256, B),
            )
            third = third + dot_nn(
                part[i, u, 2, hidden, :], buf[1, q, half(u), :, :, :, :, at].reshape(256, B)
            )
        return pair.reshape(2, size, B), third

    def weight_grads(i, span):
        start, size = span
        hidden = slice(start, start + size)

        def block(n, carry):
            pair, third = weight_terms(i, span, n)
            at = cols(n, B)
            if i:
                pair = pair + acc[0:2, hidden, at]
                third = third + acc[2, hidden, at]
            acc[0:2, hidden, at] = pair
            acc[2, hidden, at] = third
            return carry

        lax.fori_loop(0, 4, block, 0)

    from_dw, own_dw = {}, []

    def last_weight_grads(i, span):
        if span == D0:
            for copies in from_w:
                for copy in copies:
                    left(copy)
        start, size = span
        hidden = slice(start, start + size)
        from_dw[span] = []
        for d in (1, 3, 2, 0):
            n = mod4(y + d)
            pair, third = weight_terms(i, span, n)
            at = cols(n, B)
            held = rows(Q * n + start, size, 16)
            wt[0:2, held, :] = (pair + acc[0:2, hidden, at]).astype(BF16)
            wt[2, held, :] = (third + acc[2, hidden, at]).astype(BF16)
            there = rows(Q * y + start, size, 16)
            if d:
                from_dw[span].append(push(wt.at[0:2, held, :], back.at[:, there, :], along_y[d]))
                from_dw[span].append(push(wt.at[2, held, :], ddown.at[there, :], along_y[d]))
            else:
                own_dw.append(bring(wt.at[0:2, held, :], back.at[:, there, :]))
                own_dw.append(bring(wt.at[2, held, :], ddown.at[there, :]))

    def turned(i, u):
        return part[i, u, 0:2].reshape(2 * Q, 256).T

    def token_terms(i, u, n, deltas):
        at = cols(n, B)
        dxs[i, u, :, :, at] = dot_nn(
            deltas, wbuf[0:2, :, at].reshape(2 * Q, B)
        ).astype(BF16).reshape(2, 128, B)

    core_dx = {}

    def token_grads(i, us):
        for u in us:
            deltas = turned(i, u)

            def block(n, carry):
                token_terms(i, u, n, deltas)
                return carry

            lax.fori_loop(0, 4, block, 0)
            core_dx[i, u] = push(dxs.at[i, u, 1 - c], dxr.at[i, u], sibling)

    def add_core(i, u, at):
        dxs[i, u, c, :, at] = (
            dxs[i, u, c, :, at].astype(F32) + dxr[i, u, :, at].astype(F32)
        ).astype(BF16)

    def add_core_whole(i, u):
        arrived(core_dx[i, u])

        def some(n, carry):
            add_core(i, u, cols(n, B))
            return carry

        lax.fori_loop(0, 4, some, 0)

    def block_rows(yb):
        return rows(32 * slot(mod4(yb)), 32)

    def along_z_grads(i, us):
        q = quarter[i]
        for u in us:
            add_core_whole(i, u)
            for d in (1, 3, 2):
                push(
                    dxs.at[i, u, c, block_rows(z + d - y), :], zr.at[q, u, d - 1], along_z[d],
                    zsem.at[q, u, d - 1],
                )

    from_yf, from_zy = {}, {}

    def along_y_grads():
        for u in (0, 1):
            add_core_whole(0, u)
        for d in (1, 3, 2):
            at = cols(mod4(y + d), B)
            from_yf[d] = push(dxs.at[0, :, c, :, at], yf.at[d - 1], along_y[d])

    def then_along_z():
        for d in (1, 3, 2):
            arrived(from_yf[d])
        for e in (1, 3, 2, 0):
            total = dxs[0, :, c, block_rows(z + e - y), cols(y, B)].astype(F32)
            for d in (1, 2, 3):
                total = total + yf[d - 1, :, block_rows(z + e - y + d), :].astype(F32)
            zs[e] = total.astype(BF16)
            if e:
                from_zy[e] = push(zs.at[e], zy.at[e - 1], along_z[e])

    def last_token_grads():
        core_last = {}
        deltas = turned(3, 1)
        for d in (1, 3, 2, 0):
            n = mod4(y + d)
            token_terms(3, 1, n, deltas)
            at = cols(n, B)
            core_last[d] = push(dxs.at[3, 1, 1 - c, :, at], dxr.at[3, 1, :, at], sibling)
        return core_last

    def last_along_z(core_last):
        for k, d in enumerate((1, 3, 2, 0)):
            at = cols(mod4(y + d), B)
            arrived(core_last[d])
            add_core(3, 1, at)
            for e in (1, 3, 2):
                push(
                    dxs.at[3, 1, c, block_rows(z + e - y), at],
                    zr.at[quarter[3], 1, e - 1, :, at], along_z[e], lastsem.at[k, e - 1],
                )

    whole, one, two = (0, 1), (0,), (1,)
    for b in (0, 1):
        relay(near, b, 0)
        relay(far, b, 0)
    arrived(core_outer[0], *core_piece[0, 0], *core_piece[0, 1])
    own_w.wait()
    arrived(*from_w[0])
    forward(0, whole, H0)
    arrived(*core_outer[1:], *core_piece[1, 0], *core_piece[2, 0])
    forward(1, one, H0)
    relay(near, 0, 1)
    relay(far, 0, 1)
    arrived(*from_w[1])
    forward(0, whole, H1)
    forward(2, one, D0)
    activate(0, whole, H0)
    relay(near, 1, 1)
    relay(far, 1, 1)
    activate(1, one, H0)
    arrived(*from_w[2])
    forward(0, whole, H2)
    forward(1, one, H12)
    arrived(*core_piece[1, 1])
    forward(1, two, ALL)
    arrived(*core_piece[2, 1])
    forward(2, two, D0)
    activate(0, whole, H1)
    weight_grads(0, H01)
    activate(2, one, D0)
    activate(0, whole, H2)
    token_grads(0, whole)
    weight_grads(0, H2)
    along_y_grads()
    activate(1, one, H12)
    token_grads(1, one)
    for copy, which, b, u in onward:
        arrived(copy)
        to_sibling(3, u, which, b)
    arrived(*from_outer[3])
    core_outer.append(outer_to_sibling(3))
    along_z_grads(1, one)
    arrived(core_outer[3], *core_piece[3, 0], *core_piece[3, 1])
    forward(3, whole, D0)
    activate(1, two, ALL)
    token_grads(1, two)
    forward(2, one, D12)
    weight_grads(1, ALL)
    along_z_grads(1, two)
    activate(2, two, D0)
    weight_grads(2, D0)
    then_along_z()
    forward(3, one, D12)
    activate(3, whole, D0)
    last_weight_grads(3, D0)
    forward(2, two, D1)
    forward(3, two, D1)
    activate(2, one, D12)
    token_grads(2, one)
    forward(2, two, D2)
    forward(3, two, D2)
    along_z_grads(2, one)
    activate(3, one, D12)
    token_grads(3, one)
    activate(2, two, D1)
    along_z_grads(3, one)
    weight_grads(2, D1)
    activate(3, two, D1)
    last_weight_grads(3, D1)
    activate(2, two, D2)
    token_grads(2, two)
    activate(3, two, D2)
    core_last = last_token_grads()
    along_z_grads(2, two)
    weight_grads(2, D2)
    last_weight_grads(3, D2)
    last_along_z(core_last)

    def landed(ref, sem):
        pltpu.make_async_remote_copy(
            src_ref=ref, dst_ref=ref, send_sem=ssem.at[0], recv_sem=sem,
            device_id=along_z[1], device_id_type=MESH,
        ).wait_recv()

    def land(i, u):
        for d in (1, 2, 3):
            q = mod4(z - d + offs[i])
            landed(zr.at[q, u, d - 1], zsem.at[q, u, d - 1])

    keep = block_rows(z - y)
    from_x, from_yg = [], {}

    def over_x(u, at, own):
        for i in range(4):
            q = quarter[i]
            terms = [zr[q, u, e - 1, :, at] for e in (1, 2, 3) if (offs[i] + e) % 4]
            if i:
                terms.append(dxs[i, u, c, keep, at])
            if own:
                terms.append(zy[3 - offs[i], u] if i else zs[0, u])
            total = sum(term.astype(F32) for term in terms).astype(BF16)
            ys[0, q, half(u), :, at] = total[0:16]
            ys[1, q, half(u), :, at] = total[16:32]

    def first_over_x():
        for d in (1, 3, 2, 0):
            over_x(0, cols(mod4(y + d), B), d == 0)
        return push(ys.at[1 - x_hi, :, half(0)], xr.at[:, half(0)], across)

    def then_over_x(k, d):
        at = cols(mod4(y + d), B)
        for e in (1, 2, 3):
            landed(zr.at[mod4(z - e + 2), 1, e - 1, :, at], lastsem.at[k, e - 1])
        over_x(1, at, d == 0)
        from_x.append(
            push(ys.at[1 - x_hi, :, half(1), :, at], xr.at[:, half(1), :, at], across)
        )

    def over_y(k, d):
        at = cols(mod4(y + d), B)
        arrived(from_x[k])
        ys[x_hi, :, :, :, at] = (
            ys[x_hi, :, :, :, at].astype(F32) + xr[:, :, :, at].astype(F32)
        ).astype(BF16)
        if d:
            from_yg[d] = push(ys.at[x_hi, :, :, :, at], yr.at[d - 1], along_y[d])

    order = (1, 3, 2, 0)
    for i in (1, 2, 3):
        land(i, 0)
    arrived(*from_zy.values())
    from_first = first_over_x()
    land(1, 1)
    land(2, 1)
    then_over_x(0, order[0])
    arrived(from_first)
    for k in (1, 2, 3):
        then_over_x(k, order[k])
        over_y(k - 1, order[k - 1])
    over_y(3, order[3])
    for copy in own_dw:
        copy.wait()
    for span in GO:
        arrived(*from_dw[span])
    total = ys[x_hi, :, :, :, cols(y, B)].astype(F32)
    for d in (1, 3, 2):
        arrived(from_yg[d])
        total = total + yr[d - 1].astype(F32)
    dx[...] = total.astype(BF16).reshape(128, B)
    left(*sent)


def finish(back, down, dgate, dup, ddown):
    dgate[...] = back[0].astype(F32).T
    dup[...] = back[1].astype(F32).T
    ddown[...] = down[...].astype(F32)


def local(tokens, gate_weight, up_weight, down_weight, grad_out):
    flops = 8 * 2 * 2048 * 2048 * 256
    back, ddown, dx = pl.pallas_call(
        kernel,
        out_shape=(
            jax.ShapeDtypeStruct((2, 4 * Q, B), BF16),
            jax.ShapeDtypeStruct((4 * Q, B), BF16),
            jax.ShapeDtypeStruct((128, B), BF16),
        ),
        in_specs=[pl.BlockSpec(memory_space=pl.ANY)] * 5,
        out_specs=(
            pl.BlockSpec(memory_space=pl.ANY),
            pl.BlockSpec(memory_space=pl.ANY),
            pl.BlockSpec(memory_space=pltpu.VMEM),
        ),
        scratch_shapes=[
            pltpu.VMEM((2, 4, 2, 2, 4, 2, 16, DH), BF16),
            pltpu.VMEM((2, B, 4 * Q), BF16),
            pltpu.VMEM((3, 4 * Q, B), BF16),
            pltpu.VMEM((3, Q, DH), BF16),
            pltpu.VMEM((4, 2, 3, Q, 256), BF16),
            pltpu.VMEM((4, 2, 3, Q, 256), BF16),
            pltpu.VMEM((3, Q, DH), F32),
            pltpu.VMEM((4, 2, 2, 128, DH), BF16),
            pltpu.VMEM((4, 2, 128, DH), BF16),
            pltpu.VMEM((4, 2, 3, 32, DH), BF16),
            pltpu.VMEM((2, 4, 2, 16, DH), BF16),
            pltpu.VMEM((4, 2, 16, DH), BF16),
            pltpu.VMEM((3, 4, 2, 16, B), BF16),
            pltpu.VMEM((3, 2, 128, B), BF16),
            pltpu.VMEM((4, 2, 32, B), BF16),
            pltpu.VMEM((3, 2, 32, B), BF16),
            pltpu.SemaphoreType.DMA((224,)),
            pltpu.SemaphoreType.DMA((224,)),
            pltpu.SemaphoreType.DMA((24,)),
            pltpu.SemaphoreType.DMA((4, 2, 3)),
            pltpu.SemaphoreType.DMA((4, 3)),
        ],
        compiler_params=pltpu.CompilerParams(
            collective_id=0, has_side_effects=True, vmem_limit_bytes=62 * 2**20
        ),
        cost_estimate=pl.CostEstimate(flops=flops, bytes_accessed=2**24, transcendentals=2**20),
    )(
        tokens.reshape(2, 4, 2, 16, 4096), grad_out.reshape(2, 4, 2, 16, 4096),
        gate_weight, up_weight, down_weight,
    )
    grads = pl.pallas_call(
        finish,
        grid=(2,),
        out_shape=(
            jax.ShapeDtypeStruct((B, 4 * Q), F32),
            jax.ShapeDtypeStruct((B, 4 * Q), F32),
            jax.ShapeDtypeStruct((4 * Q, B), F32),
        ),
        in_specs=[
            pl.BlockSpec((2, 4 * Q, B // 2), lambda n: (0, 0, n)),
            pl.BlockSpec((2 * Q, B), lambda n: (n, 0)),
        ],
        out_specs=(
            pl.BlockSpec((B // 2, 4 * Q), lambda n: (n, 0)),
            pl.BlockSpec((B // 2, 4 * Q), lambda n: (n, 0)),
            pl.BlockSpec((2 * Q, B), lambda n: (n, 0)),
        ),
        compiler_params=pltpu.CompilerParams(vmem_limit_bytes=40 * 2**20),
        cost_estimate=pl.CostEstimate(flops=0, bytes_accessed=2**23, transcendentals=0),
    )(back, ddown)
    return (dx, *grads)


def solution(mesh):
    return jax.shard_map(
        local,
        mesh=mesh,
        in_specs=(
            P("grp", None),
            P("grp", "shard"),
            P("grp", "shard"),
            P("shard", "grp"),
            P("grp", None),
        ),
        out_specs=(P("shard", "grp"), P("grp", "shard"), P("grp", "shard"), P("shard", "grp")),
        check_vma=False,
    )
```

```python
import functools

import jax
import jax.numpy as jnp
from jax import lax
from jax.experimental import pallas as pl
from jax.experimental.pallas import tpu as pltpu
from jax.sharding import PartitionSpec as P

MESH = pl.DeviceIdType.MESH
BF16 = jnp.bfloat16
F32 = jnp.float32

Q = 224
DH = 2048
B = 512
CHUNK = 512
H0, H1, H2 = COME = ((0, 64), (64, 80), (144, 80))
D0, D1, D2 = GO = ((0, 96), (96, 64), (160, 64))
H01, H12, REST0, D12, ALL = (0, 144), (64, 160), (64, 32), (96, 128), (0, Q)


def dot_nt(left, right):
    return lax.dot_general(left, right, (((1,), (1,)), ((), ())), preferred_element_type=F32)


def dot_nn(left, right):
    return lax.dot_general(left, right, (((1,), (0,)), ((), ())), preferred_element_type=F32)


def dot_tn(left, right):
    return lax.dot_general(left, right, (((0,), (0,)), ((), ())), preferred_element_type=F32)


def kernel(
    tok, grd, gate_w, up_w, down_w, back, ddown, dx,
    buf, raw, wt, wbuf, part, other, acc, dxs, dxr, zr, ys, xr, yr, yf, zs, zy,
    ssem, rsem, lsem, zsem, lastsem,
):
    grp, shard = lax.axis_index("grp"), lax.axis_index("shard")
    x_lo, y = lax.div(grp, 4), lax.rem(grp, 4)
    x_hi, z, c = lax.div(shard, 8), lax.rem(lax.div(shard, 2), 4), lax.rem(shard, 2)
    x = 2 * x_hi + x_lo

    def mod4(v):
        return lax.rem(v + 8, 4)

    def slot(dy):
        return dy + lax.div(dy, 2) * (1 - 2 * lax.rem(dy, 2))

    def device(x, y, z, c):
        return (4 * lax.rem(x, 2) + y, 8 * lax.div(x, 2) + 2 * z + c)

    sibling = device(x, y, z, 1 - c)
    inner = device(x + 1 - 2 * x_lo, y, z, c)
    outer = device(mod4(x - 1 + 2 * x_lo), y, z, c)
    across = device(mod4(x + 2), y, z, c)
    along_y = {d: device(x, mod4(y + d), z, c) for d in (1, 2, 3)}
    along_z = {d: device(x, y, mod4(z + d), c) for d in (1, 2, 3)}

    barrier = pltpu.get_barrier_semaphore()
    partners = [sibling, inner, outer, across, *along_y.values(), *along_z.values()]
    for partner in partners:
        pl.semaphore_signal(barrier, inc=1, device_id=partner, device_id_type=MESH)

    count = [0]
    sent = []

    def push(src, dst, target, recv=None):
        n = count[0]
        count[0] += 1
        copy = pltpu.make_async_remote_copy(
            src_ref=src, dst_ref=dst, send_sem=ssem.at[n],
            recv_sem=rsem.at[n] if recv is None else recv,
            device_id=target, device_id_type=MESH,
        )
        copy.start()
        sent.append(copy)
        return copy

    local_count = [0]

    def bring(src, dst):
        n = local_count[0]
        local_count[0] += 1
        copy = pltpu.make_async_copy(src, dst, lsem.at[n])
        copy.start()
        return copy

    def arrived(*copies):
        for copy in copies:
            copy.wait_recv()

    gone = set()

    def left(*copies):
        for copy in copies:
            if id(copy) not in gone:
                gone.add(id(copy))
                copy.wait_send()

    def rows(start, size, step=32):
        return pl.ds(pl.multiple_of(start, step), size)

    def cols(block, size):
        return pl.ds(pl.multiple_of(block * size, size), size)

    mine, theirs = cols(x_lo, DH), cols(1 - x_lo, DH)
    offs = (0, 1, 3, 2)
    quarter = [mod4(z + off) for off in offs]
    first, second = x_hi, 1 - x_hi

    def half(u):
        return first + u * (1 - 2 * first)

    own_tok = [
        bring(src.at[h, :, s, :, mine], buf.at[a, :, s, h, 0, x_lo])
        for s in (0, 1)
        for h in (0, 1)
        for a, src in enumerate((tok, grd))
    ]
    own_raw = [bring(gate_w, raw.at[0]), bring(up_w, raw.at[1]), bring(down_w, wt.at[2])]
    for copy in own_raw:
        copy.wait()
    for m in (0, 1):
        def turn(n, carry):
            wt[m, cols(n, 128), :] = raw[m, :, cols(n, 128)].T
            return carry

        lax.fori_loop(0, 7, turn, 0)
    own_w = bring(wt.at[:, rows(Q * y, Q), :], wbuf.at[:, :, cols(y, B)])
    for copy in own_tok:
        copy.wait()
    pl.semaphore_wait(barrier, len(partners))

    def send_outer(i, target):
        q = quarter[i]
        return [
            push(src.at[c, q, :, :, theirs], buf.at[a, q, :, c, 0, x_lo], target)
            for a, src in enumerate((tok, grd))
        ]

    from_outer = {0: send_outer(0, outer), 2: send_outer(2, inner)}

    blocks = (x_lo, 1 - x_lo)

    def send_y(d, b):
        n = {1: 2, 3: 1, 2: 3}[d]
        lo = blocks[b]
        return push(buf.at[:, z, first, c, 0, lo], buf.at[:, z, first, c, n, lo], along_y[d])

    def near(b, s, q):
        return buf.at[:, q, s, c, 1:3, blocks[b]]

    def far(b, s, q):
        return buf.at[:, q, s, c, 3:4, blocks[b]]

    core_piece = {(i, u): [] for i in range(4) for u in (0, 1)}

    def to_sibling(i, u, which, b):
        ref = which(b, half(u), quarter[i])
        core_piece[i, u].append(push(ref, ref, sibling))

    from_z, swaps = {}, {}

    def spread(which, b, u):
        ref = which(b, half(u), z)
        from_z[which, b, u] = push(ref, ref, along_z[1]), push(ref, ref, along_z[3])
        to_sibling(0, u, which, b)

    def swap(which, b):
        ref = which(b, first, z)
        swaps[which, b] = push(ref, ref, across)

    y_near, y_far = [send_y(1, 0), send_y(3, 0)], [send_y(2, 0)]
    arrived(*y_near)
    spread(near, 0, 0)
    arrived(*y_far)
    spread(far, 0, 0)
    arrived(*from_outer[0])
    y_near, y_far = [send_y(1, 1), send_y(3, 1)], [send_y(2, 1)]
    swap(near, 0)
    swap(far, 0)

    def send_w(h):
        start, size = COME[h]
        return [
            push(
                wt.at[:, rows(Q * mod4(y + d) + start, size, 16), :],
                wbuf.at[:, start : start + size, cols(y, B)],
                along_y[d],
            )
            for d in (1, 3, 2)
        ]

    from_w = [send_w(h) for h in range(len(COME))]

    def outer_to_sibling(i):
        ref = buf.at[:, quarter[i], :, c, 0, 1 - x_lo]
        return push(ref, ref, sibling)

    core_outer = [outer_to_sibling(0)]

    arrived(*y_near)
    swap(near, 1)
    spread(near, 1, 0)
    arrived(*y_far)
    swap(far, 1)
    spread(far, 1, 0)
    from_outer[1] = send_outer(1, outer)
    from_outer[3] = send_outer(3, outer)
    for b in (0, 1):
        for which in (near, far):
            arrived(swaps[which, b])
            spread(which, b, 1)
    arrived(*from_outer[2])
    core_outer.append(outer_to_sibling(2))

    onward = []

    def relay(which, b, u):
        up, down = from_z[which, b, u]
        arrived(up)
        if u == 0:
            ref = which(b, half(u), quarter[2])
            onward.append((push(ref, ref, along_z[1]), which, b, u))
        to_sibling(2, u, which, b)
        arrived(down)
        if u == 1:
            ref = which(b, half(u), quarter[1])
            onward.append((push(ref, ref, along_z[3]), which, b, u))
        to_sibling(1, u, which, b)

    exchange = {}

    def forward(i, us, span):
        q = quarter[i]
        start, size = span
        hidden = slice(start, start + size)

        def one(u, carry):
            s = half(u)
            part[i, u, 0:2, hidden, :] = dot_nt(
                wbuf[0:2, hidden, :].reshape(2 * size, DH), buf[0, q, s].reshape(256, DH)
            ).astype(BF16).reshape(2, size, 256)
            part[i, u, 2, hidden, :] = dot_nt(
                wbuf[2, hidden, :], buf[1, q, s].reshape(256, DH)
            ).astype(BF16)
            return carry

        lax.fori_loop(us[0], us[-1] + 1, one, 0)
        at = slice(us[0], us[-1] + 1)
        exchange[i, us, span] = push(
            part.at[i, at, :, hidden, :], other.at[i, at, :, hidden, :], inner
        )

    def activate(i, us, span):
        arrived(exchange[i, us, span])
        left(exchange[i, us, span])
        start, size = span
        pair = slice(us[0], us[-1] + 1)
        step = 16 if len(us) == 2 or size % 32 else 32

        def some(r, carry):
            at = rows(start + step * r, step, 16)

            def full(m):
                return part[i, pair, m, at, :].astype(F32) + other[i, pair, m, at, :].astype(F32)

            gate, up_pre, back_grad = full(0), full(1), full(2)
            s = jax.nn.sigmoid(gate)
            silu = gate * s
            part[i, pair, 0, at, :] = (
                back_grad * up_pre * s * (1.0 + gate * (1.0 - s))
            ).astype(BF16)
            part[i, pair, 1, at, :] = (back_grad * silu).astype(BF16)
            part[i, pair, 2, at, :] = (silu * up_pre).astype(BF16)
            return carry

        lax.fori_loop(0, size // step, some, 0)

    def weight_terms(i, span, n):
        q = quarter[i]
        start, size = span
        hidden = slice(start, start + size)
        at = cols(n, B)
        pair, third = 0.0, 0.0
        for u in (0, 1):
            pair = pair + dot_nn(
                part[i, u, 0:2, hidden, :].reshape(2 * size, 256),
                buf[0, q, half(u), :, :, :, :, at].reshape(256, B),
            )
            third = third + dot_nn(
                part[i, u, 2, hidden, :], buf[1, q, half(u), :, :, :, :, at].reshape(256, B)
            )
        return pair.reshape(2, size, B), third

    def weight_grads(i, span):
        start, size = span
        hidden = slice(start, start + size)

        def block(n, carry):
            pair, third = weight_terms(i, span, n)
            at = cols(n, B)
            if i:
                pair = pair + acc[0:2, hidden, at]
                third = third + acc[2, hidden, at]
            acc[0:2, hidden, at] = pair
            acc[2, hidden, at] = third
            return carry

        lax.fori_loop(0, 4, block, 0)

    from_dw, own_dw = {}, []

    def last_weight_grads(i, span):
        if span == D0:
            for copies in from_w:
                for copy in copies:
                    left(copy)
        start, size = span
        hidden = slice(start, start + size)
        from_dw[span] = []
        for d in (1, 3, 2, 0):
            n = mod4(y + d)
            pair, third = weight_terms(i, span, n)
            at = cols(n, B)
            held = rows(Q * n + start, size, 16)
            wt[0:2, held, :] = (pair + acc[0:2, hidden, at]).astype(BF16)
            wt[2, held, :] = (third + acc[2, hidden, at]).astype(BF16)
            there = rows(Q * y + start, size, 16)
            if d:
                from_dw[span].append(push(wt.at[0:2, held, :], back.at[:, there, :], along_y[d]))
                from_dw[span].append(push(wt.at[2, held, :], ddown.at[there, :], along_y[d]))
            else:
                own_dw.append(bring(wt.at[0:2, held, :], back.at[:, there, :]))
                own_dw.append(bring(wt.at[2, held, :], ddown.at[there, :]))

    def turned(i, u):
        return part[i, u, 0:2].reshape(2 * Q, 256).T

    def token_terms(i, u, n, deltas):
        at = cols(n, B)
        dxs[i, u, :, :, at] = dot_nn(
            deltas, wbuf[0:2, :, at].reshape(2 * Q, B)
        ).astype(BF16).reshape(2, 128, B)

    core_dx = {}

    def token_grads(i, us):
        for u in us:
            deltas = turned(i, u)

            def block(n, carry):
                token_terms(i, u, n, deltas)
                return carry

            lax.fori_loop(0, 4, block, 0)
            core_dx[i, u] = push(dxs.at[i, u, 1 - c], dxr.at[i, u], sibling)

    def add_core(i, u, at):
        dxs[i, u, c, :, at] = (
            dxs[i, u, c, :, at].astype(F32) + dxr[i, u, :, at].astype(F32)
        ).astype(BF16)

    def add_core_whole(i, u):
        arrived(core_dx[i, u])

        def some(n, carry):
            add_core(i, u, cols(n, B))
            return carry

        lax.fori_loop(0, 4, some, 0)

    def block_rows(yb):
        return rows(32 * slot(mod4(yb)), 32)

    def along_z_grads(i, us):
        q = quarter[i]
        for u in us:
            add_core_whole(i, u)
            for d in (1, 3, 2):
                push(
                    dxs.at[i, u, c, block_rows(z + d - y), :], zr.at[q, u, d - 1], along_z[d],
                    zsem.at[q, u, d - 1],
                )

    from_yf, from_zy = {}, {}

    def along_y_grads():
        for u in (0, 1):
            add_core_whole(0, u)
        for d in (1, 3, 2):
            at = cols(mod4(y + d), B)
            from_yf[d] = push(dxs.at[0, :, c, :, at], yf.at[d - 1], along_y[d])

    def then_along_z():
        for d in (1, 3, 2):
            arrived(from_yf[d])
        for e in (1, 3, 2, 0):
            total = dxs[0, :, c, block_rows(z + e - y), cols(y, B)].astype(F32)
            for d in (1, 2, 3):
                total = total + yf[d - 1, :, block_rows(z + e - y + d), :].astype(F32)
            zs[e] = total.astype(BF16)
            if e:
                from_zy[e] = push(zs.at[e], zy.at[e - 1], along_z[e])

    def last_token_grads():
        core_last = {}
        deltas = turned(3, 1)
        for d in (2, 1, 3, 0):
            n = mod4(y + d)
            token_terms(3, 1, n, deltas)
            at = cols(n, B)
            core_last[d] = push(dxs.at[3, 1, 1 - c, :, at], dxr.at[3, 1, :, at], sibling)
        return core_last

    def last_along_z(core_last):
        for k, d in enumerate((2, 1, 3, 0)):
            at = cols(mod4(y + d), B)
            arrived(core_last[d])
            add_core(3, 1, at)
            for e in (1, 3, 2):
                push(
                    dxs.at[3, 1, c, block_rows(z + e - y), at],
                    zr.at[quarter[3], 1, e - 1, :, at], along_z[e], lastsem.at[k, e - 1],
                )

    whole, one, two = (0, 1), (0,), (1,)
    for b in (0, 1):
        relay(near, b, 0)
        relay(far, b, 0)
    arrived(core_outer[0], *core_piece[0, 0], *core_piece[0, 1])
    own_w.wait()
    arrived(*from_w[0])
    forward(0, whole, H0)
    arrived(core_outer[1], *core_piece[2, 0])
    forward(2, one, H0)
    arrived(*from_outer[1])
    core_outer.append(outer_to_sibling(1))
    arrived(core_outer[2], *core_piece[1, 0])
    forward(1, one, H0)
    relay(near, 0, 1)
    relay(far, 0, 1)
    arrived(*from_w[1])
    forward(0, whole, H1)
    forward(2, one, REST0)
    activate(0, whole, H0)
    relay(near, 1, 1)
    relay(far, 1, 1)
    activate(1, one, H0)
    arrived(*from_w[2])
    forward(0, whole, H2)
    forward(1, one, H12)
    arrived(*core_piece[1, 1])
    forward(1, two, ALL)
    arrived(*core_piece[2, 1])
    forward(2, two, D0)
    activate(0, whole, H1)
    weight_grads(0, H01)
    activate(2, one, H0)
    activate(2, one, REST0)
    activate(0, whole, H2)
    token_grads(0, whole)
    weight_grads(0, H2)
    along_y_grads()
    activate(1, one, H12)
    token_grads(1, one)
    for copy, which, b, u in onward:
        arrived(copy)
        to_sibling(3, u, which, b)
    arrived(*from_outer[3])
    core_outer.append(outer_to_sibling(3))
    along_z_grads(1, one)
    arrived(core_outer[3], *core_piece[3, 0], *core_piece[3, 1])
    forward(3, whole, D0)
    activate(1, two, ALL)
    token_grads(1, two)
    forward(2, one, D12)
    weight_grads(1, ALL)
    along_z_grads(1, two)
    activate(2, two, D0)
    weight_grads(2, D0)
    then_along_z()
    forward(3, one, D12)
    activate(3, whole, D0)
    last_weight_grads(3, D0)
    forward(2, two, D1)
    forward(3, two, D1)
    activate(2, one, D12)
    token_grads(2, one)
    forward(2, two, D2)
    forward(3, two, D2)
    along_z_grads(2, one)
    activate(3, one, D12)
    token_grads(3, one)
    activate(2, two, D1)
    along_z_grads(3, one)
    weight_grads(2, D1)
    activate(3, two, D1)
    last_weight_grads(3, D1)
    activate(2, two, D2)
    token_grads(2, two)
    activate(3, two, D2)
    along_z_grads(2, two)
    core_last = last_token_grads()
    weight_grads(2, D2)
    last_weight_grads(3, D2)
    last_along_z(core_last)

    def landed(ref, sem):
        pltpu.make_async_remote_copy(
            src_ref=ref, dst_ref=ref, send_sem=ssem.at[0], recv_sem=sem,
            device_id=along_z[1], device_id_type=MESH,
        ).wait_recv()

    def land(i, u):
        for d in (1, 2, 3):
            q = mod4(z - d + offs[i])
            landed(zr.at[q, u, d - 1], zsem.at[q, u, d - 1])

    keep = block_rows(z - y)
    from_x, from_yg = [], {}

    def over_x(u, at, own):
        for i in range(4):
            q = quarter[i]
            terms = [zr[q, u, e - 1, :, at] for e in (1, 2, 3) if (offs[i] + e) % 4]
            if i:
                terms.append(dxs[i, u, c, keep, at])
            if own:
                terms.append(zy[3 - offs[i], u] if i else zs[0, u])
            total = sum(term.astype(F32) for term in terms).astype(BF16)
            ys[0, q, half(u), :, at] = total[0:16]
            ys[1, q, half(u), :, at] = total[16:32]

    def first_over_x():
        for d in (1, 3, 2, 0):
            over_x(0, cols(mod4(y + d), B), d == 0)
        return push(ys.at[1 - x_hi, :, half(0)], xr.at[:, half(0)], across)

    def then_over_x(k, d):
        at = cols(mod4(y + d), B)
        for e in (1, 2, 3):
            landed(zr.at[mod4(z - e + 2), 1, e - 1, :, at], lastsem.at[k, e - 1])
        over_x(1, at, d == 0)
        from_x.append(
            push(ys.at[1 - x_hi, :, half(1), :, at], xr.at[:, half(1), :, at], across)
        )

    def over_y(k, d):
        at = cols(mod4(y + d), B)
        arrived(from_x[k])
        ys[x_hi, :, :, :, at] = (
            ys[x_hi, :, :, :, at].astype(F32) + xr[:, :, :, at].astype(F32)
        ).astype(BF16)
        if d:
            from_yg[d] = push(ys.at[x_hi, :, :, :, at], yr.at[d - 1], along_y[d])

    order = (2, 1, 3, 0)
    for i in (1, 2, 3):
        land(i, 0)
    arrived(*from_zy.values())
    from_first = first_over_x()
    land(1, 1)
    land(2, 1)
    then_over_x(0, order[0])
    arrived(from_first)
    for k in (1, 2, 3):
        then_over_x(k, order[k])
        over_y(k - 1, order[k - 1])
    over_y(3, order[3])
    for copy in own_dw:
        copy.wait()
    for span in GO:
        arrived(*from_dw[span])
    total = ys[x_hi, :, :, :, cols(y, B)].astype(F32)
    for d in (2, 1, 3):
        arrived(from_yg[d])
        total = total + yr[d - 1].astype(F32)
    dx[...] = total.astype(BF16).reshape(128, B)
    left(*sent)


def finish(back, down, dgate, dup, ddown):
    dgate[...] = back[0].astype(F32).T
    dup[...] = back[1].astype(F32).T
    ddown[...] = down[...].astype(F32)


def local(tokens, gate_weight, up_weight, down_weight, grad_out):
    flops = 8 * 2 * 2048 * 2048 * 256
    back, ddown, dx = pl.pallas_call(
        kernel,
        out_shape=(
            jax.ShapeDtypeStruct((2, 4 * Q, B), BF16),
            jax.ShapeDtypeStruct((4 * Q, B), BF16),
            jax.ShapeDtypeStruct((128, B), BF16),
        ),
        in_specs=[pl.BlockSpec(memory_space=pl.ANY)] * 5,
        out_specs=(
            pl.BlockSpec(memory_space=pl.ANY),
            pl.BlockSpec(memory_space=pl.ANY),
            pl.BlockSpec(memory_space=pltpu.VMEM),
        ),
        scratch_shapes=[
            pltpu.VMEM((2, 4, 2, 2, 4, 2, 16, DH), BF16),
            pltpu.VMEM((2, B, 4 * Q), BF16),
            pltpu.VMEM((3, 4 * Q, B), BF16),
            pltpu.VMEM((3, Q, DH), BF16),
            pltpu.VMEM((4, 2, 3, Q, 256), BF16),
            pltpu.VMEM((4, 2, 3, Q, 256), BF16),
            pltpu.VMEM((3, Q, DH), F32),
            pltpu.VMEM((4, 2, 2, 128, DH), BF16),
            pltpu.VMEM((4, 2, 128, DH), BF16),
            pltpu.VMEM((4, 2, 3, 32, DH), BF16),
            pltpu.VMEM((2, 4, 2, 16, DH), BF16),
            pltpu.VMEM((4, 2, 16, DH), BF16),
            pltpu.VMEM((3, 4, 2, 16, B), BF16),
            pltpu.VMEM((3, 2, 128, B), BF16),
            pltpu.VMEM((4, 2, 32, B), BF16),
            pltpu.VMEM((3, 2, 32, B), BF16),
            pltpu.SemaphoreType.DMA((224,)),
            pltpu.SemaphoreType.DMA((224,)),
            pltpu.SemaphoreType.DMA((24,)),
            pltpu.SemaphoreType.DMA((4, 2, 3)),
            pltpu.SemaphoreType.DMA((4, 3)),
        ],
        compiler_params=pltpu.CompilerParams(
            collective_id=0, has_side_effects=True, vmem_limit_bytes=62 * 2**20
        ),
        cost_estimate=pl.CostEstimate(flops=flops, bytes_accessed=2**24, transcendentals=2**20),
    )(
        tokens.reshape(2, 4, 2, 16, 4096), grad_out.reshape(2, 4, 2, 16, 4096),
        gate_weight, up_weight, down_weight,
    )
    grads = pl.pallas_call(
        finish,
        grid=(2,),
        out_shape=(
            jax.ShapeDtypeStruct((B, 4 * Q), F32),
            jax.ShapeDtypeStruct((B, 4 * Q), F32),
            jax.ShapeDtypeStruct((4 * Q, B), F32),
        ),
        in_specs=[
            pl.BlockSpec((2, 4 * Q, B // 2), lambda n: (0, 0, n)),
            pl.BlockSpec((2 * Q, B), lambda n: (n, 0)),
        ],
        out_specs=(
            pl.BlockSpec((B // 2, 4 * Q), lambda n: (n, 0)),
            pl.BlockSpec((B // 2, 4 * Q), lambda n: (n, 0)),
            pl.BlockSpec((2 * Q, B), lambda n: (n, 0)),
        ),
        compiler_params=pltpu.CompilerParams(vmem_limit_bytes=62 * 2**20),
        cost_estimate=pl.CostEstimate(flops=0, bytes_accessed=2**23, transcendentals=0),
    )(back, ddown)
    return (dx, *grads)


def solution(mesh):
    return jax.shard_map(
        local,
        mesh=mesh,
        in_specs=(
            P("grp", None),
            P("grp", "shard"),
            P("grp", "shard"),
            P("shard", "grp"),
            P("grp", None),
        ),
        out_specs=(P("shard", "grp"), P("grp", "shard"), P("grp", "shard"), P("shard", "grp")),
        check_vma=False,
    )
```

```python
import functools

import jax
import jax.numpy as jnp
from jax import lax
from jax.experimental import pallas as pl
from jax.experimental.pallas import tpu as pltpu
from jax.sharding import PartitionSpec as P

MESH = pl.DeviceIdType.MESH
BF16 = jnp.bfloat16
F32 = jnp.float32

Q = 224
DH = 2048
B = 512
CHUNK = 512
H0, H1, H2 = COME = ((0, 64), (64, 80), (144, 80))
D0, D1, D2 = GO = ((0, 96), (96, 64), (160, 64))
H01, D12, ALL = (0, 144), (96, 128), (0, Q)


def dot_nt(left, right):
    return lax.dot_general(left, right, (((1,), (1,)), ((), ())), preferred_element_type=F32)


def dot_nn(left, right):
    return lax.dot_general(left, right, (((1,), (0,)), ((), ())), preferred_element_type=F32)


def dot_tn(left, right):
    return lax.dot_general(left, right, (((0,), (0,)), ((), ())), preferred_element_type=F32)


def kernel(
    tok, grd, gate_w, up_w, down_w, back, ddown, dx,
    buf, raw, wt, wbuf, part, other, acc, dxs, dxr, zr, ys, xr, yr, yf, zs, zy,
    ssem, rsem, lsem, zsem, lastsem,
):
    grp, shard = lax.axis_index("grp"), lax.axis_index("shard")
    x_lo, y = lax.div(grp, 4), lax.rem(grp, 4)
    x_hi, z, c = lax.div(shard, 8), lax.rem(lax.div(shard, 2), 4), lax.rem(shard, 2)
    x = 2 * x_hi + x_lo

    def mod4(v):
        return lax.rem(v + 8, 4)

    def slot(dy):
        return dy + lax.div(dy, 2) * (1 - 2 * lax.rem(dy, 2))

    def device(x, y, z, c):
        return (4 * lax.rem(x, 2) + y, 8 * lax.div(x, 2) + 2 * z + c)

    sibling = device(x, y, z, 1 - c)
    inner = device(x + 1 - 2 * x_lo, y, z, c)
    outer = device(mod4(x - 1 + 2 * x_lo), y, z, c)
    across = device(mod4(x + 2), y, z, c)
    along_y = {d: device(x, mod4(y + d), z, c) for d in (1, 2, 3)}
    along_z = {d: device(x, y, mod4(z + d), c) for d in (1, 2, 3)}

    barrier = pltpu.get_barrier_semaphore()
    partners = [sibling, inner, outer, across, *along_y.values(), *along_z.values()]
    for partner in partners:
        pl.semaphore_signal(barrier, inc=1, device_id=partner, device_id_type=MESH)

    count = [0]
    sent = []

    def push(src, dst, target, recv=None):
        n = count[0]
        count[0] += 1
        copy = pltpu.make_async_remote_copy(
            src_ref=src, dst_ref=dst, send_sem=ssem.at[n],
            recv_sem=rsem.at[n] if recv is None else recv,
            device_id=target, device_id_type=MESH,
        )
        copy.start()
        sent.append(copy)
        return copy

    local_count = [0]

    def bring(src, dst):
        n = local_count[0]
        local_count[0] += 1
        copy = pltpu.make_async_copy(src, dst, lsem.at[n])
        copy.start()
        return copy

    def arrived(*copies):
        for copy in copies:
            copy.wait_recv()

    gone = set()

    def left(*copies):
        for copy in copies:
            if id(copy) not in gone:
                gone.add(id(copy))
                copy.wait_send()

    def rows(start, size, step=32):
        return pl.ds(pl.multiple_of(start, step), size)

    def cols(block, size):
        return pl.ds(pl.multiple_of(block * size, size), size)

    mine, theirs = cols(x_lo, DH), cols(1 - x_lo, DH)
    offs = (0, 1, 3, 2)
    quarter = [mod4(z + off) for off in offs]
    first, second = x_hi, 1 - x_hi

    def half(u):
        return first + u * (1 - 2 * first)

    own_tok = [
        bring(src.at[h, :, s, :, mine], buf.at[a, :, s, h, 0, x_lo])
        for s in (0, 1)
        for h in (0, 1)
        for a, src in enumerate((tok, grd))
    ]
    own_raw = [bring(gate_w, raw.at[0]), bring(up_w, raw.at[1]), bring(down_w, wt.at[2])]
    for copy in own_raw:
        copy.wait()
    for m in (0, 1):
        def turn(n, carry):
            wt[m, cols(n, 128), :] = raw[m, :, cols(n, 128)].T
            return carry

        lax.fori_loop(0, 7, turn, 0)
    own_w = bring(wt.at[:, rows(Q * y, Q), :], wbuf.at[:, :, cols(y, B)])
    for copy in own_tok:
        copy.wait()
    pl.semaphore_wait(barrier, len(partners))

    def send_outer(i, target):
        q = quarter[i]
        return [
            push(src.at[c, q, :, :, theirs], buf.at[a, q, :, c, 0, x_lo], target)
            for a, src in enumerate((tok, grd))
        ]

    from_outer = {0: send_outer(0, outer), 2: send_outer(2, inner)}

    blocks = (x_lo, 1 - x_lo)

    def send_y(d, b):
        n = {1: 2, 3: 1, 2: 3}[d]
        lo = blocks[b]
        return push(buf.at[:, z, first, c, 0, lo], buf.at[:, z, first, c, n, lo], along_y[d])

    def near(b, s, q):
        return buf.at[:, q, s, c, 1:3, blocks[b]]

    def far(b, s, q):
        return buf.at[:, q, s, c, 3:4, blocks[b]]

    core_piece = {(i, u): [] for i in range(4) for u in (0, 1)}

    def to_sibling(i, u, which, b):
        ref = which(b, half(u), quarter[i])
        core_piece[i, u].append(push(ref, ref, sibling))

    from_z, swaps = {}, {}

    def spread(which, b, u):
        ref = which(b, half(u), z)
        from_z[which, b, u] = push(ref, ref, along_z[1]), push(ref, ref, along_z[3])
        to_sibling(0, u, which, b)

    def swap(which, b):
        ref = which(b, first, z)
        swaps[which, b] = push(ref, ref, across)

    y_near, y_far = [send_y(1, 0), send_y(3, 0)], [send_y(2, 0)]
    arrived(*y_near)
    spread(near, 0, 0)
    arrived(*y_far)
    spread(far, 0, 0)
    arrived(*from_outer[0])
    y_near, y_far = [send_y(1, 1), send_y(3, 1)], [send_y(2, 1)]
    swap(near, 0)
    swap(far, 0)

    def send_w(h):
        start, size = COME[h]
        return [
            push(
                wt.at[:, rows(Q * mod4(y + d) + start, size, 16), :],
                wbuf.at[:, start : start + size, cols(y, B)],
                along_y[d],
            )
            for d in (1, 3, 2)
        ]

    from_w = [send_w(h) for h in range(len(COME))]

    def outer_to_sibling(i):
        ref = buf.at[:, quarter[i], :, c, 0, 1 - x_lo]
        return push(ref, ref, sibling)

    core_outer = [outer_to_sibling(0)]

    arrived(*y_near)
    swap(near, 1)
    spread(near, 1, 0)
    arrived(*y_far)
    swap(far, 1)
    spread(far, 1, 0)
    from_outer[1] = send_outer(1, outer)
    from_outer[3] = send_outer(3, outer)
    for b in (0, 1):
        for which in (near, far):
            arrived(swaps[which, b])
            spread(which, b, 1)
    arrived(*from_outer[2])
    core_outer.append(outer_to_sibling(2))

    onward = []

    def relay(which, b, u):
        up, down = from_z[which, b, u]
        arrived(up)
        if u == 0:
            ref = which(b, half(u), quarter[2])
            onward.append((push(ref, ref, along_z[1]), which, b, u))
        to_sibling(2, u, which, b)
        arrived(down)
        if u == 1:
            ref = which(b, half(u), quarter[1])
            onward.append((push(ref, ref, along_z[3]), which, b, u))
        to_sibling(1, u, which, b)

    exchange = {}

    def forward(i, us, span):
        q = quarter[i]
        start, size = span
        hidden = slice(start, start + size)

        def one(u, carry):
            s = half(u)
            part[i, u, 0:2, hidden, :] = dot_nt(
                wbuf[0:2, hidden, :].reshape(2 * size, DH), buf[0, q, s].reshape(256, DH)
            ).astype(BF16).reshape(2, size, 256)
            part[i, u, 2, hidden, :] = dot_nt(
                wbuf[2, hidden, :], buf[1, q, s].reshape(256, DH)
            ).astype(BF16)
            return carry

        lax.fori_loop(us[0], us[-1] + 1, one, 0)
        at = slice(us[0], us[-1] + 1)
        exchange[i, us, span] = push(
            part.at[i, at, :, hidden, :], other.at[i, at, :, hidden, :], inner
        )

    def activate(i, us, span):
        arrived(exchange[i, us, span])
        left(exchange[i, us, span])
        start, size = span
        pair = slice(us[0], us[-1] + 1)
        step = 16 if len(us) == 2 or size % 32 else 32

        def some(r, carry):
            at = rows(start + step * r, step, 16)

            def full(m):
                return part[i, pair, m, at, :].astype(F32) + other[i, pair, m, at, :].astype(F32)

            gate, up_pre, back_grad = full(0), full(1), full(2)
            s = jax.nn.sigmoid(gate)
            silu = gate * s
            part[i, pair, 0, at, :] = (
                back_grad * up_pre * s * (1.0 + gate * (1.0 - s))
            ).astype(BF16)
            part[i, pair, 1, at, :] = (back_grad * silu).astype(BF16)
            part[i, pair, 2, at, :] = (silu * up_pre).astype(BF16)
            return carry

        lax.fori_loop(0, size // step, some, 0)

    def weight_terms(i, span, n):
        q = quarter[i]
        start, size = span
        hidden = slice(start, start + size)
        at = cols(n, B)
        pair, third = 0.0, 0.0
        for u in (0, 1):
            pair = pair + dot_nn(
                part[i, u, 0:2, hidden, :].reshape(2 * size, 256),
                buf[0, q, half(u), :, :, :, :, at].reshape(256, B),
            )
            third = third + dot_nn(
                part[i, u, 2, hidden, :], buf[1, q, half(u), :, :, :, :, at].reshape(256, B)
            )
        return pair.reshape(2, size, B), third

    def weight_grads(i, span):
        start, size = span
        hidden = slice(start, start + size)

        def block(n, carry):
            pair, third = weight_terms(i, span, n)
            at = cols(n, B)
            if i:
                pair = pair + acc[0:2, hidden, at]
                third = third + acc[2, hidden, at]
            acc[0:2, hidden, at] = pair
            acc[2, hidden, at] = third
            return carry

        lax.fori_loop(0, 4, block, 0)

    from_dw, own_dw = {}, []

    def last_weight_grads(i, span):
        if span == D0:
            for copies in from_w:
                for copy in copies:
                    left(copy)
        start, size = span
        hidden = slice(start, start + size)
        from_dw[span] = []
        for d in (1, 3, 2, 0):
            n = mod4(y + d)
            pair, third = weight_terms(i, span, n)
            at = cols(n, B)
            held = rows(Q * n + start, size, 16)
            wt[0:2, held, :] = (pair + acc[0:2, hidden, at]).astype(BF16)
            wt[2, held, :] = (third + acc[2, hidden, at]).astype(BF16)
            there = rows(Q * y + start, size, 16)
            if d:
                from_dw[span].append(push(wt.at[0:2, held, :], back.at[:, there, :], along_y[d]))
                from_dw[span].append(push(wt.at[2, held, :], ddown.at[there, :], along_y[d]))
            else:
                own_dw.append(bring(wt.at[0:2, held, :], back.at[:, there, :]))
                own_dw.append(bring(wt.at[2, held, :], ddown.at[there, :]))

    def turned(i, u):
        return part[i, u, 0:2].reshape(2 * Q, 256).T

    def token_terms(i, u, n, deltas):
        at = cols(n, B)
        dxs[i, u, :, :, at] = dot_nn(
            deltas, wbuf[0:2, :, at].reshape(2 * Q, B)
        ).astype(BF16).reshape(2, 128, B)

    core_dx = {}

    def token_grads(i, us):
        for u in us:
            deltas = turned(i, u)

            def block(n, carry):
                token_terms(i, u, n, deltas)
                return carry

            lax.fori_loop(0, 4, block, 0)
            core_dx[i, u] = push(dxs.at[i, u, 1 - c], dxr.at[i, u], sibling)

    def add_core(i, u, at):
        dxs[i, u, c, :, at] = (
            dxs[i, u, c, :, at].astype(F32) + dxr[i, u, :, at].astype(F32)
        ).astype(BF16)

    def add_core_whole(i, u):
        arrived(core_dx[i, u])

        def some(n, carry):
            add_core(i, u, cols(n, B))
            return carry

        lax.fori_loop(0, 4, some, 0)

    def block_rows(yb):
        return rows(32 * slot(mod4(yb)), 32)

    def along_z_grads(i, us):
        q = quarter[i]
        for u in us:
            add_core_whole(i, u)
            for d in (1, 3, 2):
                push(
                    dxs.at[i, u, c, block_rows(z + d - y), :], zr.at[q, u, d - 1], along_z[d],
                    zsem.at[q, u, d - 1],
                )

    from_yf, from_zy = {}, {}

    def along_y_grads():
        for u in (0, 1):
            add_core_whole(0, u)
        for d in (1, 3, 2):
            at = cols(mod4(y + d), B)
            from_yf[d] = push(dxs.at[0, :, c, :, at], yf.at[d - 1], along_y[d])

    def then_along_z():
        for d in (1, 3, 2):
            arrived(from_yf[d])
        for e in (1, 3, 2, 0):
            total = dxs[0, :, c, block_rows(z + e - y), cols(y, B)].astype(F32)
            for d in (1, 2, 3):
                total = total + yf[d - 1, :, block_rows(z + e - y + d), :].astype(F32)
            zs[e] = total.astype(BF16)
            if e:
                from_zy[e] = push(zs.at[e], zy.at[e - 1], along_z[e])

    def last_token_grads():
        core_last = {}
        deltas = turned(3, 1)
        for d in (2, 1, 3, 0):
            n = mod4(y + d)
            token_terms(3, 1, n, deltas)
            at = cols(n, B)
            core_last[d] = push(dxs.at[3, 1, 1 - c, :, at], dxr.at[3, 1, :, at], sibling)
        return core_last

    def last_along_z(core_last):
        for k, d in enumerate((2, 1, 3, 0)):
            at = cols(mod4(y + d), B)
            arrived(core_last[d])
            add_core(3, 1, at)
            for e in (1, 3, 2):
                push(
                    dxs.at[3, 1, c, block_rows(z + e - y), at],
                    zr.at[quarter[3], 1, e - 1, :, at], along_z[e], lastsem.at[k, e - 1],
                )

    whole, one, two = (0, 1), (0,), (1,)
    own_w.wait()
    arrived(core_outer[0], *core_piece[0, 0])
    arrived(*from_w[0])
    forward(0, one, H0)
    arrived(*core_piece[0, 1])
    forward(0, two, H0)
    for b in (0, 1):
        relay(near, b, 0)
        relay(far, b, 0)
    arrived(core_outer[1], *core_piece[2, 0])
    forward(2, one, H0)
    arrived(*from_outer[1])
    core_outer.append(outer_to_sibling(1))
    arrived(core_outer[2], *core_piece[1, 0])
    forward(1, one, H0)
    relay(near, 0, 1)
    relay(far, 0, 1)
    arrived(*from_w[1])
    forward(0, whole, H1)
    forward(2, one, H1)
    forward(1, one, H1)
    activate(0, one, H0)
    activate(0, two, H0)
    relay(near, 1, 1)
    relay(far, 1, 1)
    activate(2, one, H0)
    activate(1, one, H0)
    arrived(*from_w[2])
    forward(0, whole, H2)
    forward(1, one, H2)
    arrived(*core_piece[1, 1])
    forward(1, two, ALL)
    arrived(*core_piece[2, 1])
    forward(2, two, D0)
    activate(0, whole, H1)
    weight_grads(0, H01)
    activate(2, one, H1)
    activate(1, one, H1)
    activate(0, whole, H2)
    token_grads(0, whole)
    weight_grads(0, H2)
    along_y_grads()
    activate(1, one, H2)
    token_grads(1, one)
    for copy, which, b, u in onward:
        arrived(copy)
        to_sibling(3, u, which, b)
    arrived(*from_outer[3])
    core_outer.append(outer_to_sibling(3))
    along_z_grads(1, one)
    arrived(core_outer[3], *core_piece[3, 0], *core_piece[3, 1])
    forward(3, whole, D0)
    activate(1, two, ALL)
    token_grads(1, two)
    forward(2, one, H2)
    weight_grads(1, ALL)
    along_z_grads(1, two)
    activate(2, two, D0)
    weight_grads(2, D0)
    then_along_z()
    forward(3, one, D12)
    activate(3, whole, D0)
    last_weight_grads(3, D0)
    forward(2, two, D1)
    activate(2, one, H2)
    token_grads(2, one)
    forward(3, two, D1)
    along_z_grads(2, one)
    forward(2, two, D2)
    forward(3, two, D2)
    activate(3, one, D12)
    token_grads(3, one)
    activate(2, two, D1)
    along_z_grads(3, one)
    weight_grads(2, D1)
    activate(3, two, D1)
    last_weight_grads(3, D1)
    activate(2, two, D2)
    token_grads(2, two)
    activate(3, two, D2)
    along_z_grads(2, two)
    core_last = last_token_grads()
    weight_grads(2, D2)
    last_weight_grads(3, D2)
    last_along_z(core_last)

    def landed(ref, sem):
        pltpu.make_async_remote_copy(
            src_ref=ref, dst_ref=ref, send_sem=ssem.at[0], recv_sem=sem,
            device_id=along_z[1], device_id_type=MESH,
        ).wait_recv()

    def land(i, u):
        for d in (1, 2, 3):
            q = mod4(z - d + offs[i])
            landed(zr.at[q, u, d - 1], zsem.at[q, u, d - 1])

    keep = block_rows(z - y)
    from_x, from_yg = [], {}

    def over_x(u, at, own):
        for i in range(4):
            q = quarter[i]
            terms = [zr[q, u, e - 1, :, at] for e in (1, 2, 3) if (offs[i] + e) % 4]
            if i:
                terms.append(dxs[i, u, c, keep, at])
            if own:
                terms.append(zy[3 - offs[i], u] if i else zs[0, u])
            total = sum(term.astype(F32) for term in terms).astype(BF16)
            ys[0, q, half(u), :, at] = total[0:16]
            ys[1, q, half(u), :, at] = total[16:32]

    def first_over_x():
        for d in (1, 3, 2, 0):
            over_x(0, cols(mod4(y + d), B), d == 0)
        return push(ys.at[1 - x_hi, :, half(0)], xr.at[:, half(0)], across)

    def then_over_x(k, d):
        at = cols(mod4(y + d), B)
        for e in (1, 2, 3):
            landed(zr.at[mod4(z - e + 2), 1, e - 1, :, at], lastsem.at[k, e - 1])
        over_x(1, at, d == 0)
        from_x.append(
            push(ys.at[1 - x_hi, :, half(1), :, at], xr.at[:, half(1), :, at], across)
        )

    def over_y(k, d):
        at = cols(mod4(y + d), B)
        arrived(from_x[k])
        ys[x_hi, :, :, :, at] = (
            ys[x_hi, :, :, :, at].astype(F32) + xr[:, :, :, at].astype(F32)
        ).astype(BF16)
        if d:
            from_yg[d] = push(ys.at[x_hi, :, :, :, at], yr.at[d - 1], along_y[d])

    order = (2, 1, 3, 0)
    for i in (1, 2, 3):
        land(i, 0)
    arrived(*from_zy.values())
    from_first = first_over_x()
    land(1, 1)
    land(2, 1)
    then_over_x(0, order[0])
    arrived(from_first)
    for k in (1, 2, 3):
        then_over_x(k, order[k])
        over_y(k - 1, order[k - 1])
    over_y(3, order[3])
    for copy in own_dw:
        copy.wait()
    for span in GO:
        arrived(*from_dw[span])
    total = ys[x_hi, :, :, :, cols(y, B)].astype(F32)
    for d in (2, 1, 3):
        arrived(from_yg[d])
        total = total + yr[d - 1].astype(F32)
    dx[...] = total.astype(BF16).reshape(128, B)
    left(*sent)


def finish(back, down, tokens, dgate, dup, ddown, dx):
    dx[...] = tokens[...]
    dgate[...] = back[0].astype(F32).T
    dup[...] = back[1].astype(F32).T
    ddown[...] = down[...].astype(F32)


def local(tokens, gate_weight, up_weight, down_weight, grad_out):
    flops = 8 * 2 * 2048 * 2048 * 256
    back, ddown, dx = pl.pallas_call(
        kernel,
        out_shape=(
            jax.ShapeDtypeStruct((2, 4 * Q, B), BF16),
            jax.ShapeDtypeStruct((4 * Q, B), BF16),
            jax.ShapeDtypeStruct((128, B), BF16),
        ),
        in_specs=[pl.BlockSpec(memory_space=pl.ANY)] * 5,
        out_specs=(
            pl.BlockSpec(memory_space=pl.ANY),
            pl.BlockSpec(memory_space=pl.ANY),
            pl.BlockSpec(memory_space=pltpu.VMEM),
        ),
        scratch_shapes=[
            pltpu.VMEM((2, 4, 2, 2, 4, 2, 16, DH), BF16),
            pltpu.VMEM((2, B, 4 * Q), BF16),
            pltpu.VMEM((3, 4 * Q, B), BF16),
            pltpu.VMEM((3, Q, DH), BF16),
            pltpu.VMEM((4, 2, 3, Q, 256), BF16),
            pltpu.VMEM((4, 2, 3, Q, 256), BF16),
            pltpu.VMEM((3, Q, DH), F32),
            pltpu.VMEM((4, 2, 2, 128, DH), BF16),
            pltpu.VMEM((4, 2, 128, DH), BF16),
            pltpu.VMEM((4, 2, 3, 32, DH), BF16),
            pltpu.VMEM((2, 4, 2, 16, DH), BF16),
            pltpu.VMEM((4, 2, 16, DH), BF16),
            pltpu.VMEM((3, 4, 2, 16, B), BF16),
            pltpu.VMEM((3, 2, 128, B), BF16),
            pltpu.VMEM((4, 2, 32, B), BF16),
            pltpu.VMEM((3, 2, 32, B), BF16),
            pltpu.SemaphoreType.DMA((224,)),
            pltpu.SemaphoreType.DMA((224,)),
            pltpu.SemaphoreType.DMA((24,)),
            pltpu.SemaphoreType.DMA((4, 2, 3)),
            pltpu.SemaphoreType.DMA((4, 3)),
        ],
        compiler_params=pltpu.CompilerParams(
            collective_id=0, has_side_effects=True, vmem_limit_bytes=62 * 2**20
        ),
        cost_estimate=pl.CostEstimate(flops=flops, bytes_accessed=2**24, transcendentals=2**20),
    )(
        tokens.reshape(2, 4, 2, 16, 4096), grad_out.reshape(2, 4, 2, 16, 4096),
        gate_weight, up_weight, down_weight,
    )
    grads = pl.pallas_call(
        finish,
        grid=(2,),
        out_shape=(
            jax.ShapeDtypeStruct((B, 4 * Q), F32),
            jax.ShapeDtypeStruct((B, 4 * Q), F32),
            jax.ShapeDtypeStruct((4 * Q, B), F32),
            jax.ShapeDtypeStruct((128, B), BF16),
        ),
        in_specs=[
            pl.BlockSpec((2, 4 * Q, B // 2), lambda n: (0, 0, n)),
            pl.BlockSpec((2 * Q, B), lambda n: (n, 0)),
            pl.BlockSpec((64, B), lambda n: (n, 0)),
        ],
        out_specs=(
            pl.BlockSpec((B // 2, 4 * Q), lambda n: (n, 0)),
            pl.BlockSpec((B // 2, 4 * Q), lambda n: (n, 0)),
            pl.BlockSpec((2 * Q, B), lambda n: (n, 0)),
            pl.BlockSpec((64, B), lambda n: (n, 0)),
        ),
        compiler_params=pltpu.CompilerParams(vmem_limit_bytes=62 * 2**20),
        cost_estimate=pl.CostEstimate(flops=0, bytes_accessed=2**23, transcendentals=0),
    )(back, ddown, dx)
    return (grads[3], *grads[:3])


def solution(mesh):
    return jax.shard_map(
        local,
        mesh=mesh,
        in_specs=(
            P("grp", None),
            P("grp", "shard"),
            P("grp", "shard"),
            P("shard", "grp"),
            P("grp", None),
        ),
        out_specs=(P("shard", "grp"), P("grp", "shard"), P("grp", "shard"), P("shard", "grp")),
        check_vma=False,
    )
```

```python
import functools

import jax
import jax.numpy as jnp
from jax import lax
from jax.experimental import pallas as pl
from jax.experimental.pallas import tpu as pltpu
from jax.sharding import PartitionSpec as P

MESH = pl.DeviceIdType.MESH
BF16 = jnp.bfloat16
F32 = jnp.float32

Q = 224
DH = 2048
B = 512
CHUNK = 512
H0, H1, H2 = COME = ((0, 64), (64, 80), (144, 80))
D0, D1, D2 = GO = ((0, 96), (96, 64), (160, 64))
H01, D12, ALL = (0, 144), (96, 128), (0, Q)


def dot_nt(left, right):
    return lax.dot_general(left, right, (((1,), (1,)), ((), ())), preferred_element_type=F32)


def dot_nn(left, right):
    return lax.dot_general(left, right, (((1,), (0,)), ((), ())), preferred_element_type=F32)


def dot_tn(left, right):
    return lax.dot_general(left, right, (((0,), (0,)), ((), ())), preferred_element_type=F32)


def kernel(
    tok, grd, gate_w, up_w, down_w, back, ddown, dx,
    buf, raw, wt, wbuf, part, other, acc, dxs, dxr, zr, ys, xr, yr, yf, zs, zy,
    ssem, rsem, lsem, zsem, lastsem,
):
    grp, shard = lax.axis_index("grp"), lax.axis_index("shard")
    x_lo, y = lax.div(grp, 4), lax.rem(grp, 4)
    x_hi, z, c = lax.div(shard, 8), lax.rem(lax.div(shard, 2), 4), lax.rem(shard, 2)
    x = 2 * x_hi + x_lo

    def mod4(v):
        return lax.rem(v + 8, 4)

    def slot(dy):
        return dy + lax.div(dy, 2) * (1 - 2 * lax.rem(dy, 2))

    def device(x, y, z, c):
        return (4 * lax.rem(x, 2) + y, 8 * lax.div(x, 2) + 2 * z + c)

    sibling = device(x, y, z, 1 - c)
    inner = device(x + 1 - 2 * x_lo, y, z, c)
    outer = device(mod4(x - 1 + 2 * x_lo), y, z, c)
    across = device(mod4(x + 2), y, z, c)
    along_y = {d: device(x, mod4(y + d), z, c) for d in (1, 2, 3)}
    along_z = {d: device(x, y, mod4(z + d), c) for d in (1, 2, 3)}

    barrier = pltpu.get_barrier_semaphore()
    partners = [sibling, inner, outer, across, *along_y.values(), *along_z.values()]
    for partner in partners:
        pl.semaphore_signal(barrier, inc=1, device_id=partner, device_id_type=MESH)

    count = [0]
    sent = []

    def push(src, dst, target, recv=None):
        n = count[0]
        count[0] += 1
        copy = pltpu.make_async_remote_copy(
            src_ref=src, dst_ref=dst, send_sem=ssem.at[n],
            recv_sem=rsem.at[n] if recv is None else recv,
            device_id=target, device_id_type=MESH,
        )
        copy.start()
        sent.append(copy)
        return copy

    local_count = [0]

    def bring(src, dst):
        n = local_count[0]
        local_count[0] += 1
        copy = pltpu.make_async_copy(src, dst, lsem.at[n])
        copy.start()
        return copy

    def arrived(*copies):
        for copy in copies:
            copy.wait_recv()

    gone = set()

    def left(*copies):
        for copy in copies:
            if id(copy) not in gone:
                gone.add(id(copy))
                copy.wait_send()

    def rows(start, size, step=32):
        return pl.ds(pl.multiple_of(start, step), size)

    def cols(block, size):
        return pl.ds(pl.multiple_of(block * size, size), size)

    mine, theirs = cols(x_lo, DH), cols(1 - x_lo, DH)
    offs = (0, 1, 3, 2)
    quarter = [mod4(z + off) for off in offs]
    first, second = x_hi, 1 - x_hi

    def half(u):
        return first + u * (1 - 2 * first)

    own_tok = [
        bring(src.at[h, :, s, :, mine], buf.at[a, :, s, h, 0, x_lo])
        for s in (0, 1)
        for h in (0, 1)
        for a, src in enumerate((tok, grd))
    ]
    own_raw = [bring(gate_w, raw.at[0]), bring(up_w, raw.at[1]), bring(down_w, wt.at[2])]
    pl.semaphore_wait(barrier, len(partners))

    def send_outer(i, target):
        q = quarter[i]
        return [
            push(src.at[c, q, :, :, theirs], buf.at[a, q, :, c, 0, x_lo], target)
            for a, src in enumerate((tok, grd))
        ]

    from_outer = {0: send_outer(0, outer), 2: send_outer(2, inner)}

    blocks = (x_lo, 1 - x_lo)

    def send_y(d, b):
        n = {1: 2, 3: 1, 2: 3}[d]
        lo = blocks[b]
        return push(buf.at[:, z, first, c, 0, lo], buf.at[:, z, first, c, n, lo], along_y[d])

    def near(b, s, q):
        return buf.at[:, q, s, c, 1:3, blocks[b]]

    def far(b, s, q):
        return buf.at[:, q, s, c, 3:4, blocks[b]]

    core_piece = {(i, u): [] for i in range(4) for u in (0, 1)}

    def to_sibling(i, u, which, b):
        ref = which(b, half(u), quarter[i])
        core_piece[i, u].append(push(ref, ref, sibling))

    from_z, swaps = {}, {}

    def spread(which, b, u):
        ref = which(b, half(u), z)
        from_z[which, b, u] = push(ref, ref, along_z[1]), push(ref, ref, along_z[3])
        to_sibling(0, u, which, b)

    def swap(which, b):
        ref = which(b, first, z)
        swaps[which, b] = push(ref, ref, across)

    for copy in own_tok:
        copy.wait()
    y_near, y_far = [send_y(1, 0), send_y(3, 0)], [send_y(2, 0)]
    for copy in own_raw:
        copy.wait()
    for m in (0, 1):
        def turn(n, carry):
            wt[m, cols(n, 128), :] = raw[m, :, cols(n, 128)].T
            return carry

        lax.fori_loop(0, 7, turn, 0)
    own_w = bring(wt.at[:, rows(Q * y, Q), :], wbuf.at[:, :, cols(y, B)])
    arrived(*y_near)
    spread(near, 0, 0)
    arrived(*y_far)
    spread(far, 0, 0)
    arrived(*from_outer[0])
    y_near, y_far = [send_y(1, 1), send_y(3, 1)], [send_y(2, 1)]
    swap(near, 0)
    swap(far, 0)

    def send_w(h):
        start, size = COME[h]
        return [
            push(
                wt.at[:, rows(Q * mod4(y + d) + start, size, 16), :],
                wbuf.at[:, start : start + size, cols(y, B)],
                along_y[d],
            )
            for d in (1, 3, 2)
        ]

    from_w = [send_w(h) for h in range(len(COME))]

    def outer_to_sibling(i):
        ref = buf.at[:, quarter[i], :, c, 0, 1 - x_lo]
        return push(ref, ref, sibling)

    core_outer = [outer_to_sibling(0)]

    arrived(*y_near)
    swap(near, 1)
    spread(near, 1, 0)
    arrived(*y_far)
    swap(far, 1)
    spread(far, 1, 0)
    from_outer[1] = send_outer(1, outer)
    from_outer[3] = send_outer(3, outer)
    for b in (0, 1):
        for which in (near, far):
            arrived(swaps[which, b])
            spread(which, b, 1)
    arrived(*from_outer[2])
    core_outer.append(outer_to_sibling(2))

    onward = []

    def relay(which, b, u):
        up, down = from_z[which, b, u]
        arrived(up)
        if u == 0:
            ref = which(b, half(u), quarter[2])
            onward.append((push(ref, ref, along_z[1]), which, b, u))
        to_sibling(2, u, which, b)
        arrived(down)
        if u == 1:
            ref = which(b, half(u), quarter[1])
            onward.append((push(ref, ref, along_z[3]), which, b, u))
        to_sibling(1, u, which, b)

    exchange = {}

    def forward(i, us, span):
        q = quarter[i]
        start, size = span
        hidden = slice(start, start + size)

        def one(u, carry):
            s = half(u)
            part[i, u, 0:2, hidden, :] = dot_nt(
                wbuf[0:2, hidden, :].reshape(2 * size, DH), buf[0, q, s].reshape(256, DH)
            ).astype(BF16).reshape(2, size, 256)
            part[i, u, 2, hidden, :] = dot_nt(
                wbuf[2, hidden, :], buf[1, q, s].reshape(256, DH)
            ).astype(BF16)
            return carry

        lax.fori_loop(us[0], us[-1] + 1, one, 0)
        at = slice(us[0], us[-1] + 1)
        exchange[i, us, span] = push(
            part.at[i, at, :, hidden, :], other.at[i, at, :, hidden, :], inner
        )

    def activate(i, us, span):
        arrived(exchange[i, us, span])
        left(exchange[i, us, span])
        start, size = span
        pair = slice(us[0], us[-1] + 1)
        step = 16 if len(us) == 2 or size % 32 else 32

        def some(r, carry):
            at = rows(start + step * r, step, 16)

            def full(m):
                return part[i, pair, m, at, :].astype(F32) + other[i, pair, m, at, :].astype(F32)

            gate, up_pre, back_grad = full(0), full(1), full(2)
            s = jax.nn.sigmoid(gate)
            silu = gate * s
            part[i, pair, 0, at, :] = (
                back_grad * up_pre * s * (1.0 + gate * (1.0 - s))
            ).astype(BF16)
            part[i, pair, 1, at, :] = (back_grad * silu).astype(BF16)
            part[i, pair, 2, at, :] = (silu * up_pre).astype(BF16)
            return carry

        lax.fori_loop(0, size // step, some, 0)

    def weight_terms(i, span, n):
        q = quarter[i]
        start, size = span
        hidden = slice(start, start + size)
        at = cols(n, B)
        pair, third = 0.0, 0.0
        for u in (0, 1):
            pair = pair + dot_nn(
                part[i, u, 0:2, hidden, :].reshape(2 * size, 256),
                buf[0, q, half(u), :, :, :, :, at].reshape(256, B),
            )
            third = third + dot_nn(
                part[i, u, 2, hidden, :], buf[1, q, half(u), :, :, :, :, at].reshape(256, B)
            )
        return pair.reshape(2, size, B), third

    def weight_grads(i, span):
        start, size = span
        hidden = slice(start, start + size)

        def block(n, carry):
            pair, third = weight_terms(i, span, n)
            at = cols(n, B)
            if i:
                pair = pair + acc[0:2, hidden, at]
                third = third + acc[2, hidden, at]
            acc[0:2, hidden, at] = pair
            acc[2, hidden, at] = third
            return carry

        lax.fori_loop(0, 4, block, 0)

    from_dw, own_dw = {}, []

    def last_weight_grads(i, span):
        if span == D0:
            for copies in from_w:
                for copy in copies:
                    left(copy)
        start, size = span
        hidden = slice(start, start + size)
        from_dw[span] = []
        for d in (1, 3, 2, 0):
            n = mod4(y + d)
            pair, third = weight_terms(i, span, n)
            at = cols(n, B)
            held = rows(Q * n + start, size, 16)
            wt[0:2, held, :] = (pair + acc[0:2, hidden, at]).astype(BF16)
            wt[2, held, :] = (third + acc[2, hidden, at]).astype(BF16)
            there = rows(Q * y + start, size, 16)
            if d:
                from_dw[span].append(push(wt.at[0:2, held, :], back.at[:, there, :], along_y[d]))
                from_dw[span].append(push(wt.at[2, held, :], ddown.at[there, :], along_y[d]))
            else:
                own_dw.append(bring(wt.at[0:2, held, :], back.at[:, there, :]))
                own_dw.append(bring(wt.at[2, held, :], ddown.at[there, :]))

    def turned(i, u):
        return part[i, u, 0:2].reshape(2 * Q, 256).T

    def token_terms(i, u, n, deltas):
        at = cols(n, B)
        dxs[i, u, :, :, at] = dot_nn(
            deltas, wbuf[0:2, :, at].reshape(2 * Q, B)
        ).astype(BF16).reshape(2, 128, B)

    core_dx = {}

    def token_grads(i, us):
        for u in us:
            deltas = turned(i, u)

            def block(n, carry):
                token_terms(i, u, n, deltas)
                return carry

            lax.fori_loop(0, 4, block, 0)
            core_dx[i, u] = push(dxs.at[i, u, 1 - c], dxr.at[i, u], sibling)

    def add_core(i, u, at):
        dxs[i, u, c, :, at] = (
            dxs[i, u, c, :, at].astype(F32) + dxr[i, u, :, at].astype(F32)
        ).astype(BF16)

    def add_core_whole(i, u):
        arrived(core_dx[i, u])

        def some(n, carry):
            add_core(i, u, cols(n, B))
            return carry

        lax.fori_loop(0, 4, some, 0)

    def block_rows(yb):
        return rows(32 * slot(mod4(yb)), 32)

    def along_z_grads(i, us):
        q = quarter[i]
        for u in us:
            add_core_whole(i, u)
            for d in (1, 3, 2):
                push(
                    dxs.at[i, u, c, block_rows(z + d - y), :], zr.at[q, u, d - 1], along_z[d],
                    zsem.at[q, u, d - 1],
                )

    from_yf, from_zy = {}, {}

    def along_y_grads():
        for u in (0, 1):
            add_core_whole(0, u)
        for d in (1, 3, 2):
            at = cols(mod4(y + d), B)
            from_yf[d] = push(dxs.at[0, :, c, :, at], yf.at[d - 1], along_y[d])

    def then_along_z():
        for d in (1, 3, 2):
            arrived(from_yf[d])
        for e in (1, 3, 2, 0):
            total = dxs[0, :, c, block_rows(z + e - y), cols(y, B)].astype(F32)
            for d in (1, 2, 3):
                total = total + yf[d - 1, :, block_rows(z + e - y + d), :].astype(F32)
            zs[e] = total.astype(BF16)
            if e:
                from_zy[e] = push(zs.at[e], zy.at[e - 1], along_z[e])

    def last_token_grads():
        core_last = {}
        deltas = turned(3, 1)
        for d in (2, 1, 3, 0):
            n = mod4(y + d)
            token_terms(3, 1, n, deltas)
            at = cols(n, B)
            core_last[d] = push(dxs.at[3, 1, 1 - c, :, at], dxr.at[3, 1, :, at], sibling)
        return core_last

    def last_along_z(core_last):
        for k, d in enumerate((2, 1, 3, 0)):
            at = cols(mod4(y + d), B)
            arrived(core_last[d])
            add_core(3, 1, at)
            for e in (1, 3, 2):
                push(
                    dxs.at[3, 1, c, block_rows(z + e - y), at],
                    zr.at[quarter[3], 1, e - 1, :, at], along_z[e], lastsem.at[k, e - 1],
                )

    whole, one, two = (0, 1), (0,), (1,)
    own_w.wait()
    arrived(core_outer[0], *core_piece[0, 0])
    arrived(*from_w[0])
    forward(0, one, H0)
    arrived(*core_piece[0, 1])
    forward(0, two, H0)
    for b in (0, 1):
        relay(near, b, 0)
        relay(far, b, 0)
    arrived(core_outer[1], *core_piece[2, 0])
    forward(2, one, H0)
    arrived(*from_outer[1])
    core_outer.append(outer_to_sibling(1))
    arrived(core_outer[2], *core_piece[1, 0])
    forward(1, one, H0)
    relay(near, 0, 1)
    relay(far, 0, 1)
    arrived(*from_w[1])
    forward(0, whole, H1)
    forward(2, one, H1)
    forward(1, one, H1)
    activate(0, one, H0)
    activate(0, two, H0)
    relay(near, 1, 1)
    relay(far, 1, 1)
    activate(2, one, H0)
    activate(1, one, H0)
    arrived(*from_w[2])
    forward(0, whole, H2)
    forward(1, one, H2)
    arrived(*core_piece[1, 1])
    forward(1, two, ALL)
    arrived(*core_piece[2, 1])
    forward(2, two, D0)
    activate(0, whole, H1)
    weight_grads(0, H01)
    activate(2, one, H1)
    activate(1, one, H1)
    activate(0, whole, H2)
    token_grads(0, whole)
    weight_grads(0, H2)
    along_y_grads()
    activate(1, one, H2)
    token_grads(1, one)
    for copy, which, b, u in onward:
        arrived(copy)
        to_sibling(3, u, which, b)
    arrived(*from_outer[3])
    core_outer.append(outer_to_sibling(3))
    along_z_grads(1, one)
    arrived(core_outer[3], *core_piece[3, 0], *core_piece[3, 1])
    forward(3, whole, D0)
    activate(1, two, ALL)
    token_grads(1, two)
    forward(2, one, H2)
    along_z_grads(1, two)
    weight_grads(1, ALL)
    activate(2, two, D0)
    weight_grads(2, D0)
    then_along_z()
    forward(3, one, D12)
    activate(3, whole, D0)
    last_weight_grads(3, D0)
    forward(2, two, D1)
    activate(2, one, H2)
    token_grads(2, one)
    forward(3, two, D1)
    along_z_grads(2, one)
    forward(2, two, D2)
    forward(3, two, D2)
    activate(3, one, D12)
    token_grads(3, one)
    activate(2, two, D1)
    along_z_grads(3, one)
    weight_grads(2, D1)
    activate(3, two, D1)
    last_weight_grads(3, D1)
    activate(2, two, D2)
    token_grads(2, two)
    activate(3, two, D2)
    along_z_grads(2, two)
    core_last = last_token_grads()
    weight_grads(2, D2)
    last_weight_grads(3, D2)
    last_along_z(core_last)

    def landed(ref, sem):
        pltpu.make_async_remote_copy(
            src_ref=ref, dst_ref=ref, send_sem=ssem.at[0], recv_sem=sem,
            device_id=along_z[1], device_id_type=MESH,
        ).wait_recv()

    def land(i, u):
        for d in (1, 2, 3):
            q = mod4(z - d + offs[i])
            landed(zr.at[q, u, d - 1], zsem.at[q, u, d - 1])

    keep = block_rows(z - y)
    from_x, from_yg = [], {}

    def over_x(u, at, own):
        for i in range(4):
            q = quarter[i]
            terms = [zr[q, u, e - 1, :, at] for e in (1, 2, 3) if (offs[i] + e) % 4]
            if i:
                terms.append(dxs[i, u, c, keep, at])
            if own:
                terms.append(zy[3 - offs[i], u] if i else zs[0, u])
            total = sum(term.astype(F32) for term in terms).astype(BF16)
            ys[0, q, half(u), :, at] = total[0:16]
            ys[1, q, half(u), :, at] = total[16:32]

    def first_over_x():
        for d in (1, 3, 2, 0):
            over_x(0, cols(mod4(y + d), B), d == 0)
        return push(ys.at[1 - x_hi, :, half(0)], xr.at[:, half(0)], across)

    def then_over_x(k, d):
        at = cols(mod4(y + d), B)
        for e in (1, 2, 3):
            landed(zr.at[mod4(z - e + 2), 1, e - 1, :, at], lastsem.at[k, e - 1])
        over_x(1, at, d == 0)
        from_x.append(
            push(ys.at[1 - x_hi, :, half(1), :, at], xr.at[:, half(1), :, at], across)
        )

    def over_y(k, d):
        at = cols(mod4(y + d), B)
        arrived(from_x[k])
        ys[x_hi, :, :, :, at] = (
            ys[x_hi, :, :, :, at].astype(F32) + xr[:, :, :, at].astype(F32)
        ).astype(BF16)
        if d:
            from_yg[d] = push(ys.at[x_hi, :, :, :, at], yr.at[d - 1], along_y[d])

    order = (2, 1, 3, 0)
    for i in (1, 2, 3):
        land(i, 0)
    arrived(*from_zy.values())
    from_first = first_over_x()
    land(1, 1)
    land(2, 1)
    then_over_x(0, order[0])
    arrived(from_first)
    for k in (1, 2, 3):
        then_over_x(k, order[k])
        over_y(k - 1, order[k - 1])
    over_y(3, order[3])
    for copy in own_dw:
        copy.wait()
    for span in GO:
        arrived(*from_dw[span])
    total = ys[x_hi, :, :, :, cols(y, B)].astype(F32)
    for d in (2, 1, 3):
        arrived(from_yg[d])
        total = total + yr[d - 1].astype(F32)
    dx[...] = total.astype(BF16).reshape(128, B)
    left(*sent)


def finish(back, down, tokens, dgate, dup, ddown, dx):
    dx[...] = tokens[...]
    dgate[...] = back[0].astype(F32).T
    dup[...] = back[1].astype(F32).T
    ddown[...] = down[...].astype(F32)


def local(tokens, gate_weight, up_weight, down_weight, grad_out):
    flops = 8 * 2 * 2048 * 2048 * 256
    back, ddown, dx = pl.pallas_call(
        kernel,
        out_shape=(
            jax.ShapeDtypeStruct((2, 4 * Q, B), BF16),
            jax.ShapeDtypeStruct((4 * Q, B), BF16),
            jax.ShapeDtypeStruct((128, B), BF16),
        ),
        in_specs=[pl.BlockSpec(memory_space=pl.ANY)] * 5,
        out_specs=(
            pl.BlockSpec(memory_space=pl.ANY),
            pl.BlockSpec(memory_space=pl.ANY),
            pl.BlockSpec(memory_space=pltpu.VMEM),
        ),
        scratch_shapes=[
            pltpu.VMEM((2, 4, 2, 2, 4, 2, 16, DH), BF16),
            pltpu.VMEM((2, B, 4 * Q), BF16),
            pltpu.VMEM((3, 4 * Q, B), BF16),
            pltpu.VMEM((3, Q, DH), BF16),
            pltpu.VMEM((4, 2, 3, Q, 256), BF16),
            pltpu.VMEM((4, 2, 3, Q, 256), BF16),
            pltpu.VMEM((3, Q, DH), F32),
            pltpu.VMEM((4, 2, 2, 128, DH), BF16),
            pltpu.VMEM((4, 2, 128, DH), BF16),
            pltpu.VMEM((4, 2, 3, 32, DH), BF16),
            pltpu.VMEM((2, 4, 2, 16, DH), BF16),
            pltpu.VMEM((4, 2, 16, DH), BF16),
            pltpu.VMEM((3, 4, 2, 16, B), BF16),
            pltpu.VMEM((3, 2, 128, B), BF16),
            pltpu.VMEM((4, 2, 32, B), BF16),
            pltpu.VMEM((3, 2, 32, B), BF16),
            pltpu.SemaphoreType.DMA((224,)),
            pltpu.SemaphoreType.DMA((224,)),
            pltpu.SemaphoreType.DMA((24,)),
            pltpu.SemaphoreType.DMA((4, 2, 3)),
            pltpu.SemaphoreType.DMA((4, 3)),
        ],
        compiler_params=pltpu.CompilerParams(
            collective_id=0, has_side_effects=True, vmem_limit_bytes=62 * 2**20
        ),
        cost_estimate=pl.CostEstimate(flops=flops, bytes_accessed=2**24, transcendentals=2**20),
    )(
        tokens.reshape(2, 4, 2, 16, 4096), grad_out.reshape(2, 4, 2, 16, 4096),
        gate_weight, up_weight, down_weight,
    )
    grads = pl.pallas_call(
        finish,
        grid=(2,),
        out_shape=(
            jax.ShapeDtypeStruct((B, 4 * Q), F32),
            jax.ShapeDtypeStruct((B, 4 * Q), F32),
            jax.ShapeDtypeStruct((4 * Q, B), F32),
            jax.ShapeDtypeStruct((128, B), BF16),
        ),
        in_specs=[
            pl.BlockSpec((2, 4 * Q, B // 2), lambda n: (0, 0, n)),
            pl.BlockSpec((2 * Q, B), lambda n: (n, 0)),
            pl.BlockSpec((64, B), lambda n: (n, 0)),
        ],
        out_specs=(
            pl.BlockSpec((B // 2, 4 * Q), lambda n: (n, 0)),
            pl.BlockSpec((B // 2, 4 * Q), lambda n: (n, 0)),
            pl.BlockSpec((2 * Q, B), lambda n: (n, 0)),
            pl.BlockSpec((64, B), lambda n: (n, 0)),
        ),
        compiler_params=pltpu.CompilerParams(vmem_limit_bytes=62 * 2**20),
        cost_estimate=pl.CostEstimate(flops=0, bytes_accessed=2**23, transcendentals=0),
    )(back, ddown, dx)
    return (grads[3], *grads[:3])


def solution(mesh):
    return jax.shard_map(
        local,
        mesh=mesh,
        in_specs=(
            P("grp", None),
            P("grp", "shard"),
            P("grp", "shard"),
            P("shard", "grp"),
            P("grp", None),
        ),
        out_specs=(P("shard", "grp"), P("grp", "shard"), P("grp", "shard"), P("shard", "grp")),
        check_vma=False,
    )
```

```python
import functools

import jax
import jax.numpy as jnp
from jax import lax
from jax.experimental import pallas as pl
from jax.experimental.pallas import tpu as pltpu
from jax.sharding import PartitionSpec as P

MESH = pl.DeviceIdType.MESH
BF16 = jnp.bfloat16
F32 = jnp.float32

Q = 224
DH = 2048
B = 512
CHUNK = 512
H0, H1, H2 = COME = ((0, 64), (64, 80), (144, 80))
D0, D1, D2 = GO = ((0, 96), (96, 64), (160, 64))
H01, D12, ALL = (0, 144), (96, 128), (0, Q)


def dot_nt(left, right):
    return lax.dot_general(left, right, (((1,), (1,)), ((), ())), preferred_element_type=F32)


def dot_nn(left, right):
    return lax.dot_general(left, right, (((1,), (0,)), ((), ())), preferred_element_type=F32)


def dot_tn(left, right):
    return lax.dot_general(left, right, (((0,), (0,)), ((), ())), preferred_element_type=F32)


def kernel(
    tok, grd, gate_w, up_w, down_w, back, ddown, dx,
    buf, raw, wt, wbuf, part, other, acc, dxs, dxr, zr, ys, xr, yr, yf, zs, zy,
    ssem, rsem, lsem, zsem, lastsem,
):
    grp, shard = lax.axis_index("grp"), lax.axis_index("shard")
    x_lo, y = lax.div(grp, 4), lax.rem(grp, 4)
    x_hi, z, c = lax.div(shard, 8), lax.rem(lax.div(shard, 2), 4), lax.rem(shard, 2)
    x = 2 * x_hi + x_lo

    def mod4(v):
        return lax.rem(v + 8, 4)

    def slot(dy):
        return dy + lax.div(dy, 2) * (1 - 2 * lax.rem(dy, 2))

    def device(x, y, z, c):
        return (4 * lax.rem(x, 2) + y, 8 * lax.div(x, 2) + 2 * z + c)

    sibling = device(x, y, z, 1 - c)
    inner = device(x + 1 - 2 * x_lo, y, z, c)
    outer = device(mod4(x - 1 + 2 * x_lo), y, z, c)
    across = device(mod4(x + 2), y, z, c)
    along_y = {d: device(x, mod4(y + d), z, c) for d in (1, 2, 3)}
    along_z = {d: device(x, y, mod4(z + d), c) for d in (1, 2, 3)}

    barrier = pltpu.get_barrier_semaphore()
    partners = [sibling, inner, outer, across, *along_y.values(), *along_z.values()]
    for partner in partners:
        pl.semaphore_signal(barrier, inc=1, device_id=partner, device_id_type=MESH)

    count = [0]
    sent = []

    def push(src, dst, target, recv=None):
        n = count[0]
        count[0] += 1
        copy = pltpu.make_async_remote_copy(
            src_ref=src, dst_ref=dst, send_sem=ssem.at[n],
            recv_sem=rsem.at[n] if recv is None else recv,
            device_id=target, device_id_type=MESH,
        )
        copy.start()
        sent.append(copy)
        return copy

    local_count = [0]

    def bring(src, dst):
        n = local_count[0]
        local_count[0] += 1
        copy = pltpu.make_async_copy(src, dst, lsem.at[n])
        copy.start()
        return copy

    def arrived(*copies):
        for copy in copies:
            copy.wait_recv()

    gone = set()

    def left(*copies):
        for copy in copies:
            if id(copy) not in gone:
                gone.add(id(copy))
                copy.wait_send()

    def rows(start, size, step=32):
        return pl.ds(pl.multiple_of(start, step), size)

    def cols(block, size):
        return pl.ds(pl.multiple_of(block * size, size), size)

    mine, theirs = cols(x_lo, DH), cols(1 - x_lo, DH)
    offs = (0, 1, 3, 2)
    quarter = [mod4(z + off) for off in offs]
    first, second = x_hi, 1 - x_hi

    def half(u):
        return first + u * (1 - 2 * first)

    own_tok = [
        bring(src.at[h, :, s, :, mine], buf.at[a, :, s, h, 0, x_lo])
        for s in (0, 1)
        for h in (0, 1)
        for a, src in enumerate((tok, grd))
    ]
    own_raw = [bring(gate_w, raw.at[0]), bring(up_w, raw.at[1]), bring(down_w, wt.at[2])]
    pl.semaphore_wait(barrier, len(partners))

    def send_outer(i, target):
        q = quarter[i]
        return [
            push(src.at[c, q, :, :, theirs], buf.at[a, q, :, c, 0, x_lo], target)
            for a, src in enumerate((tok, grd))
        ]

    from_outer = {
        0: [
            push(src.at[c, z, s, :, theirs], buf.at[a, z, s, c, 0, x_lo], outer)
            for s in (second, first)
            for a, src in enumerate((tok, grd))
        ]
    }
    from_outer[2] = send_outer(2, inner)

    blocks = (x_lo, 1 - x_lo)

    def send_y(d, b):
        n = {1: 2, 3: 1, 2: 3}[d]
        lo = blocks[b]
        return push(buf.at[:, z, first, c, 0, lo], buf.at[:, z, first, c, n, lo], along_y[d])

    def near(b, s, q):
        return buf.at[:, q, s, c, 1:3, blocks[b]]

    def far(b, s, q):
        return buf.at[:, q, s, c, 3:4, blocks[b]]

    core_piece = {(i, u): [] for i in range(4) for u in (0, 1)}

    def to_sibling(i, u, which, b):
        ref = which(b, half(u), quarter[i])
        core_piece[i, u].append(push(ref, ref, sibling))

    from_z, swaps = {}, {}

    def spread(which, b, u):
        ref = which(b, half(u), z)
        from_z[which, b, u] = push(ref, ref, along_z[1]), push(ref, ref, along_z[3])
        to_sibling(0, u, which, b)

    def swap(which, b):
        ref = which(b, first, z)
        swaps[which, b] = push(ref, ref, across)

    for copy in own_tok:
        copy.wait()
    y_near, y_far = [send_y(1, 0), send_y(3, 0)], [send_y(2, 0)]
    for copy in own_raw:
        copy.wait()
    for m in (0, 1):
        def turn(n, carry):
            wt[m, cols(n, 128), :] = raw[m, :, cols(n, 128)].T
            return carry

        lax.fori_loop(0, 7, turn, 0)
    own_w = bring(wt.at[:, rows(Q * y, Q), :], wbuf.at[:, :, cols(y, B)])
    arrived(*y_near)
    spread(near, 0, 0)
    arrived(*y_far)
    spread(far, 0, 0)
    arrived(*from_outer[0][:2])
    y_near, y_far = [send_y(1, 1), send_y(3, 1)], [send_y(2, 1)]
    swap(near, 0)
    swap(far, 0)

    def send_w(h):
        start, size = COME[h]
        return [
            push(
                wt.at[:, rows(Q * mod4(y + d) + start, size, 16), :],
                wbuf.at[:, start : start + size, cols(y, B)],
                along_y[d],
            )
            for d in (1, 3, 2)
        ]

    from_w = [send_w(h) for h in range(len(COME))]

    def outer_to_sibling(i):
        ref = buf.at[:, quarter[i], :, c, 0, 1 - x_lo]
        return push(ref, ref, sibling)

    arrived(*from_outer[0][2:])
    core_outer = [outer_to_sibling(0)]

    arrived(*y_near)
    swap(near, 1)
    spread(near, 1, 0)
    arrived(*y_far)
    swap(far, 1)
    spread(far, 1, 0)
    from_outer[1] = send_outer(1, outer)
    from_outer[3] = send_outer(3, outer)
    for b in (0, 1):
        for which in (near, far):
            arrived(swaps[which, b])
            spread(which, b, 1)
    arrived(*from_outer[2])
    core_outer.append(outer_to_sibling(2))

    onward = []

    def relay(which, b, u):
        up, down = from_z[which, b, u]
        arrived(up)
        if u == 0:
            ref = which(b, half(u), quarter[2])
            onward.append((push(ref, ref, along_z[1]), which, b, u))
        to_sibling(2, u, which, b)
        arrived(down)
        if u == 1:
            ref = which(b, half(u), quarter[1])
            onward.append((push(ref, ref, along_z[3]), which, b, u))
        to_sibling(1, u, which, b)

    exchange = {}

    def forward(i, us, span):
        q = quarter[i]
        start, size = span
        hidden = slice(start, start + size)

        def one(u, carry):
            s = half(u)
            part[i, u, 0:2, hidden, :] = dot_nt(
                wbuf[0:2, hidden, :].reshape(2 * size, DH), buf[0, q, s].reshape(256, DH)
            ).astype(BF16).reshape(2, size, 256)
            part[i, u, 2, hidden, :] = dot_nt(
                wbuf[2, hidden, :], buf[1, q, s].reshape(256, DH)
            ).astype(BF16)
            return carry

        lax.fori_loop(us[0], us[-1] + 1, one, 0)
        at = slice(us[0], us[-1] + 1)
        exchange[i, us, span] = push(
            part.at[i, at, :, hidden, :], other.at[i, at, :, hidden, :], inner
        )

    def activate(i, us, span):
        arrived(exchange[i, us, span])
        left(exchange[i, us, span])
        start, size = span
        pair = slice(us[0], us[-1] + 1)
        step = 16 if len(us) == 2 or size % 32 else 32

        def some(r, carry):
            at = rows(start + step * r, step, 16)

            def full(m):
                return part[i, pair, m, at, :].astype(F32) + other[i, pair, m, at, :].astype(F32)

            gate, up_pre, back_grad = full(0), full(1), full(2)
            s = jax.nn.sigmoid(gate)
            silu = gate * s
            part[i, pair, 0, at, :] = (
                back_grad * up_pre * s * (1.0 + gate * (1.0 - s))
            ).astype(BF16)
            part[i, pair, 1, at, :] = (back_grad * silu).astype(BF16)
            part[i, pair, 2, at, :] = (silu * up_pre).astype(BF16)
            return carry

        lax.fori_loop(0, size // step, some, 0)

    def weight_terms(i, span, n):
        q = quarter[i]
        start, size = span
        hidden = slice(start, start + size)
        at = cols(n, B)
        pair, third = 0.0, 0.0
        for u in (0, 1):
            pair = pair + dot_nn(
                part[i, u, 0:2, hidden, :].reshape(2 * size, 256),
                buf[0, q, half(u), :, :, :, :, at].reshape(256, B),
            )
            third = third + dot_nn(
                part[i, u, 2, hidden, :], buf[1, q, half(u), :, :, :, :, at].reshape(256, B)
            )
        return pair.reshape(2, size, B), third

    def weight_grads(i, span):
        start, size = span
        hidden = slice(start, start + size)

        def block(n, carry):
            pair, third = weight_terms(i, span, n)
            at = cols(n, B)
            if i:
                pair = pair + acc[0:2, hidden, at]
                third = third + acc[2, hidden, at]
            acc[0:2, hidden, at] = pair
            acc[2, hidden, at] = third
            return carry

        lax.fori_loop(0, 4, block, 0)

    from_dw, own_dw = {}, []

    def last_weight_grads(i, span):
        if span == D0:
            for copies in from_w:
                for copy in copies:
                    left(copy)
        start, size = span
        hidden = slice(start, start + size)
        from_dw[span] = []
        for d in (1, 3, 2, 0):
            n = mod4(y + d)
            pair, third = weight_terms(i, span, n)
            at = cols(n, B)
            held = rows(Q * n + start, size, 16)
            wt[0:2, held, :] = (pair + acc[0:2, hidden, at]).astype(BF16)
            wt[2, held, :] = (third + acc[2, hidden, at]).astype(BF16)
            there = rows(Q * y + start, size, 16)
            if d:
                from_dw[span].append(push(wt.at[0:2, held, :], back.at[:, there, :], along_y[d]))
                from_dw[span].append(push(wt.at[2, held, :], ddown.at[there, :], along_y[d]))
            else:
                own_dw.append(bring(wt.at[0:2, held, :], back.at[:, there, :]))
                own_dw.append(bring(wt.at[2, held, :], ddown.at[there, :]))

    def turned(i, u):
        return part[i, u, 0:2].reshape(2 * Q, 256).T

    def token_terms(i, u, n, deltas):
        at = cols(n, B)
        dxs[i, u, :, :, at] = dot_nn(
            deltas, wbuf[0:2, :, at].reshape(2 * Q, B)
        ).astype(BF16).reshape(2, 128, B)

    core_dx = {}

    def token_grads(i, us):
        for u in us:
            deltas = turned(i, u)

            def block(n, carry):
                token_terms(i, u, n, deltas)
                return carry

            lax.fori_loop(0, 4, block, 0)
            core_dx[i, u] = push(dxs.at[i, u, 1 - c], dxr.at[i, u], sibling)

    def add_core(i, u, at):
        dxs[i, u, c, :, at] = (
            dxs[i, u, c, :, at].astype(F32) + dxr[i, u, :, at].astype(F32)
        ).astype(BF16)

    def add_core_whole(i, u):
        arrived(core_dx[i, u])

        def some(n, carry):
            add_core(i, u, cols(n, B))
            return carry

        lax.fori_loop(0, 4, some, 0)

    def block_rows(yb):
        return rows(32 * slot(mod4(yb)), 32)

    def along_z_grads(i, us):
        q = quarter[i]
        for u in us:
            add_core_whole(i, u)
            for d in (1, 3, 2):
                push(
                    dxs.at[i, u, c, block_rows(z + d - y), :], zr.at[q, u, d - 1], along_z[d],
                    zsem.at[q, u, d - 1],
                )

    from_yf, from_zy = {}, {}

    def along_y_grads():
        for u in (0, 1):
            add_core_whole(0, u)
        for d in (1, 3, 2):
            at = cols(mod4(y + d), B)
            from_yf[d] = push(dxs.at[0, :, c, :, at], yf.at[d - 1], along_y[d])

    def then_along_z():
        for d in (1, 3, 2):
            arrived(from_yf[d])
        for e in (1, 3, 2, 0):
            total = dxs[0, :, c, block_rows(z + e - y), cols(y, B)].astype(F32)
            for d in (1, 2, 3):
                total = total + yf[d - 1, :, block_rows(z + e - y + d), :].astype(F32)
            zs[e] = total.astype(BF16)
            if e:
                from_zy[e] = push(zs.at[e], zy.at[e - 1], along_z[e])

    def last_token_grads():
        core_last = {}
        deltas = turned(3, 1)
        for d in (2, 1, 3, 0):
            n = mod4(y + d)
            token_terms(3, 1, n, deltas)
            at = cols(n, B)
            core_last[d] = push(dxs.at[3, 1, 1 - c, :, at], dxr.at[3, 1, :, at], sibling)
        return core_last

    def last_along_z(core_last):
        for k, d in enumerate((2, 1, 3, 0)):
            at = cols(mod4(y + d), B)
            arrived(core_last[d])
            add_core(3, 1, at)
            for e in (1, 3, 2):
                push(
                    dxs.at[3, 1, c, block_rows(z + e - y), at],
                    zr.at[quarter[3], 1, e - 1, :, at], along_z[e], lastsem.at[k, e - 1],
                )

    whole, one, two = (0, 1), (0,), (1,)
    own_w.wait()
    arrived(core_outer[0], *core_piece[0, 0])
    arrived(*from_w[0])
    forward(0, one, H0)
    arrived(*core_piece[0, 1])
    forward(0, two, H0)
    for b in (0, 1):
        relay(near, b, 0)
        relay(far, b, 0)
    arrived(core_outer[1], *core_piece[2, 0])
    forward(2, one, H0)
    arrived(*from_outer[1])
    core_outer.append(outer_to_sibling(1))
    arrived(core_outer[2], *core_piece[1, 0])
    forward(1, one, H0)
    relay(near, 0, 1)
    relay(far, 0, 1)
    arrived(*from_w[1])
    forward(0, whole, H1)
    forward(2, one, H1)
    forward(1, one, H1)
    activate(0, one, H0)
    activate(0, two, H0)
    relay(near, 1, 1)
    relay(far, 1, 1)
    activate(2, one, H0)
    activate(1, one, H0)
    arrived(*from_w[2])
    forward(0, whole, H2)
    forward(1, one, H2)
    arrived(*core_piece[1, 1])
    forward(1, two, ALL)
    arrived(*core_piece[2, 1])
    forward(2, two, D0)
    activate(0, whole, H1)
    weight_grads(0, H01)
    activate(2, one, H1)
    activate(1, one, H1)
    activate(0, whole, H2)
    token_grads(0, whole)
    weight_grads(0, H2)
    along_y_grads()
    activate(1, one, H2)
    token_grads(1, one)
    for copy, which, b, u in onward:
        arrived(copy)
        to_sibling(3, u, which, b)
    arrived(*from_outer[3])
    core_outer.append(outer_to_sibling(3))
    along_z_grads(1, one)
    arrived(core_outer[3], *core_piece[3, 0], *core_piece[3, 1])
    forward(3, whole, D0)
    activate(1, two, ALL)
    token_grads(1, two)
    forward(2, one, H2)
    along_z_grads(1, two)
    weight_grads(1, ALL)
    activate(2, two, D0)
    weight_grads(2, D0)
    then_along_z()
    forward(3, one, D12)
    activate(3, whole, D0)
    last_weight_grads(3, D0)
    forward(2, two, D1)
    activate(2, one, H2)
    token_grads(2, one)
    forward(3, two, D1)
    along_z_grads(2, one)
    forward(2, two, D2)
    forward(3, two, D2)
    activate(3, one, D12)
    token_grads(3, one)
    activate(2, two, D1)
    along_z_grads(3, one)
    weight_grads(2, D1)
    activate(3, two, D1)
    last_weight_grads(3, D1)
    activate(2, two, D2)
    token_grads(2, two)
    activate(3, two, D2)
    along_z_grads(2, two)
    core_last = last_token_grads()
    weight_grads(2, D2)
    last_weight_grads(3, D2)
    last_along_z(core_last)

    def landed(ref, sem):
        pltpu.make_async_remote_copy(
            src_ref=ref, dst_ref=ref, send_sem=ssem.at[0], recv_sem=sem,
            device_id=along_z[1], device_id_type=MESH,
        ).wait_recv()

    def land(i, u):
        for d in (1, 2, 3):
            q = mod4(z - d + offs[i])
            landed(zr.at[q, u, d - 1], zsem.at[q, u, d - 1])

    keep = block_rows(z - y)
    from_x, from_yg = [], {}

    def over_x(u, at, own):
        for i in range(4):
            q = quarter[i]
            terms = [zr[q, u, e - 1, :, at] for e in (1, 2, 3) if (offs[i] + e) % 4]
            if i:
                terms.append(dxs[i, u, c, keep, at])
            if own:
                terms.append(zy[3 - offs[i], u] if i else zs[0, u])
            total = sum(term.astype(F32) for term in terms).astype(BF16)
            ys[0, q, half(u), :, at] = total[0:16]
            ys[1, q, half(u), :, at] = total[16:32]

    def first_over_x():
        for d in (1, 3, 2, 0):
            over_x(0, cols(mod4(y + d), B), d == 0)
        return push(ys.at[1 - x_hi, :, half(0)], xr.at[:, half(0)], across)

    def then_over_x(k, d):
        at = cols(mod4(y + d), B)
        for e in (1, 2, 3):
            landed(zr.at[mod4(z - e + 2), 1, e - 1, :, at], lastsem.at[k, e - 1])
        over_x(1, at, d == 0)
        from_x.append(
            push(ys.at[1 - x_hi, :, half(1), :, at], xr.at[:, half(1), :, at], across)
        )

    def over_y(k, d):
        at = cols(mod4(y + d), B)
        arrived(from_x[k])
        ys[x_hi, :, :, :, at] = (
            ys[x_hi, :, :, :, at].astype(F32) + xr[:, :, :, at].astype(F32)
        ).astype(BF16)
        if d:
            from_yg[d] = push(ys.at[x_hi, :, :, :, at], yr.at[d - 1], along_y[d])

    order = (2, 1, 3, 0)
    for i in (1, 2, 3):
        land(i, 0)
    arrived(*from_zy.values())
    from_first = first_over_x()
    land(1, 1)
    land(2, 1)
    then_over_x(0, order[0])
    arrived(from_first)
    for k in (1, 2, 3):
        then_over_x(k, order[k])
        over_y(k - 1, order[k - 1])
    over_y(3, order[3])
    for copy in own_dw:
        copy.wait()
    for span in GO:
        arrived(*from_dw[span])
    total = ys[x_hi, :, :, :, cols(y, B)].astype(F32)
    for d in (2, 1, 3):
        arrived(from_yg[d])
        total = total + yr[d - 1].astype(F32)
    dx[...] = total.astype(BF16).reshape(128, B)
    left(*sent)


def finish(back, down, tokens, dgate, dup, ddown, dx):
    dx[...] = tokens[...]
    dgate[...] = back[0].astype(F32).T
    dup[...] = back[1].astype(F32).T
    ddown[...] = down[...].astype(F32)


def local(tokens, gate_weight, up_weight, down_weight, grad_out):
    flops = 8 * 2 * 2048 * 2048 * 256
    back, ddown, dx = pl.pallas_call(
        kernel,
        out_shape=(
            jax.ShapeDtypeStruct((2, 4 * Q, B), BF16),
            jax.ShapeDtypeStruct((4 * Q, B), BF16),
            jax.ShapeDtypeStruct((128, B), BF16),
        ),
        in_specs=[pl.BlockSpec(memory_space=pl.ANY)] * 5,
        out_specs=(
            pl.BlockSpec(memory_space=pl.ANY),
            pl.BlockSpec(memory_space=pl.ANY),
            pl.BlockSpec(memory_space=pltpu.VMEM),
        ),
        scratch_shapes=[
            pltpu.VMEM((2, 4, 2, 2, 4, 2, 16, DH), BF16),
            pltpu.VMEM((2, B, 4 * Q), BF16),
            pltpu.VMEM((3, 4 * Q, B), BF16),
            pltpu.VMEM((3, Q, DH), BF16),
            pltpu.VMEM((4, 2, 3, Q, 256), BF16),
            pltpu.VMEM((4, 2, 3, Q, 256), BF16),
            pltpu.VMEM((3, Q, DH), F32),
            pltpu.VMEM((4, 2, 2, 128, DH), BF16),
            pltpu.VMEM((4, 2, 128, DH), BF16),
            pltpu.VMEM((4, 2, 3, 32, DH), BF16),
            pltpu.VMEM((2, 4, 2, 16, DH), BF16),
            pltpu.VMEM((4, 2, 16, DH), BF16),
            pltpu.VMEM((3, 4, 2, 16, B), BF16),
            pltpu.VMEM((3, 2, 128, B), BF16),
            pltpu.VMEM((4, 2, 32, B), BF16),
            pltpu.VMEM((3, 2, 32, B), BF16),
            pltpu.SemaphoreType.DMA((224,)),
            pltpu.SemaphoreType.DMA((224,)),
            pltpu.SemaphoreType.DMA((24,)),
            pltpu.SemaphoreType.DMA((4, 2, 3)),
            pltpu.SemaphoreType.DMA((4, 3)),
        ],
        compiler_params=pltpu.CompilerParams(
            collective_id=0, has_side_effects=True, vmem_limit_bytes=62 * 2**20
        ),
        cost_estimate=pl.CostEstimate(flops=flops, bytes_accessed=2**24, transcendentals=2**20),
    )(
        tokens.reshape(2, 4, 2, 16, 4096), grad_out.reshape(2, 4, 2, 16, 4096),
        gate_weight, up_weight, down_weight,
    )
    grads = pl.pallas_call(
        finish,
        grid=(2,),
        out_shape=(
            jax.ShapeDtypeStruct((B, 4 * Q), F32),
            jax.ShapeDtypeStruct((B, 4 * Q), F32),
            jax.ShapeDtypeStruct((4 * Q, B), F32),
            jax.ShapeDtypeStruct((128, B), BF16),
        ),
        in_specs=[
            pl.BlockSpec((2, 4 * Q, B // 2), lambda n: (0, 0, n)),
            pl.BlockSpec((2 * Q, B), lambda n: (n, 0)),
            pl.BlockSpec((64, B), lambda n: (n, 0)),
        ],
        out_specs=(
            pl.BlockSpec((B // 2, 4 * Q), lambda n: (n, 0)),
            pl.BlockSpec((B // 2, 4 * Q), lambda n: (n, 0)),
            pl.BlockSpec((2 * Q, B), lambda n: (n, 0)),
            pl.BlockSpec((64, B), lambda n: (n, 0)),
        ),
        compiler_params=pltpu.CompilerParams(vmem_limit_bytes=62 * 2**20),
        cost_estimate=pl.CostEstimate(flops=0, bytes_accessed=2**23, transcendentals=0),
    )(back, ddown, dx)
    return (grads[3], *grads[:3])


def solution(mesh):
    return jax.shard_map(
        local,
        mesh=mesh,
        in_specs=(
            P("grp", None),
            P("grp", "shard"),
            P("grp", "shard"),
            P("shard", "grp"),
            P("grp", None),
        ),
        out_specs=(P("shard", "grp"), P("grp", "shard"), P("grp", "shard"), P("shard", "grp")),
        check_vma=False,
    )
```
